32 devices in a mesh: groups: 2 (over y), tensor: 8 (over z, x), store: 2 (over core).
Axes of the slice: x: 2, y: 2, z: 4, core: 2. Of those that a mesh axis runs over, the one named last changes fastest.
Arguments:
- tokens: bfloat16 [2560, 3072], P(('groups', 'store'), 'tensor'), parts along dimension 0, may hold values from -6 to 6
- modulation: bfloat16 [4, 8, 3, 3072], P(('groups', 'store')), parts along dimension 0, may hold values from -3 to 3
- adapter_per_request: int32 [4, 8], P('groups'), parts along dimension 0, may hold values from 0 to 255
- tokens_per_request: int32 [4, 8], P(('groups', 'store')), parts along dimension 0, may hold values from 1 to 160, 640 in all within a row
- first_weight: bfloat16 [3072, 12288], P(None, 'tensor'), may hold values from -0.109375 to 0.109375
- first_bias: bfloat16 [12288], P('tensor'), may hold values from -3 to 3
- second_weight: bfloat16 [12288, 3072], P('tensor'), may hold values from -0.0546875 to 0.0546875
- second_bias: bfloat16 [3072], P('tensor'), may hold values from -3 to 3
- adapter_down_matrices: bfloat16 [256, 3072, 64], P('store', 'tensor'), may hold values from -0.109375 to 0.109375
- adapter_up_matrices: bfloat16 [256, 64, 12288], P('store', None, 'tensor'), may hold values from -0.75 to 0.75
Outputs:
- block_out: bfloat16 [2560, 3072], P(('groups', 'store'), 'tensor'), parts along dimension 0
The draws below stay inside these ranges and needn't reach their ends.
There are 2 independent parts, one for each index of `groups`. The reference program is written for one: setup_inputs(seed, part) draws one part's arguments, and reference() takes and returns one part's arrays. A program takes and returns all parts, laid end to end along the dimension named above; an argument that names none is the same for every part. Nothing has to cross between parts.
Inputs may be any that keep to these rules, and one draw needn't show every extreme that they name: `adapter_per_request`: adapter ids of the store. `tokens_per_request`: each row sums to 640, the largest entry is exactly 160.
All inputs are finite; a program needn't handle non-finite values.
Results may differ from the reference program's by a relative error of at most 0.0043.
Values may be sent and summed in bfloat16 or wider, within the bound.
No kernel may reach another device: no remote copies, remote signals or barrier semaphores. Data moves between devices by JAX's collectives and lax.ppermute only.
A program may use at most 192 MiB of HBM per device.

```python
import math
import jax
import jax.numpy as jnp
import numpy as np
from jax import lax

MODEL_WIDTH = 3072
HIDDEN_UNITS = 12288
ADAPTER_RANK = 64
IMAGE_TOKENS = 640
REQUEST_COUNT = 8
ADAPTER_COUNT = 256
MOST = 160
TOKENS = 1280
N_STORE = 2


def with_ends(array, key, low, top_value):
    extent = array.shape
    index_at = [jax.random.randint(jax.random.fold_in(key, axis), (), 0, extent[axis]) for axis in range(len(extent))]
    array = array.at[tuple(index_at)].set(low)
    longest = extent.index(max(extent))
    index_at[longest] = (index_at[longest] + 1) % extent[longest]
    return array.at[tuple(index_at)].set(top_value)


def shard_levels(key, dims, shards, smallest, top_value):
    loudness = 1.0
    for axis_at, parts in shards:
        draws = jax.random.uniform(jax.random.fold_in(jax.random.fold_in(key, 6), axis_at), (parts,), jnp.float32, smallest / len(shards), top_value / len(shards))
        loudness = loudness * jnp.repeat(jnp.exp(draws), dims[axis_at] // parts).reshape((-1,) + (1,) * (len(dims) - 1 - axis_at))
    return loudness


def rank_bounds(count, skew):
    portions = [(1 << 20) // math.isqrt(standing ** skew) + 1 for standing in range(1, count + 1)]
    width = 1 + sum(portions) // (1 << 30)
    return np.cumsum(np.array([max(1, weight // width) for weight in portions]))


def skewed_ids(key, extent, amount, skew):
    listing = rank_bounds(amount, skew)
    ticket = jax.random.randint(jax.random.fold_in(key, 1), extent, 0, int(listing[amount - 1]))
    rank = jnp.searchsorted(jnp.asarray(listing, jnp.int32), ticket, side="right")
    return jax.random.permutation(jax.random.fold_in(key, 2), amount)[rank].astype(jnp.int32)


def split_up(number_of, total, reach, slope):
    weights = [(1 << 20) // math.isqrt(standing ** slope) + 1 for standing in range(2, number_of + 1)]
    surplus, given = total - reach - (number_of - 1), [1] * (number_of - 1)
    while surplus > 0:
        movable = [i for i in range(number_of - 1) if given[i] < reach]
        mass, left = sum([weights[i] for i in movable]), surplus
        for i in movable:
            addition = min(reach - given[i], max(1, left * weights[i] // mass), surplus)
            given[i] = given[i] + addition
            surplus = surplus - addition
    return np.array([reach] + given)


def ragged_sizes(stream_key, count, total, reach, slope):
    if count == 2:
        one = jax.random.randint(stream_key, (), max(1, total - reach), min(reach, total - 1) + 1)
        return jnp.stack([one, total - one])
    sizes = jnp.asarray(split_up(count, total, reach, slope), jnp.int32)
    pairs = (count - 1) // 2
    source_of, receiver = sizes[1:1 + 2 * pairs:2], sizes[2:2 + 2 * pairs:2]
    room = jnp.minimum(source_of - 1, reach - receiver)
    passed = jax.random.randint(jax.random.fold_in(stream_key, 1), (pairs,), 0, 1 << 20) % (room + 1)
    sizes = sizes.at[1:1 + 2 * pairs:2].set(source_of - passed).at[2:2 + 2 * pairs:2].set(receiver + passed)
    return sizes[jax.random.permutation(jax.random.fold_in(stream_key, 2), count)]


def scatter_about(stream_key, extent, width, reach, pieces=(), kind=jnp.bfloat16):
    result = jax.random.normal(stream_key, extent, jnp.float32) * width
    if len(pieces) > 0:
        result = shard_levels(stream_key, extent, pieces, -0.22, 0.18) * result
    return jnp.clip(result, min=-reach, max=reach).astype(kind)


def setup_inputs(seed: int = 0, part: int = 0) -> dict:
    arg_keys = jax.random.split(jax.random.key(seed), 11)
    part_keys = jax.random.split(jax.random.fold_in(arg_keys[10], part), 11)
    tokens = scatter_about(part_keys[0], (TOKENS, MODEL_WIDTH), 1.0, 6.0, ((0, 2), (1, 8)))
    modulation = scatter_about(part_keys[1], (N_STORE, REQUEST_COUNT, 3, MODEL_WIDTH), 0.5, 3.0, ((0, 2),))
    adapter_per_request = with_ends(skewed_ids(part_keys[2], (N_STORE, REQUEST_COUNT), ADAPTER_COUNT, 2), jax.random.fold_in(part_keys[2], 3), 0, ADAPTER_COUNT - 1).astype(jnp.int32)
    tokens_per_request = jax.vmap(lambda own: ragged_sizes(own, REQUEST_COUNT, IMAGE_TOKENS, MOST, 2))(jax.random.split(part_keys[3], N_STORE)).reshape((N_STORE, REQUEST_COUNT)).astype(jnp.int32)
    first_weight = scatter_about(arg_keys[4], (MODEL_WIDTH, HIDDEN_UNITS), MODEL_WIDTH ** -0.5, 0.109375, ((1, 8),))
    first_bias = scatter_about(arg_keys[5], (HIDDEN_UNITS,), 0.5, 3.0, ((0, 8),))
    second_weight = scatter_about(arg_keys[6], (HIDDEN_UNITS, MODEL_WIDTH), HIDDEN_UNITS ** -0.5, 0.0546875, ((0, 8),))
    second_bias = scatter_about(arg_keys[7], (MODEL_WIDTH,), 0.5, 3.0, ((0, 8),))
    adapter_down_matrices = scatter_about(arg_keys[8], (ADAPTER_COUNT, MODEL_WIDTH, ADAPTER_RANK), MODEL_WIDTH ** -0.5, 0.109375, ((0, 2), (1, 8)))
    adapter_up_matrices = scatter_about(arg_keys[9], (ADAPTER_COUNT, ADAPTER_RANK, HIDDEN_UNITS), ADAPTER_RANK ** -0.5, 0.75, ((0, 2), (2, 8)))
    return {"tokens": tokens, "modulation": modulation, "adapter_per_request": adapter_per_request, "tokens_per_request": tokens_per_request, "first_weight": first_weight, "first_bias": first_bias, "second_weight": second_weight, "second_bias": second_bias, "adapter_down_matrices": adapter_down_matrices, "adapter_up_matrices": adapter_up_matrices}


def request_onehot(lengths):
    bounds = jnp.cumsum(lengths)
    places = jnp.arange(IMAGE_TOKENS, dtype=jnp.int32)
    owner_req = lax.optimization_barrier(jnp.sum((places[:, None] >= bounds[None, :]).astype(jnp.int32), axis=1))
    return (owner_req[:, None] == jnp.arange(REQUEST_COUNT, dtype=jnp.int32)[None, :]).astype(jnp.float32)

def reference(tokens, modulation, adapter_per_request, tokens_per_request, first_weight, first_bias, second_weight, second_bias, adapter_down_matrices, adapter_up_matrices):
    outputs = []
    for half_index in range(N_STORE):
        adapter_indicator = request_onehot(tokens_per_request[half_index])
        factors = modulation[half_index].astype(jnp.float32)
        shift_rows = jnp.dot(adapter_indicator, factors[:, 0], precision=lax.Precision.HIGHEST)
        scale_rows = jnp.dot(adapter_indicator, factors[:, 1], precision=lax.Precision.HIGHEST)
        gate_rows = jnp.dot(adapter_indicator, factors[:, 2], precision=lax.Precision.HIGHEST)
        hidden_in = tokens[half_index * IMAGE_TOKENS:(half_index + 1) * IMAGE_TOKENS].astype(jnp.float32)
        center = lax.optimization_barrier(jnp.mean(hidden_in, axis=1, keepdims=True))
        spread = lax.optimization_barrier(jnp.mean((hidden_in - center) ** 2, axis=1, keepdims=True))
        normed = (hidden_in - center) * lax.rsqrt(spread + 1e-06)
        modded = ((1.0 + scale_rows) * normed + shift_rows).astype(jnp.bfloat16)
        selected_adapters = adapter_per_request[half_index]
        selected_down = adapter_down_matrices[selected_adapters].astype(jnp.float32)
        selected_up = adapter_up_matrices[selected_adapters]
        low_rank_every = jnp.einsum('td,kdr->tkr', modded.astype(jnp.float32), selected_down, precision=lax.Precision.HIGHEST)
        adapter_low_rank = lax.optimization_barrier(jnp.sum(adapter_indicator[:, :, None] * low_rank_every, axis=1)).astype(jnp.bfloat16)
        broadcast_low_rank = (adapter_indicator[:, :, None] * adapter_low_rank.astype(jnp.float32)[:, None, :]).reshape(IMAGE_TOKENS, REQUEST_COUNT * ADAPTER_RANK).astype(jnp.bfloat16)
        preact = jnp.dot(modded, first_weight, preferred_element_type=jnp.float32) + first_bias.astype(jnp.float32)
        preact = preact + jnp.dot(broadcast_low_rank, selected_up.reshape(REQUEST_COUNT * ADAPTER_RANK, HIDDEN_UNITS), preferred_element_type=jnp.float32)
        activated = jax.nn.gelu(preact, approximate=True).astype(jnp.bfloat16)
        mixed_rows = jnp.dot(activated, second_weight, preferred_element_type=jnp.float32)
        outputs.append((hidden_in + gate_rows * (mixed_rows + second_bias.astype(jnp.float32))).astype(jnp.bfloat16))
    return jnp.concatenate(outputs, axis=0)
```

```python
import functools

import jax
import jax.numpy as jnp
from jax import lax
from jax.experimental import pallas as pl
from jax.experimental.pallas import tpu as pltpu
from jax.sharding import PartitionSpec as P

BF = jnp.bfloat16
F32 = jnp.float32
VMEM_LIMIT = 56 * 1024 * 1024
HIGH = lax.Precision.HIGHEST
ANY = pl.BlockSpec(memory_space=pl.ANY)
SMEM = pl.BlockSpec(memory_space=pltpu.SMEM)
WHOLE = pl.BlockSpec(memory_space=pltpu.VMEM)


def params(**more):
    return pltpu.CompilerParams(vmem_limit_bytes=VMEM_LIMIT, **more)


def cost(flops, nbytes, trans=0):
    return pl.CostEstimate(
        flops=int(flops), bytes_accessed=int(nbytes), transcendentals=int(trans)
    )


def ring_order(count):
    cols = 2 if count < 32 else 4
    rows = count // cols
    walk = [r * cols for r in range(rows)]
    for i, r in enumerate(reversed(range(rows))):
        across = list(range(1, cols))
        walk += [r * cols + c for c in (across if i % 2 == 0 else across[::-1])]
    return walk


def send_kernel(ids, down_ref, up_ref, down_out, up_out, sem):
    count = down_out.shape[0]
    copies = []
    for r in range(count):
        copies.append(pltpu.make_async_copy(down_ref.at[ids[r]], down_out.at[r], sem.at[2 * r]))
        copies.append(pltpu.make_async_copy(up_ref.at[ids[r]], up_out.at[r], sem.at[2 * r + 1]))
    for c in copies:
        c.start()
    for c in copies:
        c.wait()


def fetch_adapters(ids, owned, store_ref, recv_ref, dst, sem, wait):
    count = recv_ref.shape[0]
    rank = recv_ref.shape[1]
    for r in range(count):
        here = dst.at[pl.ds(r * rank, rank)]
        if wait:
            pltpu.make_async_copy(recv_ref.at[r], here, sem.at[r]).wait()
            continue

        @pl.when(owned[r] == 1)
        def _():
            pltpu.make_async_copy(store_ref.at[ids[r]], here, sem.at[r]).start()

        @pl.when(owned[r] == 0)
        def _():
            pltpu.make_async_copy(recv_ref.at[r], here, sem.at[r]).start()


def prep_kernel(
    ids, owned, lengths, x_ref, mod_ref, down_ref, recv_ref,
    low_out, stat_out, side_out, hot_out, down_now, sem,
):
    rows, feat = x_ref.shape
    reqs = recv_ref.shape[0]
    rank = recv_ref.shape[1]
    fetch_adapters(ids, owned, down_ref, recv_ref, down_now, sem, False)
    x = x_ref[...].astype(F32)
    mean = jnp.mean(x, axis=1, keepdims=True)
    cent = x - mean
    m2 = jnp.sum(cent * cent, axis=1, keepdims=True)
    row = lax.broadcasted_iota(jnp.int32, (rows, 128), 0)
    lane = lax.broadcasted_iota(jnp.int32, (rows, 128), 1)
    hot = jnp.zeros((rows, 128), F32)
    begin = jnp.int32(0)
    for r in range(reqs):
        end = begin + lengths[r]
        hot = jnp.where((lane == r) & (row >= begin) & (row < end), 1.0, hot)
        begin = end
    hot_out[...] = hot.astype(BF)
    stat_out[...] = jnp.where(lane == 0, mean, jnp.where(lane == 1, m2, 0.0)).T[:8]
    hot8 = hot[:, :reqs].astype(BF)
    scale_rows = jnp.dot(hot8, mod_ref[1], preferred_element_type=F32)
    lhs = (cent * (1.0 + scale_rows)).astype(BF)
    hot_t = hot.T
    fetch_adapters(ids, owned, down_ref, recv_ref, down_now, sem, True)
    every = lax.dot_general(
        down_now[...], lhs, (((1,), (1,)), ((), ())), preferred_element_type=F32
    )
    total = jnp.zeros((rank, rows), F32)
    side = jnp.zeros((rank, 128), F32)
    lane_s = lax.broadcasted_iota(jnp.int32, (rank, 128), 1)
    for r in range(reqs):
        total = total + every[r * rank : (r + 1) * rank] * hot_t[r : r + 1]
        mat = down_now[pl.ds(r * rank, rank), :].astype(F32)
        per_scale = jnp.sum(mat * (1.0 + mod_ref[1, pl.ds(r, 1), :].astype(F32)), axis=1, keepdims=True)
        per_shift = jnp.sum(mat * mod_ref[0, pl.ds(r, 1), :].astype(F32), axis=1, keepdims=True)
        side = jnp.where(lane_s == r, per_scale, side)
        side = jnp.where(lane_s == reqs + r, per_shift, side)
    low_out[...] = total.astype(BF)
    side_out[...] = side


def merge(count, low_a, stat_a, side_a, low_b, stat_b, side_b, hot_ref):
    hot_t = hot_ref[...].astype(F32).T
    sa, sb = stat_a[...], stat_b[...]
    gap = sa[0:1] - sb[0:1]
    mean = 0.5 * (sa[0:1] + sb[0:1])
    m2 = sa[1:2] + sb[1:2] + gap * gap * (count * 0.5)
    fa, fb = side_a[...], side_b[...]
    back = jnp.dot(fa - fb, hot_t, precision=HIGH, preferred_element_type=F32)
    low = low_a[...].astype(F32) + low_b[...].astype(F32) + (0.5 * gap) * back
    return low, mean, m2, fa + fb, hot_t


def merge_kernel(count, *refs):
    low_out, stat_out, side_out = refs[-3:]
    low, mean, m2, side, _ = merge(count, *refs[:-3])
    low_out[...] = low.astype(BF)
    stat_out[...] = jnp.concatenate([mean, m2, jnp.zeros((6, mean.shape[1]), F32)], axis=0)
    side_out[...] = side


def last_merge_kernel(count, reqs, *refs):
    wide_out, col_out = refs[-2:]
    low, mean, m2, side, hot_t = merge(count, *refs[:-2])
    rank, rows = low.shape
    rstd = lax.rsqrt(m2 / (2 * count) + 1e-06)
    sums = jnp.dot(pltpu.roll(side, 128 - reqs, 1), hot_t, precision=HIGH, preferred_element_type=F32)
    low = (low * rstd + sums).astype(BF).astype(F32)
    low = jnp.concatenate([low] * (128 // rank), axis=0).T.astype(BF)[:, :rank]
    src = lax.broadcasted_iota(jnp.int32, (rank, reqs * rank), 0)
    dst = lax.broadcasted_iota(jnp.int32, (rank, reqs * rank), 1)
    spread = jnp.where(dst % rank == src, 1.0, 0.0).astype(BF)
    hot8 = refs[6][...][:, :reqs]
    who = lax.broadcasted_iota(jnp.int32, (reqs, reqs * rank), 0)
    col = lax.broadcasted_iota(jnp.int32, (reqs, reqs * rank), 1)
    mask = jnp.dot(
        hot8, jnp.where(col // rank == who, 1.0, 0.0).astype(BF), preferred_element_type=F32
    )
    wide_out[...] = (jnp.dot(low, spread, preferred_element_type=F32) * mask).astype(BF)
    both = jnp.concatenate([mean, rstd, jnp.zeros((126, rows), F32)], axis=0)
    col_out[...] = both.T


def normed(x, hot8, mod_ref, cols):
    scale_rows = jnp.dot(hot8, mod_ref[1], preferred_element_type=F32)
    shift_rows = jnp.dot(hot8, mod_ref[0], preferred_element_type=F32)
    flat = (x.astype(F32) - cols[:, 0:1]) * cols[:, 1:2]
    return ((1.0 + scale_rows) * flat + shift_rows).astype(BF)


def first_kernel(blocks, reqs, fresh, idx, *refs):
    xs = refs[:blocks]
    hot_ref, col_ref, mod_ref, w_ref = refs[blocks : blocks + 4]
    acc_in = None if fresh else refs[blocks + 4]
    acc_out = refs[-1]
    step = pl.program_id(0)
    hot8 = hot_ref[...][:, :reqs]
    cols = col_ref[...]
    for k in range(blocks):

        @pl.when(step == k)
        def _(k=k):
            lhs = normed(xs[k][...], hot8, mod_ref, cols)
            part = jnp.dot(lhs, w_ref[...], preferred_element_type=F32)
            if k == 0 and fresh:
                acc_out[...] = part
            elif k == 0:
                acc_out[...] = acc_in[...] + part
            else:
                acc_out[...] += part


def first_call(idx, xs, hot, cols, mod, weight, acc):
    blocks = len(xs)
    rows, feat = xs[0].shape
    hidden = weight.shape[1]
    reqs = mod.shape[1]
    fresh = acc is None
    full = pl.BlockSpec((rows, hidden), lambda i, s: (0, 0))
    in_specs = [pl.BlockSpec((rows, feat), lambda i, s: (0, 0))] * blocks + [
        pl.BlockSpec((rows, 128), lambda i, s: (0, 0)),
        pl.BlockSpec((rows, 128), lambda i, s: (0, 0)),
        pl.BlockSpec((3, reqs, feat), lambda i, s: (0, 0, s[i])),
        pl.BlockSpec((feat, hidden), lambda i, s: (s[i], 0)),
    ]
    args = list(xs) + [hot, cols, mod, weight]
    if not fresh:
        in_specs.append(full)
        args.append(acc)
    return pl.pallas_call(
        functools.partial(first_kernel, blocks, reqs, fresh),
        grid_spec=pltpu.PrefetchScalarGridSpec(
            num_scalar_prefetch=1,
            grid=(blocks,),
            in_specs=in_specs,
            out_specs=full,
        ),
        out_shape=jax.ShapeDtypeStruct((rows, hidden), F32),
        compiler_params=params(),
        cost_estimate=cost(2 * rows * feat * hidden * blocks, (blocks + 4) * feat * hidden * 2),
        name="first_blocks",
    )(idx, *args)


def finish_kernel(
    reqs, idx, ids, owned, x_ref, hot_ref, col_ref, mod_ref, w_ref, acc_ref, wide_ref,
    bias_ref, up_ref, recv_ref, w2_ref, act_out, part_out, up_now, sem,
):
    step = pl.program_id(0)

    @pl.when(step == 0)
    def _():
        fetch_adapters(ids, owned, up_ref, recv_ref, up_now, sem, False)

    lhs = normed(x_ref[...], hot_ref[...][:, :reqs], mod_ref, col_ref[...])
    pre = acc_ref[...] + jnp.dot(lhs, w_ref[...], preferred_element_type=F32)
    pre = pre + bias_ref[...].astype(F32)

    @pl.when(step == 0)
    def _():
        fetch_adapters(ids, owned, up_ref, recv_ref, up_now, sem, True)

    pre = pre + jnp.dot(wide_ref[...], up_now[...], preferred_element_type=F32)
    act = jax.nn.gelu(pre, approximate=True).astype(BF)
    act_out[...] = act
    part_out[...] = jnp.dot(act, w2_ref[...], preferred_element_type=F32).astype(BF)


def finish_call(idx, ids, owned, x, hot, cols, mod, weight, acc, wide, bias, up, recv, weight2, tiles):
    rows, feat = x.shape
    tile = rows // tiles
    hidden = weight.shape[1]
    reqs, rank = recv.shape[:2]
    tiled = lambda width: pl.BlockSpec((tile, width), lambda i, *s: (i, 0))
    return pl.pallas_call(
        functools.partial(finish_kernel, reqs),
        grid_spec=pltpu.PrefetchScalarGridSpec(
            num_scalar_prefetch=3,
            grid=(tiles,),
            in_specs=[
                tiled(feat),
                tiled(128),
                tiled(128),
                pl.BlockSpec((3, reqs, feat), lambda i, *s: (0, 0, s[0][0])),
                pl.BlockSpec((feat, hidden), lambda i, *s: (s[0][0], 0)),
                tiled(hidden),
                tiled(reqs * rank),
                pl.BlockSpec((1, hidden), lambda i, *s: (0, 0)),
                ANY,
                ANY,
                pl.BlockSpec((hidden, feat), lambda i, *s: (0, s[0][0])),
            ],
            out_specs=[tiled(hidden), tiled(feat)],
            scratch_shapes=[
                pltpu.VMEM((reqs * rank, hidden), BF),
                pltpu.SemaphoreType.DMA((reqs,)),
            ],
        ),
        out_shape=[
            jax.ShapeDtypeStruct((rows, hidden), BF),
            jax.ShapeDtypeStruct((rows, feat), BF),
        ],
        compiler_params=params(),
        cost_estimate=cost(
            2 * rows * hidden * (2 * feat + reqs * rank), 14 * rows * hidden, rows * hidden
        ),
        name="finish_first",
    )(idx, ids, owned, x, hot, cols, mod, weight, acc, wide, bias, up, recv, weight2)


def second_kernel(idx, act_ref, w_ref, out_ref):
    out_ref[0] = jnp.dot(act_ref[...], w_ref[...], preferred_element_type=F32)


def second_call(idx, act, weight2, feat):
    blocks = idx.shape[0]
    rows, hidden = act.shape
    return pl.pallas_call(
        second_kernel,
        grid_spec=pltpu.PrefetchScalarGridSpec(
            num_scalar_prefetch=1,
            grid=(blocks,),
            in_specs=[
                pl.BlockSpec((rows, hidden), lambda i, s: (0, 0)),
                pl.BlockSpec((hidden, feat), lambda i, s: (0, s[i])),
            ],
            out_specs=pl.BlockSpec((1, rows, feat), lambda i, s: (i, 0, 0)),
        ),
        out_shape=jax.ShapeDtypeStruct((blocks, rows, feat), F32),
        compiler_params=params(),
        cost_estimate=cost(2 * rows * hidden * feat * blocks, blocks * rows * feat * 8),
        name="second_blocks",
    )(idx, act, weight2)


def ring_device(
    count, tokens, modulation, adapter_per_request, tokens_per_request, first_weight,
    first_bias, second_weight, second_bias, adapter_down_matrices, adapter_up_matrices,
):
    me = lax.axis_index("tensor")
    store = lax.axis_index("store")
    rows, feat = tokens.shape
    hidden = first_weight.shape[1]
    stored, rank = adapter_up_matrices.shape[:2]
    reqs = tokens_per_request.shape[1]
    order = ring_order(count)
    forth = [(order[i], order[(i + 1) % count]) for i in range(count)]
    back = [(b, a) for a, b in forth]
    table = [[0] * count for _ in range(count)]
    for at, dev in enumerate(order):
        table[dev] = [order[(at + k) % count] for k in range(count)]
    mine = lax.dynamic_index_in_dim(jnp.array(table, jnp.int32), me, 0, keepdims=False)
    half = count // 2

    def at(*steps):
        return jnp.stack([mine[k % count] for k in steps])

    def go(x, route):
        return lax.ppermute(x, "tensor", route)

    down = jnp.swapaxes(adapter_down_matrices, 1, 2)
    mod = jnp.swapaxes(modulation[0], 0, 1)
    lengths = tokens_per_request[0]

    my_ids = lax.dynamic_index_in_dim(adapter_per_request, store, 0, keepdims=False)
    their_ids = lax.dynamic_index_in_dim(adapter_per_request, 1 - store, 0, keepdims=False)
    owned = (my_ids // stored == store).astype(jnp.int32)
    my_ids = jnp.clip(my_ids - store * stored, 0, stored - 1)
    their_ids = jnp.clip(their_ids - store * stored, 0, stored - 1)
    send_down, send_up = pl.pallas_call(
        send_kernel,
        in_specs=[SMEM, ANY, ANY],
        out_specs=[ANY, ANY],
        out_shape=[
            jax.ShapeDtypeStruct((reqs, rank, feat), BF),
            jax.ShapeDtypeStruct((reqs, rank, hidden), BF),
        ],
        scratch_shapes=[pltpu.SemaphoreType.DMA((2 * reqs,))],
        cost_estimate=cost(0, 4 * reqs * rank * (feat + hidden)),
        name="adapters_to_send",
    )(their_ids, down, adapter_up_matrices)
    swap = [(s, s ^ 1) for s in range(lax.axis_size("store"))]
    recv_down = lax.ppermute(send_down, "store", swap)
    recv_up = lax.ppermute(send_up, "store", swap)

    my_mod = lax.dynamic_slice_in_dim(mod, me * feat, feat, 2)
    low, stat, side, hot = pl.pallas_call(
        prep_kernel,
        in_specs=[SMEM, SMEM, SMEM, WHOLE, WHOLE, ANY, ANY],
        out_specs=[WHOLE] * 4,
        out_shape=[
            jax.ShapeDtypeStruct((rank, rows), BF),
            jax.ShapeDtypeStruct((8, rows), F32),
            jax.ShapeDtypeStruct((rank, 128), F32),
            jax.ShapeDtypeStruct((rows, 128), BF),
        ],
        scratch_shapes=[
            pltpu.VMEM((reqs * rank, feat), BF),
            pltpu.SemaphoreType.DMA((reqs,)),
        ],
        compiler_params=params(),
        cost_estimate=cost(2 * rows * feat * reqs * rank, 4 * rows * feat),
        name="own_features",
    )(my_ids, owned, lengths, tokens, my_mod, down, recv_down)
    span = 1
    while span < count:
        route = [(t, t ^ span) for t in range(count)]
        theirs = [go(v, route) for v in (low, stat, side)]
        last = 2 * span == count
        args = (low, stat, side, *theirs, hot)
        if last:
            kernel = functools.partial(last_merge_kernel, span * feat, reqs)
            shapes = [
                jax.ShapeDtypeStruct((rows, reqs * rank), BF),
                jax.ShapeDtypeStruct((rows, 128), F32),
            ]
        else:
            kernel = functools.partial(merge_kernel, span * feat)
            shapes = [jax.ShapeDtypeStruct(v.shape, v.dtype) for v in (low, stat, side)]
        out = pl.pallas_call(
            kernel,
            in_specs=[WHOLE] * 7,
            out_specs=[WHOLE] * len(shapes),
            out_shape=shapes,
            compiler_params=params(),
            cost_estimate=cost(2 * 6 * rank * 128 * rows, 8 * rank * rows),
            name="merge_sums",
        )(*args)
        if last:
            wide, cols = out
        else:
            low, stat, side = out
        span *= 2

    cut = rows // 2
    a = b = tokens
    seen = [(0, tokens)]
    for k in range(1, half):
        a, b = go(a, forth), go(b, back)
        seen += [(-k, a), (k, b)]
    far = jnp.concatenate([go(a[:cut], forth), go(b[cut:], back)])

    bias = first_bias.reshape(1, hidden)
    acc = None
    early = 2 * half - 3
    groups = [seen[:early], seen[early:]] if half > 2 else [seen]
    for group in groups:
        acc = first_call(
            at(*[k for k, _ in group]), [x for _, x in group], hot, cols, mod, first_weight, acc
        )
    act, far_part = finish_call(
        at(half), my_ids, owned, far, hot, cols, mod, first_weight, acc, wide, bias,
        adapter_up_matrices, recv_up, second_weight, 4,
    )

    steps = [s for k in range(half - 1, 0, -1) for s in (k, -k)] + [0]
    parts = {}
    for group in (steps[:2], steps[2:]):
        got = second_call(at(*group), act, second_weight, feat)
        for i, s in enumerate(group):
            parts[s] = got[i]
    gate = jnp.dot(
        hot[:, :reqs], lax.dynamic_slice_in_dim(mod[2], me * feat, feat, 1),
        preferred_element_type=F32,
    )
    outs = []
    chains = 2
    size = rows // chains
    for c in range(chains):
        lo = c * size
        mid = size // 2
        right = go(far_part[lo : lo + mid], forth)
        left = go(far_part[lo + mid : lo + size], back)
        for k in range(half - 1, 0, -1):
            r = parts[k][lo : lo + size]
            l = parts[-k][lo : lo + size]
            if k == half - 1:
                r = jnp.concatenate([r[:mid] + right.astype(F32), r[mid:]])
                l = jnp.concatenate([l[:mid], l[mid:] + left.astype(F32)])
            else:
                r = r + right.astype(F32)
                l = l + left.astype(F32)
            right = go(r.astype(BF), forth)
            left = go(l.astype(BF), back)
        mixed = parts[0][lo : lo + size] + right.astype(F32) + left.astype(F32)
        outs.append(
            tokens[lo : lo + size].astype(F32)
            + gate[lo : lo + size] * (mixed + second_bias.astype(F32))
        )
    return jnp.concatenate(outs).astype(BF)


def partner(block, axis, stride):
    count = lax.axis_size(axis)
    route = []
    for low in range(count):
        high = low | 1 << stride
        if high != low and high < count:
            route += [(low, high), (high, low)]
    return lax.ppermute(block, axis, route)


def request_onehot(lengths, row_count, req_count):
    bounds = jnp.cumsum(lengths)
    places = jnp.arange(row_count, dtype=jnp.int32)
    owner_req = jnp.sum((places[:, None] >= bounds[None, :]).astype(jnp.int32), axis=1)
    return (owner_req[:, None] == jnp.arange(req_count, dtype=jnp.int32)[None, :]).astype(
        jnp.float32
    )


def plain_device(
    tokens,
    modulation,
    adapter_per_request,
    tokens_per_request,
    first_weight,
    first_bias,
    second_weight,
    second_bias,
    adapter_down_matrices,
    adapter_up_matrices,
):
    tensor_index = lax.axis_index("tensor")
    store_index = lax.axis_index("store")
    tok_rows, feat_width = tokens.shape
    req_count = tokens_per_request.shape[1]
    rank_column_width = adapter_down_matrices.shape[2]
    hidden_width = first_weight.shape[1]
    store_request_count = adapter_down_matrices.shape[0]
    gathered = lax.all_gather(tokens, "tensor", axis=1, tiled=True).astype(jnp.float32)
    adapter_indicator = request_onehot(tokens_per_request[0], tok_rows, req_count)
    factors = modulation[0].astype(jnp.float32)
    shift_rows = jnp.dot(adapter_indicator, factors[:, 0], precision=lax.Precision.HIGHEST)
    scale_rows = jnp.dot(adapter_indicator, factors[:, 1], precision=lax.Precision.HIGHEST)
    gate_own = lax.dynamic_slice_in_dim(factors[:, 2], tensor_index * feat_width, feat_width, 1)
    gate_rows = jnp.dot(adapter_indicator, gate_own, precision=lax.Precision.HIGHEST)
    center = jnp.mean(gathered, axis=1, keepdims=True)
    spread = jnp.mean((gathered - center) ** 2, axis=1, keepdims=True)
    normed = (gathered - center) * lax.rsqrt(spread + 1e-06)
    modded = ((1.0 + scale_rows) * normed + shift_rows).astype(jnp.bfloat16)

    def pick_owned(wanted):
        owned_mask = wanted // store_request_count == store_index
        request_index_list = jnp.clip(
            wanted - store_index * store_request_count, 0, store_request_count - 1
        )
        down_matrix_rows = jnp.take(adapter_down_matrices, request_index_list, axis=0)
        up_matrix_rows = jnp.take(adapter_up_matrices, request_index_list, axis=0)
        keep = owned_mask[:, None, None]
        return (
            owned_mask,
            jnp.where(keep, down_matrix_rows, jnp.zeros_like(down_matrix_rows)),
            jnp.where(keep, up_matrix_rows, jnp.zeros_like(up_matrix_rows)),
        )

    mine_ids = lax.dynamic_index_in_dim(adapter_per_request, store_index, 0, keepdims=False)
    other_ids = lax.dynamic_index_in_dim(adapter_per_request, 1 - store_index, 0, keepdims=False)
    mine_owned, mine_down, mine_up = pick_owned(mine_ids)
    other_owned, send_down, send_up = pick_owned(other_ids)
    recv_down, recv_up = partner((send_down, send_up), "store", 0)
    down_now = jnp.where(mine_owned[:, None, None], mine_down, recv_down)
    up_now = jnp.where(mine_owned[:, None, None], mine_up, recv_up)
    low_rank_every = jnp.einsum(
        "tn,knr->tkr",
        modded,
        lax.all_gather(down_now, "tensor", axis=1, tiled=True),
        preferred_element_type=jnp.float32,
    )
    low_rank_sum = jnp.sum(adapter_indicator[:, :, None] * low_rank_every, axis=1)
    adapter_low_rank = low_rank_sum.astype(jnp.bfloat16)
    broadcast_low_rank = (
        (adapter_indicator[:, :, None] * adapter_low_rank.astype(jnp.float32)[:, None, :])
        .reshape(tok_rows, req_count * rank_column_width)
        .astype(jnp.bfloat16)
    )
    preact = jnp.dot(modded, first_weight, preferred_element_type=jnp.float32) + first_bias.astype(
        jnp.float32
    )
    preact = preact + jnp.dot(
        broadcast_low_rank,
        up_now.reshape(req_count * rank_column_width, hidden_width),
        preferred_element_type=jnp.float32,
    )
    activated = jax.nn.gelu(preact, approximate=True).astype(jnp.bfloat16)
    own_share = lax.psum_scatter(
        lax.dot_general(
            second_weight, activated, (((0,), (1,)), ((), ())), preferred_element_type=jnp.float32
        ),
        "tensor",
        scatter_dimension=0,
        tiled=True,
    ).T
    block_out = tokens.astype(jnp.float32) + gate_rows * (
        own_share + second_bias.astype(jnp.float32)
    )
    return block_out.astype(jnp.bfloat16)


def on_device(count, tokens, *rest):
    if tokens.shape[1] % 128 == 0 and count % 4 == 0 and count & (count - 1) == 0:
        return ring_device(count, tokens, *rest)
    return plain_device(tokens, *rest)


def solution(mesh):
    in_specs = (
        P(("groups", "store"), "tensor"),
        P(("groups", "store"), None, None, None),
        P("groups", None),
        P(("groups", "store"), None),
        P(None, "tensor"),
        P("tensor"),
        P("tensor", None),
        P("tensor"),
        P("store", "tensor", None),
        P("store", None, "tensor"),
    )
    out_specs = P(("groups", "store"), "tensor")
    return jax.shard_map(
        functools.partial(on_device, mesh.shape["tensor"]), mesh=mesh, in_specs=in_specs, out_specs=out_specs, check_vma=False
    )
```

```python
import functools

import jax
import jax.numpy as jnp
from jax import lax
from jax.experimental import pallas as pl
from jax.experimental.pallas import tpu as pltpu
from jax.sharding import PartitionSpec as P

BF = jnp.bfloat16
F32 = jnp.float32
VMEM_LIMIT = 56 * 1024 * 1024
HIGH = lax.Precision.HIGHEST
ANY = pl.BlockSpec(memory_space=pl.ANY)
SMEM = pl.BlockSpec(memory_space=pltpu.SMEM)
WHOLE = pl.BlockSpec(memory_space=pltpu.VMEM)


def params(**more):
    return pltpu.CompilerParams(vmem_limit_bytes=VMEM_LIMIT, **more)


def cost(flops, nbytes, trans=0):
    return pl.CostEstimate(
        flops=int(flops), bytes_accessed=int(nbytes), transcendentals=int(trans)
    )


def ring_order(count):
    cols = 2 if count < 32 else 4
    rows = count // cols
    walk = [r * cols for r in range(rows)]
    for i, r in enumerate(reversed(range(rows))):
        across = list(range(1, cols))
        walk += [r * cols + c for c in (across if i % 2 == 0 else across[::-1])]
    return walk


def send_kernel(ids, down_ref, up_ref, down_out, up_out, sem):
    count = down_out.shape[0]
    copies = []
    for r in range(count):
        copies.append(pltpu.make_async_copy(down_ref.at[ids[r]], down_out.at[r], sem.at[2 * r]))
        copies.append(pltpu.make_async_copy(up_ref.at[ids[r]], up_out.at[r], sem.at[2 * r + 1]))
    for c in copies:
        c.start()
    for c in copies:
        c.wait()


def fetch_adapters(ids, owned, store_ref, recv_ref, dst, sem, wait):
    count = recv_ref.shape[0]
    rank = recv_ref.shape[1]
    for r in range(count):
        here = dst.at[pl.ds(r * rank, rank)]
        if wait:
            pltpu.make_async_copy(recv_ref.at[r], here, sem.at[r]).wait()
            continue

        @pl.when(owned[r] == 1)
        def _():
            pltpu.make_async_copy(store_ref.at[ids[r]], here, sem.at[r]).start()

        @pl.when(owned[r] == 0)
        def _():
            pltpu.make_async_copy(recv_ref.at[r], here, sem.at[r]).start()


def prep_kernel(
    ids, owned, lengths, x_ref, mod_ref, down_ref, recv_ref,
    low_out, stat_out, side_out, hot_out, down_now, sem,
):
    rows, feat = x_ref.shape
    reqs = recv_ref.shape[0]
    rank = recv_ref.shape[1]
    fetch_adapters(ids, owned, down_ref, recv_ref, down_now, sem, False)
    x = x_ref[...].astype(F32)
    mean = jnp.mean(x, axis=1, keepdims=True)
    cent = x - mean
    m2 = jnp.sum(cent * cent, axis=1, keepdims=True)
    row = lax.broadcasted_iota(jnp.int32, (rows, 128), 0)
    lane = lax.broadcasted_iota(jnp.int32, (rows, 128), 1)
    hot = jnp.zeros((rows, 128), F32)
    begin = jnp.int32(0)
    for r in range(reqs):
        end = begin + lengths[r]
        hot = jnp.where((lane == r) & (row >= begin) & (row < end), 1.0, hot)
        begin = end
    hot_out[...] = hot.astype(BF)
    stat_out[...] = jnp.where(lane == 0, mean, jnp.where(lane == 1, m2, 0.0)).T[:8]
    hot8 = hot[:, :reqs].astype(BF)
    scale_rows = jnp.dot(hot8, mod_ref[1], preferred_element_type=F32)
    lhs = (cent * (1.0 + scale_rows)).astype(BF)
    hot_t = hot.T
    fetch_adapters(ids, owned, down_ref, recv_ref, down_now, sem, True)
    every = lax.dot_general(
        down_now[...], lhs, (((1,), (1,)), ((), ())), preferred_element_type=F32
    )
    total = jnp.zeros((rank, rows), F32)
    side = jnp.zeros((rank, 128), F32)
    lane_s = lax.broadcasted_iota(jnp.int32, (rank, 128), 1)
    for r in range(reqs):
        total = total + every[r * rank : (r + 1) * rank] * hot_t[r : r + 1]
        mat = down_now[pl.ds(r * rank, rank), :].astype(F32)
        per_scale = jnp.sum(mat * (1.0 + mod_ref[1, pl.ds(r, 1), :].astype(F32)), axis=1, keepdims=True)
        per_shift = jnp.sum(mat * mod_ref[0, pl.ds(r, 1), :].astype(F32), axis=1, keepdims=True)
        side = jnp.where(lane_s == r, per_scale, side)
        side = jnp.where(lane_s == reqs + r, per_shift, side)
    low_out[...] = total.astype(BF)
    side_out[...] = side


def merge(count, low_a, stat_a, side_a, low_b, stat_b, side_b, hot_ref):
    hot_t = hot_ref[...].astype(F32).T
    sa, sb = stat_a[...], stat_b[...]
    gap = sa[0:1] - sb[0:1]
    mean = 0.5 * (sa[0:1] + sb[0:1])
    m2 = sa[1:2] + sb[1:2] + gap * gap * (count * 0.5)
    fa, fb = side_a[...], side_b[...]
    back = jnp.dot(fa - fb, hot_t, precision=HIGH, preferred_element_type=F32)
    low = low_a[...].astype(F32) + low_b[...].astype(F32) + (0.5 * gap) * back
    return low, mean, m2, fa + fb, hot_t


def merge_kernel(count, *refs):
    low_out, stat_out, side_out = refs[-3:]
    low, mean, m2, side, _ = merge(count, *refs[:-3])
    low_out[...] = low.astype(BF)
    stat_out[...] = jnp.concatenate([mean, m2, jnp.zeros((6, mean.shape[1]), F32)], axis=0)
    side_out[...] = side


def last_merge_kernel(count, reqs, *refs):
    wide_out, col_out = refs[-2:]
    low, mean, m2, side, hot_t = merge(count, *refs[:-2])
    rank, rows = low.shape
    rstd = lax.rsqrt(m2 / (2 * count) + 1e-06)
    sums = jnp.dot(pltpu.roll(side, 128 - reqs, 1), hot_t, precision=HIGH, preferred_element_type=F32)
    low = (low * rstd + sums).astype(BF).astype(F32)
    low = jnp.concatenate([low] * (128 // rank), axis=0).T.astype(BF)[:, :rank]
    src = lax.broadcasted_iota(jnp.int32, (rank, reqs * rank), 0)
    dst = lax.broadcasted_iota(jnp.int32, (rank, reqs * rank), 1)
    spread = jnp.where(dst % rank == src, 1.0, 0.0).astype(BF)
    hot8 = refs[6][...][:, :reqs]
    who = lax.broadcasted_iota(jnp.int32, (reqs, reqs * rank), 0)
    col = lax.broadcasted_iota(jnp.int32, (reqs, reqs * rank), 1)
    mask = jnp.dot(
        hot8, jnp.where(col // rank == who, 1.0, 0.0).astype(BF), preferred_element_type=F32
    )
    wide_out[...] = (jnp.dot(low, spread, preferred_element_type=F32) * mask).astype(BF)
    both = jnp.concatenate([mean, rstd, jnp.zeros((126, rows), F32)], axis=0)
    col_out[...] = both.T


def normed(x, hot8, mod_ref, cols):
    scale_rows = jnp.dot(hot8, mod_ref[1], preferred_element_type=F32)
    shift_rows = jnp.dot(hot8, mod_ref[0], preferred_element_type=F32)
    flat = (x.astype(F32) - cols[:, 0:1]) * cols[:, 1:2]
    return ((1.0 + scale_rows) * flat + shift_rows).astype(BF)


def first_kernel(blocks, reqs, fresh, idx, *refs):
    xs = refs[:blocks]
    hot_ref, col_ref, mod_ref, w_ref = refs[blocks : blocks + 4]
    acc_in = None if fresh else refs[blocks + 4]
    acc_out = refs[-1]
    step = pl.program_id(0)
    hot8 = hot_ref[...][:, :reqs]
    cols = col_ref[...]
    for k in range(blocks):

        @pl.when(step == k)
        def _(k=k):
            lhs = normed(xs[k][...], hot8, mod_ref, cols)
            part = jnp.dot(lhs, w_ref[...], preferred_element_type=F32)
            if k == 0 and fresh:
                acc_out[...] = part
            elif k == 0:
                acc_out[...] = acc_in[...] + part
            else:
                acc_out[...] += part


def first_call(idx, base, xs, hot, cols, mod, weight, acc):
    blocks = len(xs)
    rows, feat = xs[0].shape
    hidden = weight.shape[1]
    reqs = mod.shape[1]
    fresh = acc is None
    full = pl.BlockSpec((rows, hidden), lambda i, s: (0, 0))
    in_specs = [pl.BlockSpec((rows, feat), lambda i, s: (0, 0))] * blocks + [
        pl.BlockSpec((rows, 128), lambda i, s: (0, 0)),
        pl.BlockSpec((rows, 128), lambda i, s: (0, 0)),
        pl.BlockSpec((3, reqs, feat), lambda i, s: (0, 0, s[base + i])),
        pl.BlockSpec((feat, hidden), lambda i, s: (s[base + i], 0)),
    ]
    args = list(xs) + [hot, cols, mod, weight]
    if not fresh:
        in_specs.append(full)
        args.append(acc)
    return pl.pallas_call(
        functools.partial(first_kernel, blocks, reqs, fresh),
        grid_spec=pltpu.PrefetchScalarGridSpec(
            num_scalar_prefetch=1,
            grid=(blocks,),
            in_specs=in_specs,
            out_specs=full,
        ),
        out_shape=jax.ShapeDtypeStruct((rows, hidden), F32),
        compiler_params=params(),
        cost_estimate=cost(2 * rows * feat * hidden * blocks, (blocks + 4) * feat * hidden * 2),
        name="first_blocks",
    )(idx, *args)


def finish_kernel(
    reqs, idx, ids, owned, x_ref, hot_ref, col_ref, mod_ref, w_ref, acc_ref, wide_ref,
    bias_ref, up_ref, recv_ref, w2_ref, act_out, part_out, up_now, sem,
):
    step = pl.program_id(0)

    @pl.when(step == 0)
    def _():
        fetch_adapters(ids, owned, up_ref, recv_ref, up_now, sem, False)

    lhs = normed(x_ref[...], hot_ref[...][:, :reqs], mod_ref, col_ref[...])
    pre = acc_ref[...] + jnp.dot(lhs, w_ref[...], preferred_element_type=F32)
    pre = pre + bias_ref[...].astype(F32)

    @pl.when(step == 0)
    def _():
        fetch_adapters(ids, owned, up_ref, recv_ref, up_now, sem, True)

    pre = pre + jnp.dot(wide_ref[...], up_now[...], preferred_element_type=F32)
    act = jax.nn.gelu(pre, approximate=True).astype(BF)
    act_out[...] = act
    part_out[...] = jnp.dot(act, w2_ref[...], preferred_element_type=F32).astype(BF)


def finish_call(idx, base, ids, owned, x, hot, cols, mod, weight, acc, wide, bias, up, recv, weight2, tiles):
    rows, feat = x.shape
    tile = rows // tiles
    hidden = weight.shape[1]
    reqs, rank = recv.shape[:2]
    tiled = lambda width: pl.BlockSpec((tile, width), lambda i, *s: (i, 0))
    return pl.pallas_call(
        functools.partial(finish_kernel, reqs),
        grid_spec=pltpu.PrefetchScalarGridSpec(
            num_scalar_prefetch=3,
            grid=(tiles,),
            in_specs=[
                tiled(feat),
                tiled(128),
                tiled(128),
                pl.BlockSpec((3, reqs, feat), lambda i, *s: (0, 0, s[0][base])),
                pl.BlockSpec((feat, hidden), lambda i, *s: (s[0][base], 0)),
                tiled(hidden),
                tiled(reqs * rank),
                pl.BlockSpec((1, hidden), lambda i, *s: (0, 0)),
                ANY,
                ANY,
                pl.BlockSpec((hidden, feat), lambda i, *s: (0, s[0][base])),
            ],
            out_specs=[tiled(hidden), tiled(feat)],
            scratch_shapes=[
                pltpu.VMEM((reqs * rank, hidden), BF),
                pltpu.SemaphoreType.DMA((reqs,)),
            ],
        ),
        out_shape=[
            jax.ShapeDtypeStruct((rows, hidden), BF),
            jax.ShapeDtypeStruct((rows, feat), BF),
        ],
        compiler_params=params(),
        cost_estimate=cost(
            2 * rows * hidden * (2 * feat + reqs * rank), 14 * rows * hidden, rows * hidden
        ),
        name="finish_first",
    )(idx, ids, owned, x, hot, cols, mod, weight, acc, wide, bias, up, recv, weight2)


def second_kernel(idx, act_ref, w_ref, out_ref):
    out_ref[0] = jnp.dot(act_ref[...], w_ref[...], preferred_element_type=F32)


def second_call(idx, base, blocks, act, weight2, feat):
    rows, hidden = act.shape
    return pl.pallas_call(
        second_kernel,
        grid_spec=pltpu.PrefetchScalarGridSpec(
            num_scalar_prefetch=1,
            grid=(blocks,),
            in_specs=[
                pl.BlockSpec((rows, hidden), lambda i, s: (0, 0)),
                pl.BlockSpec((hidden, feat), lambda i, s: (0, s[base - i])),
            ],
            out_specs=pl.BlockSpec((1, rows, feat), lambda i, s: (i, 0, 0)),
        ),
        out_shape=jax.ShapeDtypeStruct((blocks, rows, feat), F32),
        compiler_params=params(),
        cost_estimate=cost(2 * rows * hidden * feat * blocks, blocks * rows * feat * 8),
        name="second_blocks",
    )(idx, act, weight2)


def ring_device(
    count, tokens, modulation, adapter_per_request, tokens_per_request, first_weight,
    first_bias, second_weight, second_bias, adapter_down_matrices, adapter_up_matrices,
):
    me = lax.axis_index("tensor")
    store = lax.axis_index("store")
    rows, feat = tokens.shape
    hidden = first_weight.shape[1]
    stored, rank = adapter_up_matrices.shape[:2]
    reqs = tokens_per_request.shape[1]
    order = ring_order(count)
    forth = [(order[i], order[(i + 1) % count]) for i in range(count)]
    back = [(b, a) for a, b in forth]
    table = [[0] * count for _ in range(count)]
    half = count // 2
    visits = [0] + [s for k in range(1, half) for s in (-k, k)] + [half]
    for at, dev in enumerate(order):
        table[dev] = [order[(at + k) % count] for k in visits]
    mine = lax.dynamic_index_in_dim(jnp.array(table, jnp.int32), me, 0, keepdims=False)
    def go(x, route):
        return lax.ppermute(x, "tensor", route)

    down = jnp.swapaxes(adapter_down_matrices, 1, 2)
    mod = jnp.swapaxes(modulation[0], 0, 1)
    lengths = tokens_per_request[0]

    my_ids = lax.dynamic_index_in_dim(adapter_per_request, store, 0, keepdims=False)
    their_ids = lax.dynamic_index_in_dim(adapter_per_request, 1 - store, 0, keepdims=False)
    owned = (my_ids // stored == store).astype(jnp.int32)
    my_ids = jnp.clip(my_ids - store * stored, 0, stored - 1)
    their_ids = jnp.clip(their_ids - store * stored, 0, stored - 1)
    send_down, send_up = pl.pallas_call(
        send_kernel,
        in_specs=[SMEM, ANY, ANY],
        out_specs=[WHOLE, WHOLE],
        out_shape=[
            jax.ShapeDtypeStruct((reqs, rank, feat), BF),
            jax.ShapeDtypeStruct((reqs, rank, hidden), BF),
        ],
        scratch_shapes=[pltpu.SemaphoreType.DMA((2 * reqs,))],
        compiler_params=params(),
        cost_estimate=cost(0, 4 * reqs * rank * (feat + hidden)),
        name="adapters_to_send",
    )(their_ids, down, adapter_up_matrices)
    swap = [(s, s ^ 1) for s in range(lax.axis_size("store"))]
    recv_down = lax.ppermute(send_down, "store", swap)
    recv_up = lax.ppermute(send_up, "store", swap)

    my_mod = lax.dynamic_slice_in_dim(mod, me * feat, feat, 2)
    low, stat, side, hot = pl.pallas_call(
        prep_kernel,
        in_specs=[SMEM, SMEM, SMEM, WHOLE, WHOLE, ANY, ANY],
        out_specs=[WHOLE] * 4,
        out_shape=[
            jax.ShapeDtypeStruct((rank, rows), BF),
            jax.ShapeDtypeStruct((8, rows), F32),
            jax.ShapeDtypeStruct((rank, 128), F32),
            jax.ShapeDtypeStruct((rows, 128), BF),
        ],
        scratch_shapes=[
            pltpu.VMEM((reqs * rank, feat), BF),
            pltpu.SemaphoreType.DMA((reqs,)),
        ],
        compiler_params=params(),
        cost_estimate=cost(2 * rows * feat * reqs * rank, 4 * rows * feat),
        name="own_features",
    )(my_ids, owned, lengths, tokens, my_mod, down, recv_down)
    span = 1
    while span < count:
        route = [(t, t ^ span) for t in range(count)]
        theirs = [go(v, route) for v in (low, stat, side)]
        last = 2 * span == count
        args = (low, stat, side, *theirs, hot)
        if last:
            kernel = functools.partial(last_merge_kernel, span * feat, reqs)
            shapes = [
                jax.ShapeDtypeStruct((rows, reqs * rank), BF),
                jax.ShapeDtypeStruct((rows, 128), F32),
            ]
        else:
            kernel = functools.partial(merge_kernel, span * feat)
            shapes = [jax.ShapeDtypeStruct(v.shape, v.dtype) for v in (low, stat, side)]
        out = pl.pallas_call(
            kernel,
            in_specs=[WHOLE] * 7,
            out_specs=[WHOLE] * len(shapes),
            out_shape=shapes,
            compiler_params=params(),
            cost_estimate=cost(2 * 6 * rank * 128 * rows, 8 * rank * rows),
            name="merge_sums",
        )(*args)
        if last:
            wide, cols = out
        else:
            low, stat, side = out
        span *= 2

    cut = rows // 2
    a = b = tokens
    seen = [(0, tokens)]
    for k in range(1, half):
        a, b = go(a, forth), go(b, back)
        seen += [(-k, a), (k, b)]
    far = jnp.concatenate([go(a[:cut], forth), go(b[cut:], back)])

    bias = first_bias.reshape(1, hidden)
    acc = None
    early = 2 * half - 3
    groups = [seen[:early], seen[early:]] if half > 2 else [seen]
    base = 0
    for group in groups:
        acc = first_call(
            mine, base, [x for _, x in group], hot, cols, mod, first_weight, acc
        )
        base += len(group)
    act, far_part = finish_call(
        mine, base, my_ids, owned, far, hot, cols, mod, first_weight, acc, wide, bias,
        adapter_up_matrices, recv_up, second_weight, 4,
    )

    steps = [s for k in range(half - 1, 0, -1) for s in (k, -k)] + [0]
    parts = {}
    base = count - 2
    for group in (steps[:2], steps[2:]):
        got = second_call(mine, base, len(group), act, second_weight, feat)
        base -= len(group)
        for i, s in enumerate(group):
            parts[s] = got[i]
    gate = jnp.dot(
        hot[:, :reqs], lax.dynamic_slice_in_dim(mod[2], me * feat, feat, 1),
        preferred_element_type=F32,
    )
    outs = []
    chains = 2
    size = rows // chains
    for c in range(chains):
        lo = c * size
        mid = size // 2
        right = go(far_part[lo : lo + mid], forth)
        left = go(far_part[lo + mid : lo + size], back)
        for k in range(half - 1, 0, -1):
            r = parts[k][lo : lo + size]
            l = parts[-k][lo : lo + size]
            if k == half - 1:
                r = jnp.concatenate([r[:mid] + right.astype(F32), r[mid:]])
                l = jnp.concatenate([l[:mid], l[mid:] + left.astype(F32)])
            else:
                r = r + right.astype(F32)
                l = l + left.astype(F32)
            right = go(r.astype(BF), forth)
            left = go(l.astype(BF), back)
        mixed = parts[0][lo : lo + size] + right.astype(F32) + left.astype(F32)
        outs.append(
            tokens[lo : lo + size].astype(F32)
            + gate[lo : lo + size] * (mixed + second_bias.astype(F32))
        )
    return jnp.concatenate(outs).astype(BF)


def partner(block, axis, stride):
    count = lax.axis_size(axis)
    route = []
    for low in range(count):
        high = low | 1 << stride
        if high != low and high < count:
            route += [(low, high), (high, low)]
    return lax.ppermute(block, axis, route)


def request_onehot(lengths, row_count, req_count):
    bounds = jnp.cumsum(lengths)
    places = jnp.arange(row_count, dtype=jnp.int32)
    owner_req = jnp.sum((places[:, None] >= bounds[None, :]).astype(jnp.int32), axis=1)
    return (owner_req[:, None] == jnp.arange(req_count, dtype=jnp.int32)[None, :]).astype(
        jnp.float32
    )


def plain_device(
    tokens,
    modulation,
    adapter_per_request,
    tokens_per_request,
    first_weight,
    first_bias,
    second_weight,
    second_bias,
    adapter_down_matrices,
    adapter_up_matrices,
):
    tensor_index = lax.axis_index("tensor")
    store_index = lax.axis_index("store")
    tok_rows, feat_width = tokens.shape
    req_count = tokens_per_request.shape[1]
    rank_column_width = adapter_down_matrices.shape[2]
    hidden_width = first_weight.shape[1]
    store_request_count = adapter_down_matrices.shape[0]
    gathered = lax.all_gather(tokens, "tensor", axis=1, tiled=True).astype(jnp.float32)
    adapter_indicator = request_onehot(tokens_per_request[0], tok_rows, req_count)
    factors = modulation[0].astype(jnp.float32)
    shift_rows = jnp.dot(adapter_indicator, factors[:, 0], precision=lax.Precision.HIGHEST)
    scale_rows = jnp.dot(adapter_indicator, factors[:, 1], precision=lax.Precision.HIGHEST)
    gate_own = lax.dynamic_slice_in_dim(factors[:, 2], tensor_index * feat_width, feat_width, 1)
    gate_rows = jnp.dot(adapter_indicator, gate_own, precision=lax.Precision.HIGHEST)
    center = jnp.mean(gathered, axis=1, keepdims=True)
    spread = jnp.mean((gathered - center) ** 2, axis=1, keepdims=True)
    normed = (gathered - center) * lax.rsqrt(spread + 1e-06)
    modded = ((1.0 + scale_rows) * normed + shift_rows).astype(jnp.bfloat16)

    def pick_owned(wanted):
        owned_mask = wanted // store_request_count == store_index
        request_index_list = jnp.clip(
            wanted - store_index * store_request_count, 0, store_request_count - 1
        )
        down_matrix_rows = jnp.take(adapter_down_matrices, request_index_list, axis=0)
        up_matrix_rows = jnp.take(adapter_up_matrices, request_index_list, axis=0)
        keep = owned_mask[:, None, None]
        return (
            owned_mask,
            jnp.where(keep, down_matrix_rows, jnp.zeros_like(down_matrix_rows)),
            jnp.where(keep, up_matrix_rows, jnp.zeros_like(up_matrix_rows)),
        )

    mine_ids = lax.dynamic_index_in_dim(adapter_per_request, store_index, 0, keepdims=False)
    other_ids = lax.dynamic_index_in_dim(adapter_per_request, 1 - store_index, 0, keepdims=False)
    mine_owned, mine_down, mine_up = pick_owned(mine_ids)
    other_owned, send_down, send_up = pick_owned(other_ids)
    recv_down, recv_up = partner((send_down, send_up), "store", 0)
    down_now = jnp.where(mine_owned[:, None, None], mine_down, recv_down)
    up_now = jnp.where(mine_owned[:, None, None], mine_up, recv_up)
    low_rank_every = jnp.einsum(
        "tn,knr->tkr",
        modded,
        lax.all_gather(down_now, "tensor", axis=1, tiled=True),
        preferred_element_type=jnp.float32,
    )
    low_rank_sum = jnp.sum(adapter_indicator[:, :, None] * low_rank_every, axis=1)
    adapter_low_rank = low_rank_sum.astype(jnp.bfloat16)
    broadcast_low_rank = (
        (adapter_indicator[:, :, None] * adapter_low_rank.astype(jnp.float32)[:, None, :])
        .reshape(tok_rows, req_count * rank_column_width)
        .astype(jnp.bfloat16)
    )
    preact = jnp.dot(modded, first_weight, preferred_element_type=jnp.float32) + first_bias.astype(
        jnp.float32
    )
    preact = preact + jnp.dot(
        broadcast_low_rank,
        up_now.reshape(req_count * rank_column_width, hidden_width),
        preferred_element_type=jnp.float32,
    )
    activated = jax.nn.gelu(preact, approximate=True).astype(jnp.bfloat16)
    own_share = lax.psum_scatter(
        lax.dot_general(
            second_weight, activated, (((0,), (1,)), ((), ())), preferred_element_type=jnp.float32
        ),
        "tensor",
        scatter_dimension=0,
        tiled=True,
    ).T
    block_out = tokens.astype(jnp.float32) + gate_rows * (
        own_share + second_bias.astype(jnp.float32)
    )
    return block_out.astype(jnp.bfloat16)


def on_device(count, tokens, *rest):
    if tokens.shape[1] % 128 == 0 and count % 4 == 0 and count & (count - 1) == 0:
        return ring_device(count, tokens, *rest)
    return plain_device(tokens, *rest)


def solution(mesh):
    in_specs = (
        P(("groups", "store"), "tensor"),
        P(("groups", "store"), None, None, None),
        P("groups", None),
        P(("groups", "store"), None),
        P(None, "tensor"),
        P("tensor"),
        P("tensor", None),
        P("tensor"),
        P("store", "tensor", None),
        P("store", None, "tensor"),
    )
    out_specs = P(("groups", "store"), "tensor")
    return jax.shard_map(
        functools.partial(on_device, mesh.shape["tensor"]), mesh=mesh, in_specs=in_specs, out_specs=out_specs, check_vma=False
    )
```

```python
import functools

import jax
import jax.numpy as jnp
from jax import lax
from jax.experimental import pallas as pl
from jax.experimental.pallas import tpu as pltpu
from jax.sharding import PartitionSpec as P

BF = jnp.bfloat16
F32 = jnp.float32
VMEM_LIMIT = 24 * 1024 * 1024
HIGH = lax.Precision.HIGHEST
ANY = pl.BlockSpec(memory_space=pltpu.HBM)
SMEM = pl.BlockSpec(memory_space=pltpu.SMEM)
WHOLE = pl.BlockSpec(memory_space=pltpu.VMEM)


def params(**more):
    return pltpu.CompilerParams(vmem_limit_bytes=VMEM_LIMIT, **more)


def cost(flops, nbytes, trans=0):
    return pl.CostEstimate(
        flops=int(flops), bytes_accessed=int(nbytes), transcendentals=int(trans)
    )


def ring_order(count):
    cols = 2 if count < 32 else 4
    rows = count // cols
    walk = [r * cols for r in range(rows)]
    for i, r in enumerate(reversed(range(rows))):
        across = list(range(1, cols))
        walk += [r * cols + c for c in (across if i % 2 == 0 else across[::-1])]
    return walk


def blocks_in(ref, width, at, axis):
    place = pl.ds(pl.multiple_of(at * width, width), width)
    return ref.at[place, :] if axis == 0 else ref.at[:, place]


def send_kernel(count, ints, down_ref, up_ref, down_out, up_out, sem):
    reqs = down_out.shape[0]
    copies = []
    for r in range(reqs):
        at = ints[count + reqs + r]
        copies.append(pltpu.make_async_copy(down_ref.at[at], down_out.at[r], sem.at[2 * r]))
        copies.append(pltpu.make_async_copy(up_ref.at[at], up_out.at[r], sem.at[2 * r + 1]))
    for c in copies:
        c.start()
    for c in copies:
        c.wait()


def fetch_adapters(count, ints, store_ref, recv_ref, dst, sem, wait):
    reqs, rank = recv_ref.shape[:2]
    for r in range(reqs):
        here = dst.at[pl.ds(r * rank, rank)]
        if wait:
            pltpu.make_async_copy(recv_ref.at[r], here, sem.at[r]).wait()
            continue
        own = ints[count + 2 * reqs + r]

        @pl.when(own == 1)
        def _():
            pltpu.make_async_copy(store_ref.at[ints[count + r]], here, sem.at[r]).start()

        @pl.when(own == 0)
        def _():
            pltpu.make_async_copy(recv_ref.at[r], here, sem.at[r]).start()


def own_kernel(ints, lengths, x_ref, mod_ref, u_out, hot_out, stat_out):
    rows, feat = x_ref.shape
    reqs = mod_ref.shape[1]
    x = x_ref[...].astype(F32)
    mean = jnp.mean(x, axis=1, keepdims=True)
    cent = x - mean
    m2 = jnp.sum(cent * cent, axis=1, keepdims=True)
    row = lax.broadcasted_iota(jnp.int32, (rows, 128), 0)
    lane = lax.broadcasted_iota(jnp.int32, (rows, 128), 1)
    first = jnp.zeros((1, 128), jnp.int32)
    after = jnp.zeros((1, 128), jnp.int32)
    lane1 = lax.broadcasted_iota(jnp.int32, (1, 128), 1)
    begin = jnp.int32(0)
    for r in range(reqs):
        end = begin + lengths[r]
        first = jnp.where(lane1 == r, begin, first)
        after = jnp.where(lane1 == r, end, after)
        begin = end
    hot = jnp.where((row >= first) & (row < after), 1.0, 0.0)
    hot_out[...] = hot.astype(BF)
    stat_out[...] = jnp.where(lane == 0, mean, jnp.where(lane == 1, m2, 0.0)).T[:8]
    scale_rows = jnp.dot(hot[:, :reqs].astype(BF), mod_ref[1], preferred_element_type=F32)
    u_out[...] = (cent * (1.0 + scale_rows)).astype(BF)


def low_kernel(
    count, ints, u_ref, hot_ref, stat_ref, mod_ref, down_ref, recv_ref, after_ref, low_out, pack_out, down_now, sem
):
    rows, feat = u_ref.shape
    reqs, rank = recv_ref.shape[:2]
    fetch_adapters(count, ints, down_ref, recv_ref, down_now, sem, False)
    hot_t = hot_ref[...].astype(F32).T
    fetch_adapters(count, ints, down_ref, recv_ref, down_now, sem, True)
    every = lax.dot_general(
        down_now[...], u_ref[...], (((1,), (1,)), ((), ())), preferred_element_type=F32
    )
    total = jnp.zeros((rank, rows), F32)
    side = jnp.zeros((rank, 128), F32)
    lane = lax.broadcasted_iota(jnp.int32, (rank, 128), 1)
    for r in range(reqs):
        total = total + every[r * rank : (r + 1) * rank] * hot_t[r : r + 1]
        mat = down_now[pl.ds(r * rank, rank), :].astype(F32)
        by_scale = jnp.sum(mat * (1.0 + mod_ref[1, pl.ds(r, 1), :].astype(F32)), axis=1, keepdims=True)
        by_shift = jnp.sum(mat * mod_ref[0, pl.ds(r, 1), :].astype(F32), axis=1, keepdims=True)
        side = jnp.where(lane == r, by_scale, side)
        side = jnp.where(lane == reqs + r, by_shift, side)
    low_out[...] = total.astype(BF)
    stat = stat_ref[...]
    here = lax.broadcasted_iota(jnp.int32, (count, rows), 0) == ints[0]
    pack_out[pl.ds(0, count), :] = jnp.where(here, stat[0:1], 0.0)
    turned = jnp.concatenate([side, jnp.zeros((128 - rank, 128), F32)], axis=0).T
    flat = jnp.concatenate([turned[: 2 * reqs], jnp.zeros((2 * reqs, rows - 128), F32)], axis=1)
    pack_out[pl.ds(count, 2 * reqs), :] = flat
    pack_out[pl.ds(count + 2 * reqs, 8), :] = jnp.broadcast_to(stat[1:2], (8, rows))


def merge(count, span, reqs, low_a, pack_a, low_b, pack_b, hot_ref):
    hot_t = hot_ref[...].astype(F32).T[:reqs]
    pa, pb = pack_a[...], pack_b[...]
    rank = low_a.shape[0]
    gap = (jnp.sum(pa[:count], axis=0, keepdims=True) - jnp.sum(pb[:count], axis=0, keepdims=True)) / span
    diff = (pa - pb)[count : count + reqs, :rank]
    back = lax.dot_general(
        diff, hot_t, (((0,), (0,)), ((), ())), precision=HIGH, preferred_element_type=F32
    )
    low = low_a[...].astype(F32) + low_b[...].astype(F32) + (0.5 * gap) * back
    return low, pa + pb, hot_t


def merge_kernel(count, span, reqs, *refs):
    low, pack, _ = merge(count, span, reqs, *refs[:5])
    refs[5][...] = low.astype(BF)
    refs[6][...] = pack


def last_merge_kernel(count, span, reqs, feat, *refs):
    wide_out, col_out = refs[5:]
    low, pack, hot_t = merge(count, span, reqs, *refs[:5])
    rank, rows = low.shape
    means = pack[:count]
    mean = jnp.sum(means, axis=0, keepdims=True) / count
    dev = means - mean
    m2 = pack[count + 2 * reqs : count + 2 * reqs + 1] + feat * jnp.sum(dev * dev, axis=0, keepdims=True)
    rstd = lax.rsqrt(m2 / (count * feat) + 1e-06)
    shifted = lax.dot_general(
        pack[count + reqs : count + 2 * reqs, :rank], hot_t, (((0,), (0,)), ((), ())),
        precision=HIGH, preferred_element_type=F32,
    )
    low = (low * rstd + shifted).astype(BF).astype(F32)
    pad = 128 - rank - count - 1
    turned = jnp.concatenate([low, dev * rstd, rstd, jnp.zeros((pad, rows), F32)], axis=0).T
    col_out[...] = jnp.broadcast_to(turned[:, rank + count : rank + count + 1], (rows, 128))
    turned = turned.astype(BF)
    hot8 = refs[4][...][:, :reqs]

    def spread(src_count, width, rule):
        src = lax.broadcasted_iota(jnp.int32, (src_count, width), 0)
        dst = lax.broadcasted_iota(jnp.int32, (src_count, width), 1)
        return jnp.where(rule(src, dst), 1.0, 0.0).astype(BF)

    def times(a, b):
        return jnp.dot(a, b, preferred_element_type=F32)

    width = reqs * rank
    lora = times(turned, spread(128, width, lambda s, d: (d % rank == s) & (s < rank)))
    lora = lora * times(hot8, spread(reqs, width, lambda s, d: d // rank == s))
    pairs = count * reqs
    coef = times(turned, spread(128, 128, lambda s, d: (s == rank + d // reqs) & (d < pairs)))
    coef = coef * times(hot8, spread(reqs, 128, lambda s, d: (d % reqs == s) & (d < pairs)))
    coef = coef + times(
        hot8, spread(reqs, 128, lambda s, d: (d % reqs == s) & (d >= pairs) & (d < pairs + 2 * reqs))
    )
    wide_out[:, pl.ds(0, width)] = lora.astype(BF)
    wide_out[:, pl.ds(width, 128)] = coef.astype(BF)


def means_kernel(count, mod_ref, w_ref, bias_ref, after_ref, out_ref, total):
    step = pl.program_id(0)
    reqs = mod_ref.shape[1]
    feat = mod_ref.shape[2]
    lhs = jnp.concatenate([jnp.ones((reqs, feat), F32), mod_ref[1].astype(F32), mod_ref[0].astype(F32)], axis=0)
    lhs = jnp.concatenate([lhs, jnp.zeros((8, feat), F32)], axis=0).astype(BF)
    got = jnp.dot(lhs, w_ref[...], preferred_element_type=F32)
    total[0, pl.ds(pl.multiple_of(step * reqs, reqs), reqs), :] = got[:reqs] + got[reqs : 2 * reqs]

    @pl.when(step == 0)
    def _():
        total[1, pl.ds(0, reqs), :] = got[2 * reqs : 3 * reqs] + bias_ref[...].astype(F32)

    @pl.when(step > 0)
    def _():
        total[1, pl.ds(0, reqs), :] += got[2 * reqs : 3 * reqs]

    @pl.when(step == count - 1)
    def _():
        shift = total[1, pl.ds(0, reqs), :]
        high = shift.astype(BF).astype(F32)
        both = jnp.concatenate([high, shift - high], axis=0)
        left = 128 - count * reqs - 2 * reqs
        rows = [total[0, pl.ds(0, count * reqs), :], both]
        if left:
            rows.append(jnp.zeros((left, both.shape[1]), F32))
        out_ref[...] = jnp.concatenate(rows, axis=0).astype(BF)


N_TILE = 512


def first_kernel(count, blocks, base, ints, *refs):
    xs = refs[:blocks]
    w_ref, acc_out, w_now, sem = refs[blocks:]
    feat = xs[0].shape[1]
    hidden = acc_out.shape[1]
    tiles = hidden // N_TILE

    def copy(k, n):
        cols = pl.ds(n * N_TILE, N_TILE)
        at = pl.multiple_of(ints[base + k] * feat, feat)
        return pltpu.make_async_copy(
            w_ref.at[pl.ds(at, feat), cols], w_now.at[n, pl.ds(k * feat, feat), :], sem.at[k, n]
        )

    for n in range(tiles):
        for k in range(blocks):
            copy(k, n).start()
    lhs = jnp.concatenate([x[...] for x in xs], axis=1)
    for n in range(tiles):
        for k in range(blocks):
            copy(k, n).wait()
        acc_out[:, pl.ds(n * N_TILE, N_TILE)] = jnp.dot(lhs, w_now[n], preferred_element_type=F32)


def lora_kernel(
    count, blocks, base, ints, *refs
):
    xs = refs[:blocks]
    (w_ref, acc_in, wide_ref, col_ref, tail_ref, up_ref, recv_ref, acc_out, w_now, up_now, sem, up_sem) = refs[blocks:]
    feat = xs[0].shape[1]
    hidden = acc_out.shape[1]
    tiles = hidden // N_TILE
    reqs, rank = recv_ref.shape[:2]

    def copy(k, n):
        cols = pl.ds(n * N_TILE, N_TILE)
        at = pl.multiple_of(ints[base + k] * feat, feat)
        return pltpu.make_async_copy(
            w_ref.at[pl.ds(at, feat), cols], w_now.at[n, pl.ds(k * feat, feat), :], sem.at[k, n]
        )

    for n in range(tiles):
        for k in range(blocks):
            copy(k, n).start()
    fetch_adapters(count, ints, up_ref, recv_ref, up_now, up_sem, False)
    lhs = jnp.concatenate([x[...] for x in xs], axis=1)
    scale = col_ref[:, 0:1]
    for n in range(tiles):
        cols = pl.ds(n * N_TILE, N_TILE)
        for k in range(blocks):
            copy(k, n).wait()
        part = acc_in[:, cols] + jnp.dot(lhs, w_now[n], preferred_element_type=F32)
        acc_out[:, cols] = part * scale
    fetch_adapters(count, ints, up_ref, recv_ref, up_now, up_sem, True)
    width = reqs * rank
    wide = wide_ref[...]
    for n in range(tiles):
        cols = pl.ds(n * N_TILE, N_TILE)
        both = jnp.concatenate([up_now[:, cols], tail_ref[:, cols]], axis=0)
        acc_out[:, cols] += jnp.dot(wide, both, preferred_element_type=F32)


def finish_kernel(ints, c_ref, d_ref, col_ref, w_ref, acc_ref, w2_ref, act_out, part_out):
    upper = pl.program_id(0) < pl.num_programs(0) // 2
    x = jnp.where(upper, c_ref[...].astype(F32), d_ref[...].astype(F32)).astype(BF)
    pre = acc_ref[...] + jnp.dot(x, w_ref[...], preferred_element_type=F32) * col_ref[:, 0:1]
    act = jax.nn.gelu(pre, approximate=True).astype(BF)
    act_out[...] = act
    part_out[...] = jnp.dot(act, w2_ref[...], preferred_element_type=F32).astype(BF)


def second_kernel(blocks, base, ints, act_ref, w_ref, *refs):
    outs = refs[:blocks]
    w_now, sem = refs[blocks:]
    feat = outs[0].shape[1]

    def copy(k):
        at = pl.multiple_of(ints[base - k] * feat, feat)
        return pltpu.make_async_copy(
            w_ref.at[:, pl.ds(at, feat)], w_now.at[:, pl.ds(k * feat, feat)], sem.at[k]
        )

    for k in range(blocks):
        copy(k).start()
    for k in range(blocks):
        copy(k).wait()
    got = jnp.dot(act_ref[...], w_now[...], preferred_element_type=F32)
    for k in range(blocks):
        outs[k][...] = got[:, k * feat : (k + 1) * feat]


def ring_device(
    count, tokens, modulation, adapter_per_request, tokens_per_request, first_weight,
    first_bias, second_weight, second_bias, adapter_down_matrices, adapter_up_matrices,
):
    me = lax.axis_index("tensor")
    store = lax.axis_index("store")
    rows, feat = tokens.shape
    hidden = first_weight.shape[1]
    stored, rank = adapter_up_matrices.shape[:2]
    reqs = tokens_per_request.shape[1]
    order = ring_order(count)
    forth = [(order[i], order[(i + 1) % count]) for i in range(count)]
    back = [(b, a) for a, b in forth]
    half = count // 2
    visits = [0] + [s for k in range(1, half) for s in (-k, k)] + [half]
    table = [[0] * count for _ in range(count)]
    for at, dev in enumerate(order):
        table[dev] = [order[(at + k) % count] for k in visits]
    mine = lax.dynamic_index_in_dim(jnp.array(table, jnp.int32), me, 0, keepdims=False)

    def go(x, route):
        return lax.ppermute(x, "tensor", route)

    def like(*shape, kind=BF):
        return jax.ShapeDtypeStruct(shape, kind)

    down = jnp.swapaxes(adapter_down_matrices, 1, 2)
    mod = jnp.swapaxes(modulation[0], 0, 1)

    my_ids = lax.dynamic_index_in_dim(adapter_per_request, store, 0, keepdims=False)
    their_ids = lax.dynamic_index_in_dim(adapter_per_request, 1 - store, 0, keepdims=False)
    ids = jnp.concatenate([my_ids, their_ids])
    ints = jnp.concatenate(
        [
            mine,
            jnp.clip(ids - store * stored, 0, stored - 1),
            (my_ids // stored == store).astype(jnp.int32),
        ]
    )

    own_mod = pl.BlockSpec((3, reqs, feat), lambda i, s, *_: (0, 0, s[0]))
    flat = lambda *shape: pl.BlockSpec(shape, lambda i, *_: (0,) * len(shape))
    u, hot, stat = pl.pallas_call(
        own_kernel,
        grid_spec=pltpu.PrefetchScalarGridSpec(
            num_scalar_prefetch=2,
            grid=(1,),
            in_specs=[flat(rows, feat), own_mod],
            out_specs=[flat(rows, feat), flat(rows, 128), flat(8, rows)],
        ),
        out_shape=[like(rows, feat), like(rows, 128), like(8, rows, kind=F32)],
        compiler_params=params(),
        cost_estimate=cost(20 * rows * feat, 6 * rows * feat),
        name="own_features",
    )(ints, tokens_per_request[0], tokens, mod)

    send_down, send_up = pl.pallas_call(
        functools.partial(send_kernel, count),
        in_specs=[SMEM, ANY, ANY],
        out_specs=[WHOLE, WHOLE],
        out_shape=[like(reqs, rank, feat), like(reqs, rank, hidden)],
        scratch_shapes=[pltpu.SemaphoreType.DMA((2 * reqs,))],
        compiler_params=params(),
        cost_estimate=cost(0, 4 * reqs * rank * (feat + hidden)),
        name="adapters_to_send",
    )(ints, down, adapter_up_matrices)
    swap = [(s, s ^ 1) for s in range(lax.axis_size("store"))]
    recv_down = lax.ppermute(send_down, "store", swap)
    recv_up = lax.ppermute(send_up, "store", swap)

    tail = pl.pallas_call(
        functools.partial(means_kernel, count),
        grid=(count,),
        in_specs=[
            pl.BlockSpec((3, reqs, feat), lambda i: (0, 0, i)),
            pl.BlockSpec((feat, hidden), lambda i: (i, 0)),
            pl.BlockSpec((1, hidden), lambda i: (0, 0)),
            ANY,
        ],
        out_specs=pl.BlockSpec((128, hidden), lambda i: (0, 0)),
        out_shape=like(128, hidden),
        scratch_shapes=[pltpu.VMEM((2, count * reqs, hidden), F32)],
        compiler_params=params(),
        cost_estimate=cost(64 * count * feat * hidden, 2 * count * feat * hidden),
        name="means_part",
    )(mod, first_weight, first_bias.reshape(1, hidden), send_down)

    low, pack = pl.pallas_call(
        functools.partial(low_kernel, count),
        grid_spec=pltpu.PrefetchScalarGridSpec(
            num_scalar_prefetch=1,
            grid=(1,),
            in_specs=[flat(rows, feat), flat(rows, 128), flat(8, rows), own_mod, ANY, ANY, ANY],
            out_specs=[flat(rank, rows), flat(count + 2 * reqs + 8, rows)],
            scratch_shapes=[
                pltpu.VMEM((reqs * rank, feat), BF),
                pltpu.SemaphoreType.DMA((reqs,)),
            ],
        ),
        out_shape=[like(rank, rows), like(count + 2 * reqs + 8, rows, kind=F32)],
        compiler_params=params(),
        cost_estimate=cost(2 * rows * feat * reqs * rank, 4 * rows * feat),
        name="low_rank_parts",
    )(ints, u, hot, stat, mod, down, recv_down, tail)
    gates = [low]
    span = 1
    while span < count:
        route = [(t, t ^ span) for t in range(count)]
        args = (low, pack, go(low, route), go(pack, route), hot)
        if 2 * span == count:
            kernel = functools.partial(last_merge_kernel, count, span, reqs, feat)
            shapes = [like(rows, reqs * rank + 128), like(rows, 128, kind=F32)]
        else:
            kernel = functools.partial(merge_kernel, count, span, reqs)
            shapes = [like(*low.shape), like(*pack.shape, kind=F32)]
        low, pack = pl.pallas_call(
            kernel,
            in_specs=[WHOLE] * 5,
            out_specs=[WHOLE] * 2,
            out_shape=shapes,
            compiler_params=params(),
            cost_estimate=cost(4e10, 8 * rank * rows),
            name="merge_sums",
        )(*args)
        gates.append(low)
        span *= 2
    wide, cols = low, pack

    cut = rows // 2
    a = b = u
    seen = [u]
    for k in range(1, half):
        a, b = go(a, forth), go(b, back)
        seen += [a, b]
        a, b, _ = lax.optimization_barrier((a, b, gates[k - 1]))
    far_c, far_d = go(a[:cut], forth), go(b[cut:], back)

    tiles = hidden // N_TILE
    early, late = seen[:-2], seen[-2:]
    w_scratch = lambda n: [
        pltpu.VMEM((tiles, n * feat, N_TILE), BF),
    ]
    acc = pl.pallas_call(
        functools.partial(first_kernel, count, len(early), 0),
        in_specs=[SMEM] + [WHOLE] * len(early) + [ANY],
        out_specs=WHOLE,
        out_shape=like(rows, hidden, kind=F32),
        scratch_shapes=w_scratch(len(early)) + [pltpu.SemaphoreType.DMA((len(early), tiles))],
        compiler_params=params(),
        cost_estimate=cost(2 * rows * feat * hidden * len(early), 2 * feat * hidden * len(early)),
        name="first_blocks",
    )(ints, *early, first_weight)
    acc = pl.pallas_call(
        functools.partial(lora_kernel, count, len(late), len(early)),
        in_specs=[SMEM] + [WHOLE] * len(late) + [ANY] + [WHOLE] * 4 + [ANY, ANY],
        out_specs=WHOLE,
        out_shape=like(rows, hidden, kind=F32),
        scratch_shapes=w_scratch(len(late))
        + [
            pltpu.VMEM((reqs * rank, hidden), BF),
            pltpu.SemaphoreType.DMA((len(late), tiles)),
            pltpu.SemaphoreType.DMA((reqs,)),
        ],
        compiler_params=params(),
        cost_estimate=cost(
            2 * rows * hidden * (feat * len(late) + reqs * rank), 2 * feat * hidden * len(late)
        ),
        name="low_rank_added",
    )(ints, *late, first_weight, acc, wide, cols, tail, adapter_up_matrices, recv_up)
    steps = 4
    tile = rows // steps
    last = count - 1
    tiled = lambda width: pl.BlockSpec((tile, width), lambda i, *s: (i, 0))
    act, far_part = pl.pallas_call(
        finish_kernel,
        grid_spec=pltpu.PrefetchScalarGridSpec(
            num_scalar_prefetch=1,
            grid=(steps,),
            in_specs=[
                pl.BlockSpec((tile, feat), lambda i, s: (jnp.minimum(i, steps // 2 - 1), 0)),
                pl.BlockSpec((tile, feat), lambda i, s: (jnp.maximum(i - steps // 2, 0), 0)),
                tiled(128),
                pl.BlockSpec((feat, hidden), lambda i, s: (s[last], 0)),
                tiled(hidden),
                pl.BlockSpec((hidden, feat), lambda i, s: (0, s[last])),
            ],
            out_specs=[tiled(hidden), tiled(feat)],
        ),
        out_shape=[like(rows, hidden), like(rows, feat)],
        compiler_params=params(),
        cost_estimate=cost(4 * rows * hidden * feat, 14 * rows * hidden, rows * hidden),
        name="finish_first",
    )(ints, far_c, far_d, cols, first_weight, acc, second_weight)

    def second(blocks, base, name):
        return pl.pallas_call(
            functools.partial(second_kernel, blocks, base),
            in_specs=[SMEM, WHOLE, ANY],
            out_specs=[WHOLE] * blocks,
            out_shape=[like(rows, feat, kind=F32)] * blocks,
            scratch_shapes=[
                pltpu.VMEM((hidden, blocks * feat), BF),
                pltpu.SemaphoreType.DMA((blocks,)),
            ],
            compiler_params=params(),
            cost_estimate=cost(2 * rows * hidden * feat * blocks, blocks * rows * feat * 8),
            name=name,
        )(ints, act, second_weight)

    parts = {}
    base = count - 2
    for k in range(half - 1, 0, -1):
        blocks = 3 if k == 1 else 2
        got = second(blocks, base, "second_blocks")
        base -= blocks
        parts[k], parts[-k] = got[0], got[1]
    parts[0] = got[2]
    gate = jnp.dot(
        hot[:, :reqs], lax.dynamic_slice_in_dim(mod[2], me * feat, feat, 1),
        preferred_element_type=F32,
    )
    rights, lefts = [], []
    chains = 2
    size = rows // chains
    for c in range(chains):
        lo = c * size
        mid = size // 2
        right = go(far_part[lo : lo + mid], forth)
        left = go(far_part[lo + mid : lo + size], back)
        for k in range(half - 1, 0, -1):
            r = parts[k][lo : lo + size]
            l = parts[-k][lo : lo + size]
            if k == half - 1:
                r = jnp.concatenate([r[:mid] + right.astype(F32), r[mid:]])
                l = jnp.concatenate([l[:mid], l[mid:] + left.astype(F32)])
            else:
                r = r + right.astype(F32)
                l = l + left.astype(F32)
            right = go(r.astype(BF), forth)
            left = go(l.astype(BF), back)
        rights.append(right)
        lefts.append(left)
    mixed = parts[0] + jnp.concatenate(rights).astype(F32) + jnp.concatenate(lefts).astype(F32)
    return (tokens.astype(F32) + gate * (mixed + second_bias.astype(F32))).astype(BF)


def partner(block, axis, stride):
    count = lax.axis_size(axis)
    route = []
    for low in range(count):
        high = low | 1 << stride
        if high != low and high < count:
            route += [(low, high), (high, low)]
    return lax.ppermute(block, axis, route)


def request_onehot(lengths, row_count, req_count):
    bounds = jnp.cumsum(lengths)
    places = jnp.arange(row_count, dtype=jnp.int32)
    owner_req = jnp.sum((places[:, None] >= bounds[None, :]).astype(jnp.int32), axis=1)
    return (owner_req[:, None] == jnp.arange(req_count, dtype=jnp.int32)[None, :]).astype(
        jnp.float32
    )


def plain_device(
    tokens,
    modulation,
    adapter_per_request,
    tokens_per_request,
    first_weight,
    first_bias,
    second_weight,
    second_bias,
    adapter_down_matrices,
    adapter_up_matrices,
):
    tensor_index = lax.axis_index("tensor")
    store_index = lax.axis_index("store")
    tok_rows, feat_width = tokens.shape
    req_count = tokens_per_request.shape[1]
    rank_column_width = adapter_down_matrices.shape[2]
    hidden_width = first_weight.shape[1]
    store_request_count = adapter_down_matrices.shape[0]
    gathered = lax.all_gather(tokens, "tensor", axis=1, tiled=True).astype(jnp.float32)
    adapter_indicator = request_onehot(tokens_per_request[0], tok_rows, req_count)
    factors = modulation[0].astype(jnp.float32)
    shift_rows = jnp.dot(adapter_indicator, factors[:, 0], precision=lax.Precision.HIGHEST)
    scale_rows = jnp.dot(adapter_indicator, factors[:, 1], precision=lax.Precision.HIGHEST)
    gate_own = lax.dynamic_slice_in_dim(factors[:, 2], tensor_index * feat_width, feat_width, 1)
    gate_rows = jnp.dot(adapter_indicator, gate_own, precision=lax.Precision.HIGHEST)
    center = jnp.mean(gathered, axis=1, keepdims=True)
    spread = jnp.mean((gathered - center) ** 2, axis=1, keepdims=True)
    normed = (gathered - center) * lax.rsqrt(spread + 1e-06)
    modded = ((1.0 + scale_rows) * normed + shift_rows).astype(jnp.bfloat16)

    def pick_owned(wanted):
        owned_mask = wanted // store_request_count == store_index
        request_index_list = jnp.clip(
            wanted - store_index * store_request_count, 0, store_request_count - 1
        )
        down_matrix_rows = jnp.take(adapter_down_matrices, request_index_list, axis=0)
        up_matrix_rows = jnp.take(adapter_up_matrices, request_index_list, axis=0)
        keep = owned_mask[:, None, None]
        return (
            owned_mask,
            jnp.where(keep, down_matrix_rows, jnp.zeros_like(down_matrix_rows)),
            jnp.where(keep, up_matrix_rows, jnp.zeros_like(up_matrix_rows)),
        )

    mine_ids = lax.dynamic_index_in_dim(adapter_per_request, store_index, 0, keepdims=False)
    other_ids = lax.dynamic_index_in_dim(adapter_per_request, 1 - store_index, 0, keepdims=False)
    mine_owned, mine_down, mine_up = pick_owned(mine_ids)
    other_owned, send_down, send_up = pick_owned(other_ids)
    recv_down, recv_up = partner((send_down, send_up), "store", 0)
    down_now = jnp.where(mine_owned[:, None, None], mine_down, recv_down)
    up_now = jnp.where(mine_owned[:, None, None], mine_up, recv_up)
    low_rank_every = jnp.einsum(
        "tn,knr->tkr",
        modded,
        lax.all_gather(down_now, "tensor", axis=1, tiled=True),
        preferred_element_type=jnp.float32,
    )
    low_rank_sum = jnp.sum(adapter_indicator[:, :, None] * low_rank_every, axis=1)
    adapter_low_rank = low_rank_sum.astype(jnp.bfloat16)
    broadcast_low_rank = (
        (adapter_indicator[:, :, None] * adapter_low_rank.astype(jnp.float32)[:, None, :])
        .reshape(tok_rows, req_count * rank_column_width)
        .astype(jnp.bfloat16)
    )
    preact = jnp.dot(modded, first_weight, preferred_element_type=jnp.float32) + first_bias.astype(
        jnp.float32
    )
    preact = preact + jnp.dot(
        broadcast_low_rank,
        up_now.reshape(req_count * rank_column_width, hidden_width),
        preferred_element_type=jnp.float32,
    )
    activated = jax.nn.gelu(preact, approximate=True).astype(jnp.bfloat16)
    own_share = lax.psum_scatter(
        lax.dot_general(
            second_weight, activated, (((0,), (1,)), ((), ())), preferred_element_type=jnp.float32
        ),
        "tensor",
        scatter_dimension=0,
        tiled=True,
    ).T
    block_out = tokens.astype(jnp.float32) + gate_rows * (
        own_share + second_bias.astype(jnp.float32)
    )
    return block_out.astype(jnp.bfloat16)


def on_device(count, tokens, *rest):
    if tokens.shape[1] % 128 == 0 and count % 4 == 0 and count & (count - 1) == 0:
        return ring_device(count, tokens, *rest)
    return plain_device(tokens, *rest)


def solution(mesh):
    in_specs = (
        P(("groups", "store"), "tensor"),
        P(("groups", "store"), None, None, None),
        P("groups", None),
        P(("groups", "store"), None),
        P(None, "tensor"),
        P("tensor"),
        P("tensor", None),
        P("tensor"),
        P("store", "tensor", None),
        P("store", None, "tensor"),
    )
    out_specs = P(("groups", "store"), "tensor")
    return jax.shard_map(
        functools.partial(on_device, mesh.shape["tensor"]), mesh=mesh, in_specs=in_specs, out_specs=out_specs, check_vma=False
    )
```

```python
import functools

import jax
import jax.numpy as jnp
from jax import lax
from jax.experimental import pallas as pl
from jax.experimental.pallas import tpu as pltpu
from jax.sharding import PartitionSpec as P

BF = jnp.bfloat16
F32 = jnp.float32
SEND_MIB = 60
HIGH = lax.Precision.HIGHEST
ANY = pl.BlockSpec(memory_space=pltpu.HBM)
SMEM = pl.BlockSpec(memory_space=pltpu.SMEM)
WHOLE = pl.BlockSpec(memory_space=pltpu.VMEM)


def params(mib=24):
    return pltpu.CompilerParams(vmem_limit_bytes=mib * 1024 * 1024)


def cost(flops, nbytes, trans=0, scale=1.0):
    flops, nbytes, trans = flops * scale, nbytes * scale, trans * scale
    return pl.CostEstimate(
        flops=int(flops), bytes_accessed=int(nbytes), transcendentals=int(trans)
    )


def ring_order(count):
    cols = 2 if count < 32 else 4
    rows = count // cols
    walk = [r * cols for r in range(rows)]
    for i, r in enumerate(reversed(range(rows))):
        across = list(range(1, cols))
        walk += [r * cols + c for c in (across if i % 2 == 0 else across[::-1])]
    return walk


def blocks_in(ref, width, at, axis):
    place = pl.ds(pl.multiple_of(at * width, width), width)
    return ref.at[place, :] if axis == 0 else ref.at[:, place]


def place(ids, whose, r, stored):
    return jnp.clip(ids[whose, r] - lax.axis_index("store") * stored, 0, stored - 1)


def send_kernel(ids, down_ref, up_ref, down_out, mine_out, up_out, sem):
    reqs = down_out.shape[0]
    stored = down_ref.shape[0]
    me = lax.axis_index("store")
    copies = []
    for r in range(reqs):
        at = place(ids, 1 - me, r, stored)
        own = place(ids, me, r, stored)
        copies.append(pltpu.make_async_copy(down_ref.at[at], down_out.at[r], sem.at[0, r]))
        copies.append(pltpu.make_async_copy(down_ref.at[own], mine_out.at[r], sem.at[1, r]))
        copies.append(pltpu.make_async_copy(up_ref.at[at], up_out.at[r], sem.at[2, r]))
    for c in copies:
        c.start()
    for c in copies:
        c.wait()


def fetch_adapters(count, ints, store_ref, recv_ref, dst, sem, wait):
    reqs, rank = recv_ref.shape[:2]
    for r in range(reqs):
        here = dst.at[pl.ds(r * rank, rank)]
        if wait:
            pltpu.make_async_copy(recv_ref.at[r], here, sem.at[r]).wait()
            continue
        own = ints[count + 2 * reqs + r]

        @pl.when(own == 1)
        def _():
            pltpu.make_async_copy(store_ref.at[ints[count + r]], here, sem.at[r]).start()

        @pl.when(own == 0)
        def _():
            pltpu.make_async_copy(recv_ref.at[r], here, sem.at[r]).start()


def own_kernel(lengths, x_ref, mod_ref, u_out, hot_out, stat_out):
    rows, feat = x_ref.shape
    reqs = mod_ref.shape[1]
    own = pl.ds(pl.multiple_of(lax.axis_index("tensor") * feat, feat), feat)
    x = x_ref[...].astype(F32)
    mean = jnp.mean(x, axis=1, keepdims=True)
    cent = x - mean
    m2 = jnp.sum(cent * cent, axis=1, keepdims=True)
    row = lax.broadcasted_iota(jnp.int32, (rows, 128), 0)
    lane = lax.broadcasted_iota(jnp.int32, (rows, 128), 1)
    first = jnp.zeros((1, 128), jnp.int32)
    after = jnp.zeros((1, 128), jnp.int32)
    lane1 = lax.broadcasted_iota(jnp.int32, (1, 128), 1)
    begin = jnp.int32(0)
    for r in range(reqs):
        end = begin + lengths[0, r]
        first = jnp.where(lane1 == r, begin, first)
        after = jnp.where(lane1 == r, end, after)
        begin = end
    hot = jnp.where((row >= first) & (row < after), 1.0, 0.0)
    hot_out[...] = hot.astype(BF)
    stat_out[...] = jnp.where(lane == 0, mean, jnp.where(lane == 1, m2, 0.0)).T[:8]
    scale_rows = jnp.dot(hot[:, :reqs].astype(BF), mod_ref[1, :, own], preferred_element_type=F32)
    u_out[...] = (cent * (1.0 + scale_rows)).astype(BF)


def low_kernel(
    count, stored, ids, u_ref, hot_ref, stat_ref, mod_ref, mine_ref, recv_ref, low_out, pack_out, down_now
):
    rows, feat = u_ref.shape
    reqs, rank = recv_ref.shape[:2]
    me = lax.axis_index("tensor")
    store = lax.axis_index("store")
    own = pl.ds(pl.multiple_of(me * feat, feat), feat)
    for r in range(reqs):
        here = pl.ds(r * rank, rank)

        @pl.when(ids[store, r] // stored == store)
        def _():
            down_now[here, :] = mine_ref[r]

        @pl.when(ids[store, r] // stored != store)
        def _():
            down_now[here, :] = recv_ref[r]

    hot_t = hot_ref[...].astype(F32).T
    every = lax.dot_general(
        down_now[...], u_ref[...], (((1,), (1,)), ((), ())), preferred_element_type=F32
    )
    total = jnp.zeros((rank, rows), F32)
    side = jnp.zeros((rank, 128), F32)
    lane = lax.broadcasted_iota(jnp.int32, (rank, 128), 1)
    for r in range(reqs):
        total = total + every[r * rank : (r + 1) * rank] * hot_t[r : r + 1]
        mat = down_now[pl.ds(r * rank, rank), :].astype(F32)
        by_scale = jnp.sum(mat * (1.0 + mod_ref[1, pl.ds(r, 1), own].astype(F32)), axis=1, keepdims=True)
        by_shift = jnp.sum(mat * mod_ref[0, pl.ds(r, 1), own].astype(F32), axis=1, keepdims=True)
        side = jnp.where(lane == r, by_scale, side)
        side = jnp.where(lane == reqs + r, by_shift, side)
    low_out[...] = total.astype(BF)
    stat = stat_ref[...]
    here = lax.broadcasted_iota(jnp.int32, (count, rows), 0) == me
    pack_out[pl.ds(0, count), :] = jnp.where(here, stat[0:1], 0.0)
    turned = jnp.concatenate([side, jnp.zeros((128 - rank, 128), F32)], axis=0).T
    flat = jnp.concatenate([turned[: 2 * reqs], jnp.zeros((2 * reqs, rows - 128), F32)], axis=1)
    pack_out[pl.ds(count, 2 * reqs), :] = flat
    pack_out[pl.ds(count + 2 * reqs, 8), :] = jnp.broadcast_to(stat[1:2], (8, rows))


def merge(count, span, reqs, low_a, pack_a, low_b, pack_b, hot_ref):
    hot_t = hot_ref[...].astype(F32).T[:reqs]
    pa, pb = pack_a[...], pack_b[...]
    rank = low_a.shape[0]
    gap = (jnp.sum(pa[:count], axis=0, keepdims=True) - jnp.sum(pb[:count], axis=0, keepdims=True)) / span
    diff = (pa - pb)[count : count + reqs, :rank]
    back = lax.dot_general(
        diff, hot_t, (((0,), (0,)), ((), ())), precision=HIGH, preferred_element_type=F32
    )
    low = low_a[...].astype(F32) + low_b[...].astype(F32) + (0.5 * gap) * back
    return low, pa + pb, hot_t


def merge_kernel(count, span, reqs, *refs):
    low, pack, _ = merge(count, span, reqs, *refs[:5])
    refs[5][...] = low.astype(BF)
    refs[6][...] = pack


def last_merge_kernel(count, span, reqs, feat, *refs):
    wide_out, col_out = refs[5:]
    low, pack, hot_t = merge(count, span, reqs, *refs[:5])
    rank, rows = low.shape
    means = pack[:count]
    mean = jnp.sum(means, axis=0, keepdims=True) / count
    dev = means - mean
    m2 = pack[count + 2 * reqs : count + 2 * reqs + 1] + feat * jnp.sum(dev * dev, axis=0, keepdims=True)
    rstd = lax.rsqrt(m2 / (count * feat) + 1e-06)
    shifted = lax.dot_general(
        pack[count + reqs : count + 2 * reqs, :rank], hot_t, (((0,), (0,)), ((), ())),
        precision=HIGH, preferred_element_type=F32,
    )
    low = (low * rstd + shifted).astype(BF).astype(F32)
    pad = 128 - rank - count - 1
    turned = jnp.concatenate([low, dev * rstd, rstd, jnp.zeros((pad, rows), F32)], axis=0).T
    col_out[...] = jnp.broadcast_to(turned[:, rank + count : rank + count + 1], (rows, 128))
    turned = turned.astype(BF)
    hot8 = refs[4][...][:, :reqs]

    def spread(src_count, width, rule):
        src = lax.broadcasted_iota(jnp.int32, (src_count, width), 0)
        dst = lax.broadcasted_iota(jnp.int32, (src_count, width), 1)
        return jnp.where(rule(src, dst), 1.0, 0.0).astype(BF)

    def times(a, b):
        return jnp.dot(a, b, preferred_element_type=F32)

    width = reqs * rank
    lora = times(turned, spread(128, width, lambda s, d: (d % rank == s) & (s < rank)))
    lora = lora * times(hot8, spread(reqs, width, lambda s, d: d // rank == s))
    pairs = count * reqs
    coef = times(turned, spread(128, 128, lambda s, d: (s == rank + d // reqs) & (d < pairs)))
    coef = coef * times(hot8, spread(reqs, 128, lambda s, d: (d % reqs == s) & (d < pairs)))
    coef = coef + times(
        hot8, spread(reqs, 128, lambda s, d: (d % reqs == s) & (d >= pairs) & (d < pairs + 2 * reqs))
    )
    wide_out[:, pl.ds(0, width)] = lora.astype(BF)
    wide_out[:, pl.ds(width, 128)] = coef.astype(BF)


def means_kernel(count, mod_ref, w_ref, bias_ref, after_ref, out_ref, total):
    step = pl.program_id(0)
    reqs = mod_ref.shape[1]
    feat = mod_ref.shape[2]
    lhs = jnp.concatenate([jnp.ones((reqs, feat), F32), mod_ref[1].astype(F32), mod_ref[0].astype(F32)], axis=0)
    lhs = jnp.concatenate([lhs, jnp.zeros((8, feat), F32)], axis=0).astype(BF)
    got = jnp.dot(lhs, w_ref[...], preferred_element_type=F32)
    total[0, pl.ds(pl.multiple_of(step * reqs, reqs), reqs), :] = got[:reqs] + got[reqs : 2 * reqs]

    @pl.when(step == 0)
    def _():
        total[1, pl.ds(0, reqs), :] = got[2 * reqs : 3 * reqs] + bias_ref[...].astype(F32)

    @pl.when(step > 0)
    def _():
        total[1, pl.ds(0, reqs), :] += got[2 * reqs : 3 * reqs]

    @pl.when(step == count - 1)
    def _():
        shift = total[1, pl.ds(0, reqs), :]
        high = shift.astype(BF).astype(F32)
        both = jnp.concatenate([high, shift - high], axis=0)
        left = 128 - count * reqs - 2 * reqs
        rows = [total[0, pl.ds(0, count * reqs), :], both]
        if left:
            rows.append(jnp.zeros((left, both.shape[1]), F32))
        out_ref[...] = jnp.concatenate(rows, axis=0).astype(BF)


N_TILE = 512


def first_kernel(count, blocks, base, ints, *refs):
    xs = refs[:blocks]
    w_ref, acc_out, w_now, sem = refs[blocks:]
    feat = xs[0].shape[1]
    hidden = acc_out.shape[1]
    tiles = hidden // N_TILE

    def copy(k, n):
        cols = pl.ds(n * N_TILE, N_TILE)
        at = pl.multiple_of(ints[base + k] * feat, feat)
        return pltpu.make_async_copy(
            w_ref.at[pl.ds(at, feat), cols], w_now.at[n, pl.ds(k * feat, feat), :], sem.at[k, n]
        )

    for n in range(tiles):
        for k in range(blocks):
            copy(k, n).start()
    lhs = jnp.concatenate([x[...] for x in xs], axis=1)
    for n in range(tiles):
        for k in range(blocks):
            copy(k, n).wait()
        acc_out[:, pl.ds(n * N_TILE, N_TILE)] = jnp.dot(lhs, w_now[n], preferred_element_type=F32)


def lora_kernel(
    count, blocks, base, ints, *refs
):
    xs = refs[:blocks]
    (w_ref, acc_in, wide_ref, col_ref, tail_ref, up_ref, recv_ref, acc_out, w_now, up_now, sem, up_sem) = refs[blocks:]
    feat = xs[0].shape[1]
    hidden = acc_out.shape[1]
    tiles = hidden // N_TILE
    reqs, rank = recv_ref.shape[:2]

    def copy(k, n):
        cols = pl.ds(n * N_TILE, N_TILE)
        at = pl.multiple_of(ints[base + k] * feat, feat)
        return pltpu.make_async_copy(
            w_ref.at[pl.ds(at, feat), cols], w_now.at[n, pl.ds(k * feat, feat), :], sem.at[k, n]
        )

    for n in range(tiles):
        for k in range(blocks):
            copy(k, n).start()
    fetch_adapters(count, ints, up_ref, recv_ref, up_now, up_sem, False)
    lhs = jnp.concatenate([x[...] for x in xs], axis=1)
    scale = col_ref[:, 0:1]
    for n in range(tiles):
        cols = pl.ds(n * N_TILE, N_TILE)
        for k in range(blocks):
            copy(k, n).wait()
        part = acc_in[:, cols] + jnp.dot(lhs, w_now[n], preferred_element_type=F32)
        acc_out[:, cols] = part * scale
    fetch_adapters(count, ints, up_ref, recv_ref, up_now, up_sem, True)
    width = reqs * rank
    wide = wide_ref[...]
    for n in range(tiles):
        cols = pl.ds(n * N_TILE, N_TILE)
        both = jnp.concatenate([up_now[:, cols], tail_ref[:, cols]], axis=0)
        acc_out[:, cols] += jnp.dot(wide, both, preferred_element_type=F32)


def finish_kernel(ints, c_ref, d_ref, col_ref, w_ref, acc_ref, w2_ref, act_out, part_out):
    upper = pl.program_id(0) < pl.num_programs(0) // 2
    x = jnp.where(upper, c_ref[...].astype(F32), d_ref[...].astype(F32)).astype(BF)
    pre = acc_ref[...] + jnp.dot(x, w_ref[...], preferred_element_type=F32) * col_ref[:, 0:1]
    act = jax.nn.gelu(pre, approximate=True).astype(BF)
    act_out[...] = act
    part_out[...] = jnp.dot(act, w2_ref[...], preferred_element_type=F32).astype(BF)


def second_kernel(blocks, base, ints, act_ref, w_ref, *refs):
    outs = refs[:blocks]
    w_now, sem = refs[blocks:]
    feat = outs[0].shape[1]

    def copy(k):
        at = pl.multiple_of(ints[base - k] * feat, feat)
        return pltpu.make_async_copy(
            w_ref.at[:, pl.ds(at, feat)], w_now.at[:, pl.ds(k * feat, feat)], sem.at[k]
        )

    for k in range(blocks):
        copy(k).start()
    for k in range(blocks):
        copy(k).wait()
    got = jnp.dot(act_ref[...], w_now[...], preferred_element_type=F32)
    for k in range(blocks):
        outs[k][...] = got[:, k * feat : (k + 1) * feat]


def ring_device(
    count, tokens, modulation, adapter_per_request, tokens_per_request, first_weight,
    first_bias, second_weight, second_bias, adapter_down_matrices, adapter_up_matrices,
):
    me = lax.axis_index("tensor")
    store = lax.axis_index("store")
    rows, feat = tokens.shape
    hidden = first_weight.shape[1]
    stored, rank = adapter_up_matrices.shape[:2]
    reqs = tokens_per_request.shape[1]
    order = ring_order(count)
    forth = [(order[i], order[(i + 1) % count]) for i in range(count)]
    back = [(b, a) for a, b in forth]
    half = count // 2
    visits = [0] + [s for k in range(1, half) for s in (-k, k)] + [half]
    table = [[0] * count for _ in range(count)]
    for at, dev in enumerate(order):
        table[dev] = [order[(at + k) % count] for k in visits]
    mine = lax.dynamic_index_in_dim(jnp.array(table, jnp.int32), me, 0, keepdims=False)

    def go(x, route):
        return lax.ppermute(x, "tensor", route)

    def like(*shape, kind=BF):
        return jax.ShapeDtypeStruct(shape, kind)

    down = jnp.swapaxes(adapter_down_matrices, 1, 2)
    mod = jnp.swapaxes(modulation[0], 0, 1)

    my_ids = lax.dynamic_index_in_dim(adapter_per_request, store, 0, keepdims=False)
    their_ids = lax.dynamic_index_in_dim(adapter_per_request, 1 - store, 0, keepdims=False)
    ids = jnp.concatenate([my_ids, their_ids])
    ints = jnp.concatenate(
        [
            mine,
            jnp.clip(ids - store * stored, 0, stored - 1),
            (my_ids // stored == store).astype(jnp.int32),
        ]
    )

    u, hot, stat = pl.pallas_call(
        own_kernel,
        in_specs=[SMEM, WHOLE, WHOLE],
        out_specs=[WHOLE] * 3,
        out_shape=[like(rows, feat), like(rows, 128), like(8, rows, kind=F32)],
        compiler_params=params(),
        cost_estimate=cost(2 * rows * feat, rows * feat),
        name="own_features",
    )(tokens_per_request, tokens, mod)

    send_down, mine_down, send_up = pl.pallas_call(
        send_kernel,
        in_specs=[SMEM, ANY, ANY],
        out_specs=[WHOLE] * 3,
        out_shape=[like(reqs, rank, feat)] * 2 + [like(reqs, rank, hidden)],
        scratch_shapes=[pltpu.SemaphoreType.DMA((3, reqs))],
        compiler_params=params(SEND_MIB),
        cost_estimate=cost(0, reqs * rank * (feat + hidden)),
        name="adapters_to_send",
    )(adapter_per_request, down, adapter_up_matrices)
    swap = [(s, s ^ 1) for s in range(lax.axis_size("store"))]
    recv_down = lax.ppermute(send_down, "store", swap)

    low, pack = pl.pallas_call(
        functools.partial(low_kernel, count, stored),
        in_specs=[SMEM] + [WHOLE] * 6,
        out_specs=[WHOLE] * 2,
        out_shape=[like(rank, rows), like(count + 2 * reqs + 8, rows, kind=F32)],
        scratch_shapes=[pltpu.VMEM((reqs * rank, feat), BF)],
        compiler_params=params(),
        cost_estimate=cost(rows * feat * reqs, rows * feat),
        name="low_rank_parts",
    )(adapter_per_request, u, hot, stat, mod, mine_down, recv_down)
    recv_up = lax.ppermute(send_up, "store", swap)
    tail = pl.pallas_call(
        functools.partial(means_kernel, count),
        grid=(count,),
        in_specs=[
            pl.BlockSpec((3, reqs, feat), lambda i: (0, 0, i)),
            pl.BlockSpec((feat, hidden), lambda i: (i, 0)),
            pl.BlockSpec((1, hidden), lambda i: (0, 0)),
            ANY,
        ],
        out_specs=pl.BlockSpec((128, hidden), lambda i: (0, 0)),
        out_shape=like(128, hidden),
        scratch_shapes=[pltpu.VMEM((2, count * reqs, hidden), F32)],
        compiler_params=params(),
        cost_estimate=cost(64 * count * feat * hidden, 2 * count * feat * hidden, scale=0.1),
        name="means_part",
    )(mod, first_weight, first_bias.reshape(1, hidden), low)

    cut = rows // 2
    a = b = u
    seen = [u]
    for k in range(1, half):
        a, b = go(a, forth), go(b, back)
        seen += [a, b]
    far_c, far_d = go(a[:cut], forth), go(b[cut:], back)

    turn = 0
    span = 1
    while span < count:
        route = [(t, t ^ span) for t in range(count)]
        low_b, pack_b = go(low, route), go(pack, route)
        turn += 1
        if turn in (1, 2):
            low_b, pack_b, *_ = lax.optimization_barrier((low_b, pack_b, seen[2 * turn - 1], seen[2 * turn]))
        args = (low, pack, low_b, pack_b, hot)
        if 2 * span == count:
            kernel = functools.partial(last_merge_kernel, count, span, reqs, feat)
            shapes = [like(rows, reqs * rank + 128), like(rows, 128, kind=F32)]
        else:
            kernel = functools.partial(merge_kernel, count, span, reqs)
            shapes = [like(*low.shape), like(*pack.shape, kind=F32)]
        low, pack = pl.pallas_call(
            kernel,
            in_specs=[WHOLE] * 5,
            out_specs=[WHOLE] * 2,
            out_shape=shapes,
            compiler_params=params(),
            cost_estimate=cost(1e+09, 8 * rank * rows),
            name="merge_sums",
        )(*args)
        span *= 2
    wide, cols = low, pack


    tiles = hidden // N_TILE
    early, late = seen[:-2], seen[-2:]
    w_scratch = lambda n: [
        pltpu.VMEM((tiles, n * feat, N_TILE), BF),
    ]
    acc = pl.pallas_call(
        functools.partial(first_kernel, count, len(early), 0),
        in_specs=[SMEM] + [WHOLE] * len(early) + [ANY],
        out_specs=WHOLE,
        out_shape=like(rows, hidden, kind=F32),
        scratch_shapes=w_scratch(len(early)) + [pltpu.SemaphoreType.DMA((len(early), tiles))],
        compiler_params=params(24),
        cost_estimate=cost(2 * rows * feat * hidden * len(early), 2 * feat * hidden * len(early), scale=1),
        name="first_blocks",
    )(ints, *early, first_weight)
    acc = pl.pallas_call(
        functools.partial(lora_kernel, count, len(late), len(early)),
        in_specs=[SMEM] + [WHOLE] * len(late) + [ANY] + [WHOLE] * 4 + [ANY, ANY],
        out_specs=WHOLE,
        out_shape=like(rows, hidden, kind=F32),
        scratch_shapes=w_scratch(len(late))
        + [
            pltpu.VMEM((reqs * rank, hidden), BF),
            pltpu.SemaphoreType.DMA((len(late), tiles)),
            pltpu.SemaphoreType.DMA((reqs,)),
        ],
        compiler_params=params(24),
        cost_estimate=cost(
            2 * rows * hidden * (feat * len(late) + reqs * rank), 2 * feat * hidden * len(late), scale=1),
        name="low_rank_added",
    )(ints, *late, first_weight, acc, wide, cols, tail, adapter_up_matrices, recv_up)
    steps = 4
    tile = rows // steps
    last = count - 1
    tiled = lambda width: pl.BlockSpec((tile, width), lambda i, *s: (i, 0))
    act, far_part = pl.pallas_call(
        finish_kernel,
        grid_spec=pltpu.PrefetchScalarGridSpec(
            num_scalar_prefetch=1,
            grid=(steps,),
            in_specs=[
                pl.BlockSpec((tile, feat), lambda i, s: (jnp.minimum(i, steps // 2 - 1), 0)),
                pl.BlockSpec((tile, feat), lambda i, s: (jnp.maximum(i - steps // 2, 0), 0)),
                tiled(128),
                pl.BlockSpec((feat, hidden), lambda i, s: (s[last], 0)),
                tiled(hidden),
                pl.BlockSpec((hidden, feat), lambda i, s: (0, s[last])),
            ],
            out_specs=[tiled(hidden), tiled(feat)],
        ),
        out_shape=[like(rows, hidden), like(rows, feat)],
        compiler_params=params(16),
        cost_estimate=cost(4 * rows * hidden * feat, 14 * rows * hidden, rows * hidden, scale=1),
        name="finish_first",
    )(ints, far_c, far_d, cols, first_weight, acc, second_weight)

    def second(blocks, base, name):
        return pl.pallas_call(
            functools.partial(second_kernel, blocks, base),
            in_specs=[SMEM, WHOLE, ANY],
            out_specs=[WHOLE] * blocks,
            out_shape=[like(rows, feat, kind=F32)] * blocks,
            scratch_shapes=[
                pltpu.VMEM((hidden, blocks * feat), BF),
                pltpu.SemaphoreType.DMA((blocks,)),
            ],
            compiler_params=params(16),
            cost_estimate=cost(2 * rows * hidden * feat * blocks, blocks * rows * feat * 8),
            name=name,
        )(ints, act, second_weight)

    parts = {}
    base = count - 2
    for k in range(half - 1, 0, -1):
        blocks = 3 if k == 1 else 2
        got = second(blocks, base, "second_blocks")
        base -= blocks
        parts[k], parts[-k] = got[0], got[1]
    parts[0] = got[2]
    gate = jnp.dot(
        hot[:, :reqs], lax.dynamic_slice_in_dim(mod[2], me * feat, feat, 1),
        preferred_element_type=F32,
    )
    rights, lefts = [], []
    chains = 1
    size = rows // chains
    for c in range(chains):
        lo = c * size
        mid = size // 2
        right = go(far_part[lo : lo + mid], forth)
        left = go(far_part[lo + mid : lo + size], back)
        for k in range(half - 1, 0, -1):
            r = parts[k][lo : lo + size]
            l = parts[-k][lo : lo + size]
            if k == half - 1:
                r = jnp.concatenate([r[:mid] + right.astype(F32), r[mid:]])
                l = jnp.concatenate([l[:mid], l[mid:] + left.astype(F32)])
            else:
                r = r + right.astype(F32)
                l = l + left.astype(F32)
            right = go(r.astype(BF), forth)
            left = go(l.astype(BF), back)
        rights.append(right)
        lefts.append(left)
    mixed = parts[0] + jnp.concatenate(rights).astype(F32) + jnp.concatenate(lefts).astype(F32)
    return (tokens.astype(F32) + gate * (mixed + second_bias.astype(F32))).astype(BF)


def partner(block, axis, stride):
    count = lax.axis_size(axis)
    route = []
    for low in range(count):
        high = low | 1 << stride
        if high != low and high < count:
            route += [(low, high), (high, low)]
    return lax.ppermute(block, axis, route)


def request_onehot(lengths, row_count, req_count):
    bounds = jnp.cumsum(lengths)
    places = jnp.arange(row_count, dtype=jnp.int32)
    owner_req = jnp.sum((places[:, None] >= bounds[None, :]).astype(jnp.int32), axis=1)
    return (owner_req[:, None] == jnp.arange(req_count, dtype=jnp.int32)[None, :]).astype(
        jnp.float32
    )


def plain_device(
    tokens,
    modulation,
    adapter_per_request,
    tokens_per_request,
    first_weight,
    first_bias,
    second_weight,
    second_bias,
    adapter_down_matrices,
    adapter_up_matrices,
):
    tensor_index = lax.axis_index("tensor")
    store_index = lax.axis_index("store")
    tok_rows, feat_width = tokens.shape
    req_count = tokens_per_request.shape[1]
    rank_column_width = adapter_down_matrices.shape[2]
    hidden_width = first_weight.shape[1]
    store_request_count = adapter_down_matrices.shape[0]
    gathered = lax.all_gather(tokens, "tensor", axis=1, tiled=True).astype(jnp.float32)
    adapter_indicator = request_onehot(tokens_per_request[0], tok_rows, req_count)
    factors = modulation[0].astype(jnp.float32)
    shift_rows = jnp.dot(adapter_indicator, factors[:, 0], precision=lax.Precision.HIGHEST)
    scale_rows = jnp.dot(adapter_indicator, factors[:, 1], precision=lax.Precision.HIGHEST)
    gate_own = lax.dynamic_slice_in_dim(factors[:, 2], tensor_index * feat_width, feat_width, 1)
    gate_rows = jnp.dot(adapter_indicator, gate_own, precision=lax.Precision.HIGHEST)
    center = jnp.mean(gathered, axis=1, keepdims=True)
    spread = jnp.mean((gathered - center) ** 2, axis=1, keepdims=True)
    normed = (gathered - center) * lax.rsqrt(spread + 1e-06)
    modded = ((1.0 + scale_rows) * normed + shift_rows).astype(jnp.bfloat16)

    def pick_owned(wanted):
        owned_mask = wanted // store_request_count == store_index
        request_index_list = jnp.clip(
            wanted - store_index * store_request_count, 0, store_request_count - 1
        )
        down_matrix_rows = jnp.take(adapter_down_matrices, request_index_list, axis=0)
        up_matrix_rows = jnp.take(adapter_up_matrices, request_index_list, axis=0)
        keep = owned_mask[:, None, None]
        return (
            owned_mask,
            jnp.where(keep, down_matrix_rows, jnp.zeros_like(down_matrix_rows)),
            jnp.where(keep, up_matrix_rows, jnp.zeros_like(up_matrix_rows)),
        )

    mine_ids = lax.dynamic_index_in_dim(adapter_per_request, store_index, 0, keepdims=False)
    other_ids = lax.dynamic_index_in_dim(adapter_per_request, 1 - store_index, 0, keepdims=False)
    mine_owned, mine_down, mine_up = pick_owned(mine_ids)
    other_owned, send_down, send_up = pick_owned(other_ids)
    recv_down, recv_up = partner((send_down, send_up), "store", 0)
    down_now = jnp.where(mine_owned[:, None, None], mine_down, recv_down)
    up_now = jnp.where(mine_owned[:, None, None], mine_up, recv_up)
    low_rank_every = jnp.einsum(
        "tn,knr->tkr",
        modded,
        lax.all_gather(down_now, "tensor", axis=1, tiled=True),
        preferred_element_type=jnp.float32,
    )
    low_rank_sum = jnp.sum(adapter_indicator[:, :, None] * low_rank_every, axis=1)
    adapter_low_rank = low_rank_sum.astype(jnp.bfloat16)
    broadcast_low_rank = (
        (adapter_indicator[:, :, None] * adapter_low_rank.astype(jnp.float32)[:, None, :])
        .reshape(tok_rows, req_count * rank_column_width)
        .astype(jnp.bfloat16)
    )
    preact = jnp.dot(modded, first_weight, preferred_element_type=jnp.float32) + first_bias.astype(
        jnp.float32
    )
    preact = preact + jnp.dot(
        broadcast_low_rank,
        up_now.reshape(req_count * rank_column_width, hidden_width),
        preferred_element_type=jnp.float32,
    )
    activated = jax.nn.gelu(preact, approximate=True).astype(jnp.bfloat16)
    own_share = lax.psum_scatter(
        lax.dot_general(
            second_weight, activated, (((0,), (1,)), ((), ())), preferred_element_type=jnp.float32
        ),
        "tensor",
        scatter_dimension=0,
        tiled=True,
    ).T
    block_out = tokens.astype(jnp.float32) + gate_rows * (
        own_share + second_bias.astype(jnp.float32)
    )
    return block_out.astype(jnp.bfloat16)


def on_device(count, tokens, *rest):
    if tokens.shape[1] % 128 == 0 and count % 4 == 0 and count & (count - 1) == 0:
        return ring_device(count, tokens, *rest)
    return plain_device(tokens, *rest)


def solution(mesh):
    in_specs = (
        P(("groups", "store"), "tensor"),
        P(("groups", "store"), None, None, None),
        P("groups", None),
        P(("groups", "store"), None),
        P(None, "tensor"),
        P("tensor"),
        P("tensor", None),
        P("tensor"),
        P("store", "tensor", None),
        P("store", None, "tensor"),
    )
    out_specs = P(("groups", "store"), "tensor")
    return jax.shard_map(
        functools.partial(on_device, mesh.shape["tensor"]), mesh=mesh, in_specs=in_specs, out_specs=out_specs, check_vma=False
    )
```

```python
import functools

import jax
import jax.numpy as jnp
from jax import lax
from jax.experimental import pallas as pl
from jax.experimental.pallas import tpu as pltpu
from jax.sharding import PartitionSpec as P

BF = jnp.bfloat16
F32 = jnp.float32
SEND_MIB = 60
HIGH = lax.Precision.HIGHEST
ANY = pl.BlockSpec(memory_space=pltpu.HBM)
SMEM = pl.BlockSpec(memory_space=pltpu.SMEM)
WHOLE = pl.BlockSpec(memory_space=pltpu.VMEM)


def params(mib=24):
    return pltpu.CompilerParams(vmem_limit_bytes=mib * 1024 * 1024)


def cost(flops, nbytes, trans=0, scale=1.0):
    flops, nbytes, trans = flops * scale, nbytes * scale, trans * scale
    return pl.CostEstimate(
        flops=int(flops), bytes_accessed=int(nbytes), transcendentals=int(trans)
    )


def ring_order(count):
    cols = 2 if count < 32 else 4
    rows = count // cols
    walk = [r * cols for r in range(rows)]
    for i, r in enumerate(reversed(range(rows))):
        across = list(range(1, cols))
        walk += [r * cols + c for c in (across if i % 2 == 0 else across[::-1])]
    return walk


def blocks_in(ref, width, at, axis):
    place = pl.ds(pl.multiple_of(at * width, width), width)
    return ref.at[place, :] if axis == 0 else ref.at[:, place]


def place(ids, whose, r, stored):
    return jnp.clip(ids[whose, r] - lax.axis_index("store") * stored, 0, stored - 1)


def send_kernel(ids, down_ref, up_ref, down_out, mine_out, up_out, sem):
    reqs = down_out.shape[0]
    stored = down_ref.shape[0]
    me = lax.axis_index("store")
    copies = []
    for r in range(reqs):
        at = place(ids, 1 - me, r, stored)
        own = place(ids, me, r, stored)
        copies.append(pltpu.make_async_copy(down_ref.at[at], down_out.at[r], sem.at[0, r]))
        copies.append(pltpu.make_async_copy(down_ref.at[own], mine_out.at[r], sem.at[1, r]))
        copies.append(pltpu.make_async_copy(up_ref.at[at], up_out.at[r], sem.at[2, r]))
    for c in copies:
        c.start()
    for c in copies:
        c.wait()


def fetch_adapters(count, ints, store_ref, recv_ref, dst, sem, wait):
    reqs, rank = recv_ref.shape[:2]
    for r in range(reqs):
        here = dst.at[pl.ds(r * rank, rank)]
        if wait:
            pltpu.make_async_copy(recv_ref.at[r], here, sem.at[r]).wait()
            continue
        own = ints[count + 2 * reqs + r]

        @pl.when(own == 1)
        def _():
            pltpu.make_async_copy(store_ref.at[ints[count + r]], here, sem.at[r]).start()

        @pl.when(own == 0)
        def _():
            pltpu.make_async_copy(recv_ref.at[r], here, sem.at[r]).start()


def own_kernel(lengths, x_ref, mod_ref, u_out, hot_out, stat_out):
    rows, feat = x_ref.shape
    reqs = mod_ref.shape[1]
    own = pl.ds(pl.multiple_of(lax.axis_index("tensor") * feat, feat), feat)
    x = x_ref[...].astype(F32)
    mean = jnp.mean(x, axis=1, keepdims=True)
    cent = x - mean
    m2 = jnp.sum(cent * cent, axis=1, keepdims=True)
    row = lax.broadcasted_iota(jnp.int32, (rows, 128), 0)
    lane = lax.broadcasted_iota(jnp.int32, (rows, 128), 1)
    first = jnp.zeros((1, 128), jnp.int32)
    after = jnp.zeros((1, 128), jnp.int32)
    lane1 = lax.broadcasted_iota(jnp.int32, (1, 128), 1)
    begin = jnp.int32(0)
    for r in range(reqs):
        end = begin + lengths[0, r]
        first = jnp.where(lane1 == r, begin, first)
        after = jnp.where(lane1 == r, end, after)
        begin = end
    hot = jnp.where((row >= first) & (row < after), 1.0, 0.0)
    hot_out[...] = hot.astype(BF)
    stat_out[...] = jnp.where(lane == 0, mean, jnp.where(lane == 1, m2, 0.0)).T[:8]
    scale_rows = jnp.dot(hot[:, :reqs].astype(BF), mod_ref[1, :, own], preferred_element_type=F32)
    u_out[...] = (cent * (1.0 + scale_rows)).astype(BF)


def low_kernel(
    count, stored, ids, u_ref, hot_ref, stat_ref, mod_ref, mine_ref, recv_ref, low_out, pack_out, down_now
):
    rows, feat = u_ref.shape
    reqs, rank = recv_ref.shape[:2]
    me = lax.axis_index("tensor")
    store = lax.axis_index("store")
    own = pl.ds(pl.multiple_of(me * feat, feat), feat)
    for r in range(reqs):
        here = pl.ds(r * rank, rank)

        @pl.when(ids[store, r] // stored == store)
        def _():
            down_now[here, :] = mine_ref[r]

        @pl.when(ids[store, r] // stored != store)
        def _():
            down_now[here, :] = recv_ref[r]

    hot_t = hot_ref[...].astype(F32).T
    every = lax.dot_general(
        down_now[...], u_ref[...], (((1,), (1,)), ((), ())), preferred_element_type=F32
    )
    total = jnp.zeros((rank, rows), F32)
    side = jnp.zeros((rank, 128), F32)
    lane = lax.broadcasted_iota(jnp.int32, (rank, 128), 1)
    for r in range(reqs):
        total = total + every[r * rank : (r + 1) * rank] * hot_t[r : r + 1]
        mat = down_now[pl.ds(r * rank, rank), :].astype(F32)
        by_scale = jnp.sum(mat * (1.0 + mod_ref[1, pl.ds(r, 1), own].astype(F32)), axis=1, keepdims=True)
        by_shift = jnp.sum(mat * mod_ref[0, pl.ds(r, 1), own].astype(F32), axis=1, keepdims=True)
        side = jnp.where(lane == r, by_scale, side)
        side = jnp.where(lane == reqs + r, by_shift, side)
    low_out[...] = total.astype(BF)
    stat = stat_ref[...]
    here = lax.broadcasted_iota(jnp.int32, (count, rows), 0) == me
    pack_out[pl.ds(0, count), :] = jnp.where(here, stat[0:1], 0.0)
    turned = jnp.concatenate([side, jnp.zeros((128 - rank, 128), F32)], axis=0).T
    flat = jnp.concatenate([turned[: 2 * reqs], jnp.zeros((2 * reqs, rows - 128), F32)], axis=1)
    pack_out[pl.ds(count, 2 * reqs), :] = flat
    pack_out[pl.ds(count + 2 * reqs, 8), :] = jnp.broadcast_to(stat[1:2], (8, rows))


def merge(count, span, reqs, low_a, pack_a, low_b, pack_b, hot_ref):
    hot_t = hot_ref[...].astype(F32).T[:reqs]
    pa, pb = pack_a[...], pack_b[...]
    rank = low_a.shape[0]
    gap = (jnp.sum(pa[:count], axis=0, keepdims=True) - jnp.sum(pb[:count], axis=0, keepdims=True)) / span
    diff = (pa - pb)[count : count + reqs, :rank]
    back = lax.dot_general(
        diff, hot_t, (((0,), (0,)), ((), ())), precision=HIGH, preferred_element_type=F32
    )
    low = low_a[...].astype(F32) + low_b[...].astype(F32) + (0.5 * gap) * back
    return low, pa + pb, hot_t


def merge_kernel(count, span, reqs, *refs):
    low, pack, _ = merge(count, span, reqs, *refs[:5])
    refs[5][...] = low.astype(BF)
    refs[6][...] = pack


def last_merge_kernel(count, span, reqs, feat, *refs):
    wide_out, col_out = refs[5:]
    low, pack, hot_t = merge(count, span, reqs, *refs[:5])
    rank, rows = low.shape
    means = pack[:count]
    mean = jnp.sum(means, axis=0, keepdims=True) / count
    dev = means - mean
    m2 = pack[count + 2 * reqs : count + 2 * reqs + 1] + feat * jnp.sum(dev * dev, axis=0, keepdims=True)
    rstd = lax.rsqrt(m2 / (count * feat) + 1e-06)
    shifted = lax.dot_general(
        pack[count + reqs : count + 2 * reqs, :rank], hot_t, (((0,), (0,)), ((), ())),
        precision=HIGH, preferred_element_type=F32,
    )
    low = (low * rstd + shifted).astype(BF).astype(F32)
    pad = 128 - rank - count - 1
    turned = jnp.concatenate([low, dev * rstd, rstd, jnp.zeros((pad, rows), F32)], axis=0).T
    col_out[...] = jnp.broadcast_to(turned[:, rank + count : rank + count + 1], (rows, 128))
    turned = turned.astype(BF)
    hot8 = refs[4][...][:, :reqs]

    def spread(src_count, width, rule):
        src = lax.broadcasted_iota(jnp.int32, (src_count, width), 0)
        dst = lax.broadcasted_iota(jnp.int32, (src_count, width), 1)
        return jnp.where(rule(src, dst), 1.0, 0.0).astype(BF)

    def times(a, b):
        return jnp.dot(a, b, preferred_element_type=F32)

    width = reqs * rank
    lora = times(turned, spread(128, width, lambda s, d: (d % rank == s) & (s < rank)))
    lora = lora * times(hot8, spread(reqs, width, lambda s, d: d // rank == s))
    pairs = count * reqs
    coef = times(turned, spread(128, 128, lambda s, d: (s == rank + d // reqs) & (d < pairs)))
    coef = coef * times(hot8, spread(reqs, 128, lambda s, d: (d % reqs == s) & (d < pairs)))
    coef = coef + times(
        hot8, spread(reqs, 128, lambda s, d: (d % reqs == s) & (d >= pairs) & (d < pairs + 2 * reqs))
    )
    wide_out[:, pl.ds(0, width)] = lora.astype(BF)
    wide_out[:, pl.ds(width, 128)] = coef.astype(BF)


def means_kernel(count, mod_ref, w_ref, bias_ref, after_ref, out_ref, total):
    step = pl.program_id(0)
    reqs = mod_ref.shape[1]
    feat = mod_ref.shape[2]
    lhs = jnp.concatenate([jnp.ones((reqs, feat), F32), mod_ref[1].astype(F32), mod_ref[0].astype(F32)], axis=0)
    lhs = jnp.concatenate([lhs, jnp.zeros((8, feat), F32)], axis=0).astype(BF)
    got = jnp.dot(lhs, w_ref[...], preferred_element_type=F32)
    total[0, pl.ds(pl.multiple_of(step * reqs, reqs), reqs), :] = got[:reqs] + got[reqs : 2 * reqs]

    @pl.when(step == 0)
    def _():
        total[1, pl.ds(0, reqs), :] = got[2 * reqs : 3 * reqs] + bias_ref[...].astype(F32)

    @pl.when(step > 0)
    def _():
        total[1, pl.ds(0, reqs), :] += got[2 * reqs : 3 * reqs]

    @pl.when(step == count - 1)
    def _():
        shift = total[1, pl.ds(0, reqs), :]
        high = shift.astype(BF).astype(F32)
        both = jnp.concatenate([high, shift - high], axis=0)
        left = 128 - count * reqs - 2 * reqs
        rows = [total[0, pl.ds(0, count * reqs), :], both]
        if left:
            rows.append(jnp.zeros((left, both.shape[1]), F32))
        out_ref[...] = jnp.concatenate(rows, axis=0).astype(BF)


N_TILE = 512


def first_kernel(count, blocks, base, ints, *refs):
    xs = refs[:blocks]
    w_ref, acc_out, w_now, sem = refs[blocks:]
    feat = xs[0].shape[1]
    hidden = acc_out.shape[1]
    tiles = hidden // N_TILE

    def copy(k, n):
        cols = pl.ds(n * N_TILE, N_TILE)
        at = pl.multiple_of(ints[base + k] * feat, feat)
        return pltpu.make_async_copy(
            w_ref.at[pl.ds(at, feat), cols], w_now.at[n, pl.ds(k * feat, feat), :], sem.at[k, n]
        )

    for n in range(tiles):
        for k in range(blocks):
            copy(k, n).start()
    lhs = jnp.concatenate([x[...] for x in xs], axis=1)
    for n in range(tiles):
        for k in range(blocks):
            copy(k, n).wait()
        acc_out[:, pl.ds(n * N_TILE, N_TILE)] = jnp.dot(lhs, w_now[n], preferred_element_type=F32)


def lora_kernel(
    count, blocks, base, ints, *refs
):
    xs = refs[:blocks]
    (w_ref, acc_in, wide_ref, col_ref, tail_ref, up_ref, recv_ref, acc_out, w_now, up_now, sem, up_sem) = refs[blocks:]
    feat = xs[0].shape[1]
    hidden = acc_out.shape[1]
    tiles = hidden // N_TILE
    reqs, rank = recv_ref.shape[:2]

    def copy(k, n):
        cols = pl.ds(n * N_TILE, N_TILE)
        at = pl.multiple_of(ints[base + k] * feat, feat)
        return pltpu.make_async_copy(
            w_ref.at[pl.ds(at, feat), cols], w_now.at[n, pl.ds(k * feat, feat), :], sem.at[k, n]
        )

    for n in range(tiles):
        for k in range(blocks):
            copy(k, n).start()
    fetch_adapters(count, ints, up_ref, recv_ref, up_now, up_sem, False)
    lhs = jnp.concatenate([x[...] for x in xs], axis=1)
    scale = col_ref[:, 0:1]
    for n in range(tiles):
        cols = pl.ds(n * N_TILE, N_TILE)
        for k in range(blocks):
            copy(k, n).wait()
        part = acc_in[:, cols] + jnp.dot(lhs, w_now[n], preferred_element_type=F32)
        acc_out[:, cols] = part * scale
    fetch_adapters(count, ints, up_ref, recv_ref, up_now, up_sem, True)
    width = reqs * rank
    wide = wide_ref[...]
    for n in range(tiles):
        cols = pl.ds(n * N_TILE, N_TILE)
        both = jnp.concatenate([up_now[:, cols], tail_ref[:, cols]], axis=0)
        acc_out[:, cols] += jnp.dot(wide, both, preferred_element_type=F32)


def finish_kernel(ints, c_ref, d_ref, col_ref, w_ref, acc_ref, w2_ref, act_out, part_out):
    upper = pl.program_id(0) < pl.num_programs(0) // 2
    x = jnp.where(upper, c_ref[...].astype(F32), d_ref[...].astype(F32)).astype(BF)
    pre = acc_ref[...] + jnp.dot(x, w_ref[...], preferred_element_type=F32) * col_ref[:, 0:1]
    act = jax.nn.gelu(pre, approximate=True).astype(BF)
    act_out[...] = act
    part_out[...] = jnp.dot(act, w2_ref[...], preferred_element_type=F32).astype(BF)


def second_kernel(blocks, base, ints, act_ref, w_ref, *refs):
    outs = refs[:blocks]
    w_now, sem = refs[blocks:]
    feat = outs[0].shape[1]

    def copy(k):
        at = pl.multiple_of(ints[base - k] * feat, feat)
        return pltpu.make_async_copy(
            w_ref.at[:, pl.ds(at, feat)], w_now.at[:, pl.ds(k * feat, feat)], sem.at[k]
        )

    for k in range(blocks):
        copy(k).start()
    for k in range(blocks):
        copy(k).wait()
    got = jnp.dot(act_ref[...], w_now[...], preferred_element_type=F32)
    for k in range(blocks):
        outs[k][...] = got[:, k * feat : (k + 1) * feat]


def ring_device(
    count, tokens, modulation, adapter_per_request, tokens_per_request, first_weight,
    first_bias, second_weight, second_bias, adapter_down_matrices, adapter_up_matrices,
):
    me = lax.axis_index("tensor")
    store = lax.axis_index("store")
    rows, feat = tokens.shape
    hidden = first_weight.shape[1]
    stored, rank = adapter_up_matrices.shape[:2]
    reqs = tokens_per_request.shape[1]
    order = ring_order(count)
    forth = [(order[i], order[(i + 1) % count]) for i in range(count)]
    back = [(b, a) for a, b in forth]
    half = count // 2
    visits = [0] + [s for k in range(1, half) for s in (-k, k)] + [half]
    table = [[0] * count for _ in range(count)]
    for at, dev in enumerate(order):
        table[dev] = [order[(at + k) % count] for k in visits]
    mine = lax.dynamic_index_in_dim(jnp.array(table, jnp.int32), me, 0, keepdims=False)

    def go(x, route):
        return lax.ppermute(x, "tensor", route)

    def like(*shape, kind=BF):
        return jax.ShapeDtypeStruct(shape, kind)

    down = jnp.swapaxes(adapter_down_matrices, 1, 2)
    mod = jnp.swapaxes(modulation[0], 0, 1)

    my_ids = lax.dynamic_index_in_dim(adapter_per_request, store, 0, keepdims=False)
    their_ids = lax.dynamic_index_in_dim(adapter_per_request, 1 - store, 0, keepdims=False)
    ids = jnp.concatenate([my_ids, their_ids])
    ints = jnp.concatenate(
        [
            mine,
            jnp.clip(ids - store * stored, 0, stored - 1),
            (my_ids // stored == store).astype(jnp.int32),
        ]
    )

    u, hot, stat = pl.pallas_call(
        own_kernel,
        in_specs=[SMEM, WHOLE, WHOLE],
        out_specs=[WHOLE] * 3,
        out_shape=[like(rows, feat), like(rows, 128), like(8, rows, kind=F32)],
        compiler_params=params(),
        cost_estimate=cost(2 * rows * feat, rows * feat),
        name="own_features",
    )(tokens_per_request, tokens, mod)

    send_down, mine_down, send_up = pl.pallas_call(
        send_kernel,
        in_specs=[SMEM, ANY, ANY],
        out_specs=[WHOLE] * 3,
        out_shape=[like(reqs, rank, feat)] * 2 + [like(reqs, rank, hidden)],
        scratch_shapes=[pltpu.SemaphoreType.DMA((3, reqs))],
        compiler_params=params(SEND_MIB),
        cost_estimate=cost(0, reqs * rank * (feat + hidden)),
        name="adapters_to_send",
    )(adapter_per_request, down, adapter_up_matrices)
    swap = [(s, s ^ 1) for s in range(lax.axis_size("store"))]
    recv_down = lax.ppermute(send_down, "store", swap)

    tail = pl.pallas_call(
        functools.partial(means_kernel, count),
        grid=(count,),
        in_specs=[
            pl.BlockSpec((3, reqs, feat), lambda i: (0, 0, i)),
            pl.BlockSpec((feat, hidden), lambda i: (i, 0)),
            pl.BlockSpec((1, hidden), lambda i: (0, 0)),
            ANY,
        ],
        out_specs=pl.BlockSpec((128, hidden), lambda i: (0, 0)),
        out_shape=like(128, hidden),
        scratch_shapes=[pltpu.VMEM((2, count * reqs, hidden), F32)],
        compiler_params=params(),
        cost_estimate=cost(64 * count * feat * hidden, 2 * count * feat * hidden, scale=0.1),
        name="means_part",
    )(mod, first_weight, first_bias.reshape(1, hidden), send_up)

    low, pack = pl.pallas_call(
        functools.partial(low_kernel, count, stored),
        in_specs=[SMEM] + [WHOLE] * 6,
        out_specs=[WHOLE] * 2,
        out_shape=[like(rank, rows), like(count + 2 * reqs + 8, rows, kind=F32)],
        scratch_shapes=[pltpu.VMEM((reqs * rank, feat), BF)],
        compiler_params=params(),
        cost_estimate=cost(rows * feat * reqs, rows * feat),
        name="low_rank_parts",
    )(adapter_per_request, u, hot, stat, mod, mine_down, recv_down)
    recv_up = lax.ppermute(send_up, "store", swap)

    cut = rows // 2
    a = b = u
    seen = [u]
    for k in range(1, half):
        a, b = go(a, forth), go(b, back)
        seen += [a, b]
        if k == 1:
            a, b, _ = lax.optimization_barrier((a, b, low))
    far_c, far_d = go(a[:cut], forth), go(b[cut:], back)

    turn = 0
    span = 1
    while span < count:
        route = [(t, t ^ span) for t in range(count)]
        low_b, pack_b = go(low, route), go(pack, route)
        turn += 1
        if turn in (1, 2):
            low_b, pack_b, *_ = lax.optimization_barrier((low_b, pack_b, seen[2 * turn - 1], seen[2 * turn]))
        args = (low, pack, low_b, pack_b, hot)
        if 2 * span == count:
            kernel = functools.partial(last_merge_kernel, count, span, reqs, feat)
            shapes = [like(rows, reqs * rank + 128), like(rows, 128, kind=F32)]
        else:
            kernel = functools.partial(merge_kernel, count, span, reqs)
            shapes = [like(*low.shape), like(*pack.shape, kind=F32)]
        low, pack = pl.pallas_call(
            kernel,
            in_specs=[WHOLE] * 5,
            out_specs=[WHOLE] * 2,
            out_shape=shapes,
            compiler_params=params(),
            cost_estimate=cost(1e+09, 8 * rank * rows),
            name="merge_sums",
        )(*args)
        span *= 2
    wide, cols = low, pack


    tiles = hidden // N_TILE
    early, late = seen[:-2], seen[-2:]
    w_scratch = lambda n: [
        pltpu.VMEM((tiles, n * feat, N_TILE), BF),
    ]
    acc = pl.pallas_call(
        functools.partial(first_kernel, count, len(early), 0),
        in_specs=[SMEM] + [WHOLE] * len(early) + [ANY],
        out_specs=WHOLE,
        out_shape=like(rows, hidden, kind=F32),
        scratch_shapes=w_scratch(len(early)) + [pltpu.SemaphoreType.DMA((len(early), tiles))],
        compiler_params=params(24),
        cost_estimate=cost(2 * rows * feat * hidden * len(early), 2 * feat * hidden * len(early), scale=1),
        name="first_blocks",
    )(ints, *early, first_weight)
    acc = pl.pallas_call(
        functools.partial(lora_kernel, count, len(late), len(early)),
        in_specs=[SMEM] + [WHOLE] * len(late) + [ANY] + [WHOLE] * 4 + [ANY, ANY],
        out_specs=WHOLE,
        out_shape=like(rows, hidden, kind=F32),
        scratch_shapes=w_scratch(len(late))
        + [
            pltpu.VMEM((reqs * rank, hidden), BF),
            pltpu.SemaphoreType.DMA((len(late), tiles)),
            pltpu.SemaphoreType.DMA((reqs,)),
        ],
        compiler_params=params(24),
        cost_estimate=cost(
            2 * rows * hidden * (feat * len(late) + reqs * rank), 2 * feat * hidden * len(late), scale=1),
        name="low_rank_added",
    )(ints, *late, first_weight, acc, wide, cols, tail, adapter_up_matrices, recv_up)
    steps = 4
    tile = rows // steps
    last = count - 1
    tiled = lambda width: pl.BlockSpec((tile, width), lambda i, *s: (i, 0))
    act, far_part = pl.pallas_call(
        finish_kernel,
        grid_spec=pltpu.PrefetchScalarGridSpec(
            num_scalar_prefetch=1,
            grid=(steps,),
            in_specs=[
                pl.BlockSpec((tile, feat), lambda i, s: (jnp.minimum(i, steps // 2 - 1), 0)),
                pl.BlockSpec((tile, feat), lambda i, s: (jnp.maximum(i - steps // 2, 0), 0)),
                tiled(128),
                pl.BlockSpec((feat, hidden), lambda i, s: (s[last], 0)),
                tiled(hidden),
                pl.BlockSpec((hidden, feat), lambda i, s: (0, s[last])),
            ],
            out_specs=[tiled(hidden), tiled(feat)],
        ),
        out_shape=[like(rows, hidden), like(rows, feat)],
        compiler_params=params(16),
        cost_estimate=cost(4 * rows * hidden * feat, 14 * rows * hidden, rows * hidden, scale=1),
        name="finish_first",
    )(ints, far_c, far_d, cols, first_weight, acc, second_weight)

    def second(blocks, base, name):
        return pl.pallas_call(
            functools.partial(second_kernel, blocks, base),
            in_specs=[SMEM, WHOLE, ANY],
            out_specs=[WHOLE] * blocks,
            out_shape=[like(rows, feat, kind=F32)] * blocks,
            scratch_shapes=[
                pltpu.VMEM((hidden, blocks * feat), BF),
                pltpu.SemaphoreType.DMA((blocks,)),
            ],
            compiler_params=params(16),
            cost_estimate=cost(2 * rows * hidden * feat * blocks, blocks * rows * feat * 8),
            name=name,
        )(ints, act, second_weight)

    parts = {}
    base = count - 2
    for k in range(half - 1, 0, -1):
        blocks = 3 if k == 1 else 2
        got = second(blocks, base, "second_blocks")
        base -= blocks
        parts[k], parts[-k] = got[0], got[1]
    parts[0] = got[2]
    gate = jnp.dot(
        hot[:, :reqs], lax.dynamic_slice_in_dim(mod[2], me * feat, feat, 1),
        preferred_element_type=F32,
    )
    rights, lefts = [], []
    chains = 1
    size = rows // chains
    for c in range(chains):
        lo = c * size
        mid = size // 2
        right = go(far_part[lo : lo + mid], forth)
        left = go(far_part[lo + mid : lo + size], back)
        for k in range(half - 1, 0, -1):
            r = parts[k][lo : lo + size]
            l = parts[-k][lo : lo + size]
            if k == half - 1:
                r = jnp.concatenate([r[:mid] + right.astype(F32), r[mid:]])
                l = jnp.concatenate([l[:mid], l[mid:] + left.astype(F32)])
            else:
                r = r + right.astype(F32)
                l = l + left.astype(F32)
            right = go(r.astype(BF), forth)
            left = go(l.astype(BF), back)
        rights.append(right)
        lefts.append(left)
    mixed = parts[0] + jnp.concatenate(rights).astype(F32) + jnp.concatenate(lefts).astype(F32)
    return (tokens.astype(F32) + gate * (mixed + second_bias.astype(F32))).astype(BF)


def partner(block, axis, stride):
    count = lax.axis_size(axis)
    route = []
    for low in range(count):
        high = low | 1 << stride
        if high != low and high < count:
            route += [(low, high), (high, low)]
    return lax.ppermute(block, axis, route)


def request_onehot(lengths, row_count, req_count):
    bounds = jnp.cumsum(lengths)
    places = jnp.arange(row_count, dtype=jnp.int32)
    owner_req = jnp.sum((places[:, None] >= bounds[None, :]).astype(jnp.int32), axis=1)
    return (owner_req[:, None] == jnp.arange(req_count, dtype=jnp.int32)[None, :]).astype(
        jnp.float32
    )


def plain_device(
    tokens,
    modulation,
    adapter_per_request,
    tokens_per_request,
    first_weight,
    first_bias,
    second_weight,
    second_bias,
    adapter_down_matrices,
    adapter_up_matrices,
):
    tensor_index = lax.axis_index("tensor")
    store_index = lax.axis_index("store")
    tok_rows, feat_width = tokens.shape
    req_count = tokens_per_request.shape[1]
    rank_column_width = adapter_down_matrices.shape[2]
    hidden_width = first_weight.shape[1]
    store_request_count = adapter_down_matrices.shape[0]
    gathered = lax.all_gather(tokens, "tensor", axis=1, tiled=True).astype(jnp.float32)
    adapter_indicator = request_onehot(tokens_per_request[0], tok_rows, req_count)
    factors = modulation[0].astype(jnp.float32)
    shift_rows = jnp.dot(adapter_indicator, factors[:, 0], precision=lax.Precision.HIGHEST)
    scale_rows = jnp.dot(adapter_indicator, factors[:, 1], precision=lax.Precision.HIGHEST)
    gate_own = lax.dynamic_slice_in_dim(factors[:, 2], tensor_index * feat_width, feat_width, 1)
    gate_rows = jnp.dot(adapter_indicator, gate_own, precision=lax.Precision.HIGHEST)
    center = jnp.mean(gathered, axis=1, keepdims=True)
    spread = jnp.mean((gathered - center) ** 2, axis=1, keepdims=True)
    normed = (gathered - center) * lax.rsqrt(spread + 1e-06)
    modded = ((1.0 + scale_rows) * normed + shift_rows).astype(jnp.bfloat16)

    def pick_owned(wanted):
        owned_mask = wanted // store_request_count == store_index
        request_index_list = jnp.clip(
            wanted - store_index * store_request_count, 0, store_request_count - 1
        )
        down_matrix_rows = jnp.take(adapter_down_matrices, request_index_list, axis=0)
        up_matrix_rows = jnp.take(adapter_up_matrices, request_index_list, axis=0)
        keep = owned_mask[:, None, None]
        return (
            owned_mask,
            jnp.where(keep, down_matrix_rows, jnp.zeros_like(down_matrix_rows)),
            jnp.where(keep, up_matrix_rows, jnp.zeros_like(up_matrix_rows)),
        )

    mine_ids = lax.dynamic_index_in_dim(adapter_per_request, store_index, 0, keepdims=False)
    other_ids = lax.dynamic_index_in_dim(adapter_per_request, 1 - store_index, 0, keepdims=False)
    mine_owned, mine_down, mine_up = pick_owned(mine_ids)
    other_owned, send_down, send_up = pick_owned(other_ids)
    recv_down, recv_up = partner((send_down, send_up), "store", 0)
    down_now = jnp.where(mine_owned[:, None, None], mine_down, recv_down)
    up_now = jnp.where(mine_owned[:, None, None], mine_up, recv_up)
    low_rank_every = jnp.einsum(
        "tn,knr->tkr",
        modded,
        lax.all_gather(down_now, "tensor", axis=1, tiled=True),
        preferred_element_type=jnp.float32,
    )
    low_rank_sum = jnp.sum(adapter_indicator[:, :, None] * low_rank_every, axis=1)
    adapter_low_rank = low_rank_sum.astype(jnp.bfloat16)
    broadcast_low_rank = (
        (adapter_indicator[:, :, None] * adapter_low_rank.astype(jnp.float32)[:, None, :])
        .reshape(tok_rows, req_count * rank_column_width)
        .astype(jnp.bfloat16)
    )
    preact = jnp.dot(modded, first_weight, preferred_element_type=jnp.float32) + first_bias.astype(
        jnp.float32
    )
    preact = preact + jnp.dot(
        broadcast_low_rank,
        up_now.reshape(req_count * rank_column_width, hidden_width),
        preferred_element_type=jnp.float32,
    )
    activated = jax.nn.gelu(preact, approximate=True).astype(jnp.bfloat16)
    own_share = lax.psum_scatter(
        lax.dot_general(
            second_weight, activated, (((0,), (1,)), ((), ())), preferred_element_type=jnp.float32
        ),
        "tensor",
        scatter_dimension=0,
        tiled=True,
    ).T
    block_out = tokens.astype(jnp.float32) + gate_rows * (
        own_share + second_bias.astype(jnp.float32)
    )
    return block_out.astype(jnp.bfloat16)


def on_device(count, tokens, *rest):
    if tokens.shape[1] % 128 == 0 and count % 4 == 0 and count & (count - 1) == 0:
        return ring_device(count, tokens, *rest)
    return plain_device(tokens, *rest)


def solution(mesh):
    in_specs = (
        P(("groups", "store"), "tensor"),
        P(("groups", "store"), None, None, None),
        P("groups", None),
        P(("groups", "store"), None),
        P(None, "tensor"),
        P("tensor"),
        P("tensor", None),
        P("tensor"),
        P("store", "tensor", None),
        P("store", None, "tensor"),
    )
    out_specs = P(("groups", "store"), "tensor")
    return jax.shard_map(
        functools.partial(on_device, mesh.shape["tensor"]), mesh=mesh, in_specs=in_specs, out_specs=out_specs, check_vma=False
    )
```

```python
import functools

import jax
import jax.numpy as jnp
from jax import lax
from jax.experimental import pallas as pl
from jax.experimental.pallas import tpu as pltpu
from jax.sharding import PartitionSpec as P

BF = jnp.bfloat16
F32 = jnp.float32
SEND_MIB = 60
HIGH = lax.Precision.HIGHEST
ANY = pl.BlockSpec(memory_space=pltpu.HBM)
SMEM = pl.BlockSpec(memory_space=pltpu.SMEM)
WHOLE = pl.BlockSpec(memory_space=pltpu.VMEM)


def params(mib=24):
    return pltpu.CompilerParams(vmem_limit_bytes=mib * 1024 * 1024)


def cost(flops, nbytes, trans=0, scale=1.0):
    flops, nbytes, trans = flops * scale, nbytes * scale, trans * scale
    return pl.CostEstimate(
        flops=int(flops), bytes_accessed=int(nbytes), transcendentals=int(trans)
    )


def ring_order(count):
    cols = 2 if count < 32 else 4
    rows = count // cols
    walk = [r * cols for r in range(rows)]
    for i, r in enumerate(reversed(range(rows))):
        across = list(range(1, cols))
        walk += [r * cols + c for c in (across if i % 2 == 0 else across[::-1])]
    return walk


def blocks_in(ref, width, at, axis):
    place = pl.ds(pl.multiple_of(at * width, width), width)
    return ref.at[place, :] if axis == 0 else ref.at[:, place]


def place(ids, whose, r, stored):
    return jnp.clip(ids[whose, r] - lax.axis_index("store") * stored, 0, stored - 1)


def send_kernel(ids, down_ref, up_ref, down_out, mine_out, up_out, sem):
    reqs = down_out.shape[0]
    stored = down_ref.shape[0]
    me = lax.axis_index("store")
    copies = []
    for r in range(reqs):
        at = place(ids, 1 - me, r, stored)
        own = place(ids, me, r, stored)
        copies.append(pltpu.make_async_copy(down_ref.at[at], down_out.at[r], sem.at[0, r]))
        copies.append(pltpu.make_async_copy(down_ref.at[own], mine_out.at[r], sem.at[1, r]))
        copies.append(pltpu.make_async_copy(up_ref.at[at], up_out.at[r], sem.at[2, r]))
    for c in copies:
        c.start()
    for c in copies:
        c.wait()


def fetch_adapters(count, ints, store_ref, recv_ref, dst, sem, wait):
    reqs, rank = recv_ref.shape[:2]
    for r in range(reqs):
        here = dst.at[pl.ds(r * rank, rank)]
        if wait:
            pltpu.make_async_copy(recv_ref.at[r], here, sem.at[r]).wait()
            continue
        own = ints[count + 2 * reqs + r]

        @pl.when(own == 1)
        def _():
            pltpu.make_async_copy(store_ref.at[ints[count + r]], here, sem.at[r]).start()

        @pl.when(own == 0)
        def _():
            pltpu.make_async_copy(recv_ref.at[r], here, sem.at[r]).start()


def own_kernel(lengths, x_ref, mod_ref, u_out, hot_out, stat_out):
    rows, feat = x_ref.shape
    reqs = mod_ref.shape[1]
    own = pl.ds(pl.multiple_of(lax.axis_index("tensor") * feat, feat), feat)
    x = x_ref[...].astype(F32)
    mean = jnp.mean(x, axis=1, keepdims=True)
    cent = x - mean
    m2 = jnp.sum(cent * cent, axis=1, keepdims=True)
    row = lax.broadcasted_iota(jnp.int32, (rows, 128), 0)
    lane = lax.broadcasted_iota(jnp.int32, (rows, 128), 1)
    first = jnp.zeros((1, 128), jnp.int32)
    after = jnp.zeros((1, 128), jnp.int32)
    lane1 = lax.broadcasted_iota(jnp.int32, (1, 128), 1)
    begin = jnp.int32(0)
    for r in range(reqs):
        end = begin + lengths[0, r]
        first = jnp.where(lane1 == r, begin, first)
        after = jnp.where(lane1 == r, end, after)
        begin = end
    hot = jnp.where((row >= first) & (row < after), 1.0, 0.0)
    hot_out[...] = hot.astype(BF)
    stat_out[...] = jnp.where(lane == 0, mean, jnp.where(lane == 1, m2, 0.0)).T[:8]
    scale_rows = jnp.dot(hot[:, :reqs].astype(BF), mod_ref[1, :, own], preferred_element_type=F32)
    u_out[...] = (cent * (1.0 + scale_rows)).astype(BF)


def low_kernel(
    count, stored, ids, u_ref, hot_ref, stat_ref, mod_ref, mine_ref, recv_ref, low_out, pack_out, down_now
):
    rows, feat = u_ref.shape
    reqs, rank = recv_ref.shape[:2]
    me = lax.axis_index("tensor")
    store = lax.axis_index("store")
    own = pl.ds(pl.multiple_of(me * feat, feat), feat)
    for r in range(reqs):
        here = pl.ds(r * rank, rank)

        @pl.when(ids[store, r] // stored == store)
        def _():
            down_now[here, :] = mine_ref[r]

        @pl.when(ids[store, r] // stored != store)
        def _():
            down_now[here, :] = recv_ref[r]

    hot_t = hot_ref[...].astype(F32).T
    every = lax.dot_general(
        down_now[...], u_ref[...], (((1,), (1,)), ((), ())), preferred_element_type=F32
    )
    total = jnp.zeros((rank, rows), F32)
    side = jnp.zeros((rank, 128), F32)
    lane = lax.broadcasted_iota(jnp.int32, (rank, 128), 1)
    for r in range(reqs):
        total = total + every[r * rank : (r + 1) * rank] * hot_t[r : r + 1]
        mat = down_now[pl.ds(r * rank, rank), :].astype(F32)
        by_scale = jnp.sum(mat * (1.0 + mod_ref[1, pl.ds(r, 1), own].astype(F32)), axis=1, keepdims=True)
        by_shift = jnp.sum(mat * mod_ref[0, pl.ds(r, 1), own].astype(F32), axis=1, keepdims=True)
        side = jnp.where(lane == r, by_scale, side)
        side = jnp.where(lane == reqs + r, by_shift, side)
    low_out[...] = total.astype(BF)
    stat = stat_ref[...]
    here = lax.broadcasted_iota(jnp.int32, (count, rows), 0) == me
    pack_out[pl.ds(0, count), :] = jnp.where(here, stat[0:1], 0.0)
    turned = jnp.concatenate([side, jnp.zeros((128 - rank, 128), F32)], axis=0).T
    flat = jnp.concatenate([turned[: 2 * reqs], jnp.zeros((2 * reqs, rows - 128), F32)], axis=1)
    pack_out[pl.ds(count, 2 * reqs), :] = flat
    pack_out[pl.ds(count + 2 * reqs, 8), :] = jnp.broadcast_to(stat[1:2], (8, rows))


def merge(count, span, reqs, low_a, pack_a, low_b, pack_b, hot_ref):
    hot_t = hot_ref[...].astype(F32).T[:reqs]
    pa, pb = pack_a[...], pack_b[...]
    rank = low_a.shape[0]
    gap = (jnp.sum(pa[:count], axis=0, keepdims=True) - jnp.sum(pb[:count], axis=0, keepdims=True)) / span
    diff = (pa - pb)[count : count + reqs, :rank]
    back = lax.dot_general(
        diff, hot_t, (((0,), (0,)), ((), ())), precision=HIGH, preferred_element_type=F32
    )
    low = low_a[...].astype(F32) + low_b[...].astype(F32) + (0.5 * gap) * back
    return low, pa + pb, hot_t


def merge_kernel(count, span, reqs, *refs):
    low, pack, _ = merge(count, span, reqs, *refs[:5])
    refs[5][...] = low.astype(BF)
    refs[6][...] = pack


def last_merge_kernel(count, span, reqs, feat, *refs):
    wide_out, col_out = refs[5:]
    low, pack, hot_t = merge(count, span, reqs, *refs[:5])
    rank, rows = low.shape
    means = pack[:count]
    mean = jnp.sum(means, axis=0, keepdims=True) / count
    dev = means - mean
    m2 = pack[count + 2 * reqs : count + 2 * reqs + 1] + feat * jnp.sum(dev * dev, axis=0, keepdims=True)
    rstd = lax.rsqrt(m2 / (count * feat) + 1e-06)
    shifted = lax.dot_general(
        pack[count + reqs : count + 2 * reqs, :rank], hot_t, (((0,), (0,)), ((), ())),
        precision=HIGH, preferred_element_type=F32,
    )
    low = (low * rstd + shifted).astype(BF).astype(F32)
    pad = 128 - rank - count - 1
    turned = jnp.concatenate([low, dev * rstd, rstd, jnp.zeros((pad, rows), F32)], axis=0).T
    col_out[...] = jnp.broadcast_to(turned[:, rank + count : rank + count + 1], (rows, 128))
    turned = turned.astype(BF)
    hot8 = refs[4][...][:, :reqs]

    def spread(src_count, width, rule):
        src = lax.broadcasted_iota(jnp.int32, (src_count, width), 0)
        dst = lax.broadcasted_iota(jnp.int32, (src_count, width), 1)
        return jnp.where(rule(src, dst), 1.0, 0.0).astype(BF)

    def times(a, b):
        return jnp.dot(a, b, preferred_element_type=F32)

    width = reqs * rank
    lora = times(turned, spread(128, width, lambda s, d: (d % rank == s) & (s < rank)))
    lora = lora * times(hot8, spread(reqs, width, lambda s, d: d // rank == s))
    pairs = count * reqs
    coef = times(turned, spread(128, 128, lambda s, d: (s == rank + d // reqs) & (d < pairs)))
    coef = coef * times(hot8, spread(reqs, 128, lambda s, d: (d % reqs == s) & (d < pairs)))
    coef = coef + times(
        hot8, spread(reqs, 128, lambda s, d: (d % reqs == s) & (d >= pairs) & (d < pairs + 2 * reqs))
    )
    wide_out[:, pl.ds(0, width)] = lora.astype(BF)
    wide_out[:, pl.ds(width, 128)] = coef.astype(BF)


def means_kernel(count, mod_ref, w_ref, bias_ref, after_ref, out_ref, total):
    step = pl.program_id(0)
    reqs = mod_ref.shape[1]
    feat = mod_ref.shape[2]
    lhs = jnp.concatenate([jnp.ones((reqs, feat), F32), mod_ref[1].astype(F32), mod_ref[0].astype(F32)], axis=0)
    lhs = jnp.concatenate([lhs, jnp.zeros((8, feat), F32)], axis=0).astype(BF)
    got = jnp.dot(lhs, w_ref[...], preferred_element_type=F32)
    total[0, pl.ds(pl.multiple_of(step * reqs, reqs), reqs), :] = got[:reqs] + got[reqs : 2 * reqs]

    @pl.when(step == 0)
    def _():
        total[1, pl.ds(0, reqs), :] = got[2 * reqs : 3 * reqs] + bias_ref[...].astype(F32)

    @pl.when(step > 0)
    def _():
        total[1, pl.ds(0, reqs), :] += got[2 * reqs : 3 * reqs]

    @pl.when(step == count - 1)
    def _():
        shift = total[1, pl.ds(0, reqs), :]
        high = shift.astype(BF).astype(F32)
        both = jnp.concatenate([high, shift - high], axis=0)
        left = 128 - count * reqs - 2 * reqs
        rows = [total[0, pl.ds(0, count * reqs), :], both]
        if left:
            rows.append(jnp.zeros((left, both.shape[1]), F32))
        out_ref[...] = jnp.concatenate(rows, axis=0).astype(BF)


N_TILE = 512


def first_kernel(count, blocks, base, ints, *refs):
    xs = refs[:blocks]
    w_ref, acc_out, w_now, sem = refs[blocks:]
    feat = xs[0].shape[1]
    hidden = acc_out.shape[1]
    tiles = hidden // N_TILE

    def copy(k, n):
        cols = pl.ds(n * N_TILE, N_TILE)
        at = pl.multiple_of(ints[base + k] * feat, feat)
        return pltpu.make_async_copy(
            w_ref.at[pl.ds(at, feat), cols], w_now.at[n, pl.ds(k * feat, feat), :], sem.at[k, n]
        )

    for n in range(tiles):
        for k in range(blocks):
            copy(k, n).start()
    lhs = jnp.concatenate([x[...] for x in xs], axis=1)
    for n in range(tiles):
        for k in range(blocks):
            copy(k, n).wait()
        acc_out[:, pl.ds(n * N_TILE, N_TILE)] = jnp.dot(lhs, w_now[n], preferred_element_type=F32)


def lora_kernel(
    count, blocks, base, ints, *refs
):
    xs = refs[:blocks]
    (w_ref, acc_in, wide_ref, col_ref, tail_ref, up_ref, recv_ref, acc_out, w_now, up_now, sem, up_sem) = refs[blocks:]
    feat = xs[0].shape[1]
    hidden = acc_out.shape[1]
    tiles = hidden // N_TILE
    reqs, rank = recv_ref.shape[:2]

    def copy(k, n):
        cols = pl.ds(n * N_TILE, N_TILE)
        at = pl.multiple_of(ints[base + k] * feat, feat)
        return pltpu.make_async_copy(
            w_ref.at[pl.ds(at, feat), cols], w_now.at[n, pl.ds(k * feat, feat), :], sem.at[k, n]
        )

    for n in range(tiles):
        for k in range(blocks):
            copy(k, n).start()
    fetch_adapters(count, ints, up_ref, recv_ref, up_now, up_sem, False)
    lhs = jnp.concatenate([x[...] for x in xs], axis=1)
    scale = col_ref[:, 0:1]
    for n in range(tiles):
        cols = pl.ds(n * N_TILE, N_TILE)
        for k in range(blocks):
            copy(k, n).wait()
        part = acc_in[:, cols] + jnp.dot(lhs, w_now[n], preferred_element_type=F32)
        acc_out[:, cols] = part * scale
    fetch_adapters(count, ints, up_ref, recv_ref, up_now, up_sem, True)
    width = reqs * rank
    wide = wide_ref[...]
    for n in range(tiles):
        cols = pl.ds(n * N_TILE, N_TILE)
        both = jnp.concatenate([up_now[:, cols], tail_ref[:, cols]], axis=0)
        acc_out[:, cols] += jnp.dot(wide, both, preferred_element_type=F32)


def finish_kernel(ints, c_ref, d_ref, col_ref, w_ref, acc_ref, w2_ref, act_out, part_out):
    upper = pl.program_id(0) < pl.num_programs(0) // 2
    x = jnp.where(upper, c_ref[...].astype(F32), d_ref[...].astype(F32)).astype(BF)
    pre = acc_ref[...] + jnp.dot(x, w_ref[...], preferred_element_type=F32) * col_ref[:, 0:1]
    act = jax.nn.gelu(pre, approximate=True).astype(BF)
    act_out[...] = act
    part_out[...] = jnp.dot(act, w2_ref[...], preferred_element_type=F32).astype(BF)


def second_kernel(blocks, base, ints, act_ref, w_ref, *refs):
    outs = refs[:blocks]
    w_now, sem = refs[blocks:]
    feat = outs[0].shape[1]

    def copy(k):
        at = pl.multiple_of(ints[base - k] * feat, feat)
        return pltpu.make_async_copy(
            w_ref.at[:, pl.ds(at, feat)], w_now.at[:, pl.ds(k * feat, feat)], sem.at[k]
        )

    for k in range(blocks):
        copy(k).start()
    for k in range(blocks):
        copy(k).wait()
    got = jnp.dot(act_ref[...], w_now[...], preferred_element_type=F32)
    for k in range(blocks):
        outs[k][...] = got[:, k * feat : (k + 1) * feat]


def ring_device(
    count, tokens, modulation, adapter_per_request, tokens_per_request, first_weight,
    first_bias, second_weight, second_bias, adapter_down_matrices, adapter_up_matrices,
):
    me = lax.axis_index("tensor")
    store = lax.axis_index("store")
    rows, feat = tokens.shape
    hidden = first_weight.shape[1]
    stored, rank = adapter_up_matrices.shape[:2]
    reqs = tokens_per_request.shape[1]
    order = ring_order(count)
    forth = [(order[i], order[(i + 1) % count]) for i in range(count)]
    back = [(b, a) for a, b in forth]
    half = count // 2
    visits = [0] + [s for k in range(1, half) for s in (-k, k)] + [half]
    table = [[0] * count for _ in range(count)]
    for at, dev in enumerate(order):
        table[dev] = [order[(at + k) % count] for k in visits]
    mine = lax.dynamic_index_in_dim(jnp.array(table, jnp.int32), me, 0, keepdims=False)

    def go(x, route):
        return lax.ppermute(x, "tensor", route)

    def like(*shape, kind=BF):
        return jax.ShapeDtypeStruct(shape, kind)

    down = jnp.swapaxes(adapter_down_matrices, 1, 2)
    mod = jnp.swapaxes(modulation[0], 0, 1)

    my_ids = lax.dynamic_index_in_dim(adapter_per_request, store, 0, keepdims=False)
    their_ids = lax.dynamic_index_in_dim(adapter_per_request, 1 - store, 0, keepdims=False)
    ids = jnp.concatenate([my_ids, their_ids])
    ints = jnp.concatenate(
        [
            mine,
            jnp.clip(ids - store * stored, 0, stored - 1),
            (my_ids // stored == store).astype(jnp.int32),
        ]
    )

    u, hot, stat = pl.pallas_call(
        own_kernel,
        in_specs=[SMEM, WHOLE, WHOLE],
        out_specs=[WHOLE] * 3,
        out_shape=[like(rows, feat), like(rows, 128), like(8, rows, kind=F32)],
        compiler_params=params(),
        cost_estimate=cost(2 * rows * feat, rows * feat),
        name="own_features",
    )(tokens_per_request, tokens, mod)

    send_down, mine_down, send_up = pl.pallas_call(
        send_kernel,
        in_specs=[SMEM, ANY, ANY],
        out_specs=[WHOLE] * 3,
        out_shape=[like(reqs, rank, feat)] * 2 + [like(reqs, rank, hidden)],
        scratch_shapes=[pltpu.SemaphoreType.DMA((3, reqs))],
        compiler_params=params(SEND_MIB),
        cost_estimate=cost(0, reqs * rank * (feat + hidden)),
        name="adapters_to_send",
    )(adapter_per_request, down, adapter_up_matrices)
    swap = [(s, s ^ 1) for s in range(lax.axis_size("store"))]
    recv_down = lax.ppermute(send_down, "store", swap)

    tail = pl.pallas_call(
        functools.partial(means_kernel, count),
        grid=(count,),
        in_specs=[
            pl.BlockSpec((3, reqs, feat), lambda i: (0, 0, i)),
            pl.BlockSpec((feat, hidden), lambda i: (i, 0)),
            pl.BlockSpec((1, hidden), lambda i: (0, 0)),
            ANY,
        ],
        out_specs=pl.BlockSpec((128, hidden), lambda i: (0, 0)),
        out_shape=like(128, hidden),
        scratch_shapes=[pltpu.VMEM((2, count * reqs, hidden), F32)],
        compiler_params=params(),
        cost_estimate=cost(64 * count * feat * hidden, 2 * count * feat * hidden, scale=0.1),
        name="means_part",
    )(mod, first_weight, first_bias.reshape(1, hidden), send_up)

    low, pack = pl.pallas_call(
        functools.partial(low_kernel, count, stored),
        in_specs=[SMEM] + [WHOLE] * 6,
        out_specs=[WHOLE] * 2,
        out_shape=[like(rank, rows), like(count + 2 * reqs + 8, rows, kind=F32)],
        scratch_shapes=[pltpu.VMEM((reqs * rank, feat), BF)],
        compiler_params=params(),
        cost_estimate=cost(rows * feat * reqs, rows * feat),
        name="low_rank_parts",
    )(adapter_per_request, u, hot, stat, mod, mine_down, recv_down)
    recv_up = lax.ppermute(send_up, "store", swap)

    cut = rows // 2
    a = b = u
    seen = [u]
    for k in range(1, half):
        a, b = go(a, forth), go(b, back)
        seen += [a, b]
        if k == 1:
            a, b, _ = lax.optimization_barrier((a, b, low))
    far_c, far_d = go(a[:cut], forth), go(b[cut:], back)

    turn = 0
    span = 1
    while span < count:
        route = [(t, t ^ span) for t in range(count)]
        low_b, pack_b = go(low, route), go(pack, route)
        turn += 1
        if turn in (1, 2):
            low_b, pack_b, *_ = lax.optimization_barrier((low_b, pack_b, seen[2 * turn - 1], seen[2 * turn]))
        args = (low, pack, low_b, pack_b, hot)
        if 2 * span == count:
            kernel = functools.partial(last_merge_kernel, count, span, reqs, feat)
            shapes = [like(rows, reqs * rank + 128), like(rows, 128, kind=F32)]
        else:
            kernel = functools.partial(merge_kernel, count, span, reqs)
            shapes = [like(*low.shape), like(*pack.shape, kind=F32)]
        low, pack = pl.pallas_call(
            kernel,
            in_specs=[WHOLE] * 5,
            out_specs=[WHOLE] * 2,
            out_shape=shapes,
            compiler_params=params(),
            cost_estimate=cost(1e+09, 8 * rank * rows),
            name="merge_sums",
        )(*args)
        span *= 2
    wide, cols = low, pack


    tiles = hidden // N_TILE
    early, late = seen[:-2], seen[-2:]
    w_scratch = lambda n: [
        pltpu.VMEM((tiles, n * feat, N_TILE), BF),
    ]
    acc = pl.pallas_call(
        functools.partial(first_kernel, count, len(early), 0),
        in_specs=[SMEM] + [WHOLE] * len(early) + [ANY],
        out_specs=WHOLE,
        out_shape=like(rows, hidden, kind=F32),
        scratch_shapes=w_scratch(len(early)) + [pltpu.SemaphoreType.DMA((len(early), tiles))],
        compiler_params=params(24),
        cost_estimate=cost(2 * rows * feat * hidden * len(early), 2 * feat * hidden * len(early), scale=1),
        name="first_blocks",
    )(ints, *early, first_weight)
    acc = pl.pallas_call(
        functools.partial(lora_kernel, count, len(late), len(early)),
        in_specs=[SMEM] + [WHOLE] * len(late) + [ANY] + [WHOLE] * 4 + [ANY, ANY],
        out_specs=WHOLE,
        out_shape=like(rows, hidden, kind=F32),
        scratch_shapes=w_scratch(len(late))
        + [
            pltpu.VMEM((reqs * rank, hidden), BF),
            pltpu.SemaphoreType.DMA((len(late), tiles)),
            pltpu.SemaphoreType.DMA((reqs,)),
        ],
        compiler_params=params(24),
        cost_estimate=cost(
            2 * rows * hidden * (feat * len(late) + reqs * rank), 2 * feat * hidden * len(late), scale=1),
        name="low_rank_added",
    )(ints, *late, first_weight, acc, wide, cols, tail, adapter_up_matrices, recv_up)
    steps = 2
    tile = rows // steps
    last = count - 1
    tiled = lambda width: pl.BlockSpec((tile, width), lambda i, *s: (i, 0))
    act, far_part = pl.pallas_call(
        finish_kernel,
        grid_spec=pltpu.PrefetchScalarGridSpec(
            num_scalar_prefetch=1,
            grid=(steps,),
            in_specs=[
                pl.BlockSpec((tile, feat), lambda i, s: (jnp.minimum(i, steps // 2 - 1), 0)),
                pl.BlockSpec((tile, feat), lambda i, s: (jnp.maximum(i - steps // 2, 0), 0)),
                tiled(128),
                pl.BlockSpec((feat, hidden), lambda i, s: (s[last], 0)),
                tiled(hidden),
                pl.BlockSpec((hidden, feat), lambda i, s: (0, s[last])),
            ],
            out_specs=[tiled(hidden), tiled(feat)],
        ),
        out_shape=[like(rows, hidden), like(rows, feat)],
        compiler_params=params(16),
        cost_estimate=cost(4 * rows * hidden * feat, 14 * rows * hidden, rows * hidden, scale=1),
        name="finish_first",
    )(ints, far_c, far_d, cols, first_weight, acc, second_weight)

    def second(blocks, base, name):
        return pl.pallas_call(
            functools.partial(second_kernel, blocks, base),
            in_specs=[SMEM, WHOLE, ANY],
            out_specs=[WHOLE] * blocks,
            out_shape=[like(rows, feat, kind=F32)] * blocks,
            scratch_shapes=[
                pltpu.VMEM((hidden, blocks * feat), BF),
                pltpu.SemaphoreType.DMA((blocks,)),
            ],
            compiler_params=params(16),
            cost_estimate=cost(2 * rows * hidden * feat * blocks, blocks * rows * feat * 8),
            name=name,
        )(ints, act, second_weight)

    parts = {}
    base = count - 2
    for k in range(half - 1, 0, -1):
        blocks = 3 if k == 1 else 2
        got = second(blocks, base, "second_blocks")
        base -= blocks
        parts[k], parts[-k] = got[0], got[1]
    parts[0] = got[2]
    gate = jnp.dot(
        hot[:, :reqs], lax.dynamic_slice_in_dim(mod[2], me * feat, feat, 1),
        preferred_element_type=F32,
    )
    rights, lefts = [], []
    chains = 1
    size = rows // chains
    for c in range(chains):
        lo = c * size
        mid = size // 2
        right = go(far_part[lo : lo + mid], forth)
        left = go(far_part[lo + mid : lo + size], back)
        for k in range(half - 1, 0, -1):
            r = parts[k][lo : lo + size]
            l = parts[-k][lo : lo + size]
            if k == half - 1:
                r = jnp.concatenate([r[:mid] + right.astype(F32), r[mid:]])
                l = jnp.concatenate([l[:mid], l[mid:] + left.astype(F32)])
            else:
                r = r + right.astype(F32)
                l = l + left.astype(F32)
            right = go(r.astype(BF), forth)
            left = go(l.astype(BF), back)
        rights.append(right)
        lefts.append(left)
    mixed = parts[0] + jnp.concatenate(rights).astype(F32) + jnp.concatenate(lefts).astype(F32)
    return (tokens.astype(F32) + gate * (mixed + second_bias.astype(F32))).astype(BF)


def partner(block, axis, stride):
    count = lax.axis_size(axis)
    route = []
    for low in range(count):
        high = low | 1 << stride
        if high != low and high < count:
            route += [(low, high), (high, low)]
    return lax.ppermute(block, axis, route)


def request_onehot(lengths, row_count, req_count):
    bounds = jnp.cumsum(lengths)
    places = jnp.arange(row_count, dtype=jnp.int32)
    owner_req = jnp.sum((places[:, None] >= bounds[None, :]).astype(jnp.int32), axis=1)
    return (owner_req[:, None] == jnp.arange(req_count, dtype=jnp.int32)[None, :]).astype(
        jnp.float32
    )


def plain_device(
    tokens,
    modulation,
    adapter_per_request,
    tokens_per_request,
    first_weight,
    first_bias,
    second_weight,
    second_bias,
    adapter_down_matrices,
    adapter_up_matrices,
):
    tensor_index = lax.axis_index("tensor")
    store_index = lax.axis_index("store")
    tok_rows, feat_width = tokens.shape
    req_count = tokens_per_request.shape[1]
    rank_column_width = adapter_down_matrices.shape[2]
    hidden_width = first_weight.shape[1]
    store_request_count = adapter_down_matrices.shape[0]
    gathered = lax.all_gather(tokens, "tensor", axis=1, tiled=True).astype(jnp.float32)
    adapter_indicator = request_onehot(tokens_per_request[0], tok_rows, req_count)
    factors = modulation[0].astype(jnp.float32)
    shift_rows = jnp.dot(adapter_indicator, factors[:, 0], precision=lax.Precision.HIGHEST)
    scale_rows = jnp.dot(adapter_indicator, factors[:, 1], precision=lax.Precision.HIGHEST)
    gate_own = lax.dynamic_slice_in_dim(factors[:, 2], tensor_index * feat_width, feat_width, 1)
    gate_rows = jnp.dot(adapter_indicator, gate_own, precision=lax.Precision.HIGHEST)
    center = jnp.mean(gathered, axis=1, keepdims=True)
    spread = jnp.mean((gathered - center) ** 2, axis=1, keepdims=True)
    normed = (gathered - center) * lax.rsqrt(spread + 1e-06)
    modded = ((1.0 + scale_rows) * normed + shift_rows).astype(jnp.bfloat16)

    def pick_owned(wanted):
        owned_mask = wanted // store_request_count == store_index
        request_index_list = jnp.clip(
            wanted - store_index * store_request_count, 0, store_request_count - 1
        )
        down_matrix_rows = jnp.take(adapter_down_matrices, request_index_list, axis=0)
        up_matrix_rows = jnp.take(adapter_up_matrices, request_index_list, axis=0)
        keep = owned_mask[:, None, None]
        return (
            owned_mask,
            jnp.where(keep, down_matrix_rows, jnp.zeros_like(down_matrix_rows)),
            jnp.where(keep, up_matrix_rows, jnp.zeros_like(up_matrix_rows)),
        )

    mine_ids = lax.dynamic_index_in_dim(adapter_per_request, store_index, 0, keepdims=False)
    other_ids = lax.dynamic_index_in_dim(adapter_per_request, 1 - store_index, 0, keepdims=False)
    mine_owned, mine_down, mine_up = pick_owned(mine_ids)
    other_owned, send_down, send_up = pick_owned(other_ids)
    recv_down, recv_up = partner((send_down, send_up), "store", 0)
    down_now = jnp.where(mine_owned[:, None, None], mine_down, recv_down)
    up_now = jnp.where(mine_owned[:, None, None], mine_up, recv_up)
    low_rank_every = jnp.einsum(
        "tn,knr->tkr",
        modded,
        lax.all_gather(down_now, "tensor", axis=1, tiled=True),
        preferred_element_type=jnp.float32,
    )
    low_rank_sum = jnp.sum(adapter_indicator[:, :, None] * low_rank_every, axis=1)
    adapter_low_rank = low_rank_sum.astype(jnp.bfloat16)
    broadcast_low_rank = (
        (adapter_indicator[:, :, None] * adapter_low_rank.astype(jnp.float32)[:, None, :])
        .reshape(tok_rows, req_count * rank_column_width)
        .astype(jnp.bfloat16)
    )
    preact = jnp.dot(modded, first_weight, preferred_element_type=jnp.float32) + first_bias.astype(
        jnp.float32
    )
    preact = preact + jnp.dot(
        broadcast_low_rank,
        up_now.reshape(req_count * rank_column_width, hidden_width),
        preferred_element_type=jnp.float32,
    )
    activated = jax.nn.gelu(preact, approximate=True).astype(jnp.bfloat16)
    own_share = lax.psum_scatter(
        lax.dot_general(
            second_weight, activated, (((0,), (1,)), ((), ())), preferred_element_type=jnp.float32
        ),
        "tensor",
        scatter_dimension=0,
        tiled=True,
    ).T
    block_out = tokens.astype(jnp.float32) + gate_rows * (
        own_share + second_bias.astype(jnp.float32)
    )
    return block_out.astype(jnp.bfloat16)


def on_device(count, tokens, *rest):
    if tokens.shape[1] % 128 == 0 and count % 4 == 0 and count & (count - 1) == 0:
        return ring_device(count, tokens, *rest)
    return plain_device(tokens, *rest)


def solution(mesh):
    in_specs = (
        P(("groups", "store"), "tensor"),
        P(("groups", "store"), None, None, None),
        P("groups", None),
        P(("groups", "store"), None),
        P(None, "tensor"),
        P("tensor"),
        P("tensor", None),
        P("tensor"),
        P("store", "tensor", None),
        P("store", None, "tensor"),
    )
    out_specs = P(("groups", "store"), "tensor")
    return jax.shard_map(
        functools.partial(on_device, mesh.shape["tensor"]), mesh=mesh, in_specs=in_specs, out_specs=out_specs, check_vma=False
    )
```

```python
import functools

import jax
import jax.numpy as jnp
from jax import lax
from jax.experimental import pallas as pl
from jax.experimental.pallas import tpu as pltpu
from jax.sharding import PartitionSpec as P

BF = jnp.bfloat16
F32 = jnp.float32
SEND_MIB = 60
HIGH = lax.Precision.HIGHEST
ANY = pl.BlockSpec(memory_space=pltpu.HBM)
SMEM = pl.BlockSpec(memory_space=pltpu.SMEM)
WHOLE = pl.BlockSpec(memory_space=pltpu.VMEM)


def params(mib=24):
    return pltpu.CompilerParams(vmem_limit_bytes=mib * 1024 * 1024)


def cost(flops, nbytes, trans=0, scale=1.0):
    flops, nbytes, trans = flops * scale, nbytes * scale, trans * scale
    return pl.CostEstimate(
        flops=int(flops), bytes_accessed=int(nbytes), transcendentals=int(trans)
    )


def ring_order(count):
    cols = 2 if count < 32 else 4
    rows = count // cols
    walk = [r * cols for r in range(rows)]
    for i, r in enumerate(reversed(range(rows))):
        across = list(range(1, cols))
        walk += [r * cols + c for c in (across if i % 2 == 0 else across[::-1])]
    return walk


def blocks_in(ref, width, at, axis):
    place = pl.ds(pl.multiple_of(at * width, width), width)
    return ref.at[place, :] if axis == 0 else ref.at[:, place]


def place(ids, whose, r, stored):
    return jnp.clip(ids[whose, r] - lax.axis_index("store") * stored, 0, stored - 1)


def send_kernel(ids, down_ref, up_ref, down_out, mine_out, up_out, sem):
    reqs = down_out.shape[0]
    stored = down_ref.shape[0]
    me = lax.axis_index("store")
    copies = []
    for r in range(reqs):
        at = place(ids, 1 - me, r, stored)
        own = place(ids, me, r, stored)
        copies.append(pltpu.make_async_copy(down_ref.at[at], down_out.at[r], sem.at[0, r]))
        copies.append(pltpu.make_async_copy(down_ref.at[own], mine_out.at[r], sem.at[1, r]))
        copies.append(pltpu.make_async_copy(up_ref.at[at], up_out.at[r], sem.at[2, r]))
    for c in copies:
        c.start()
    for c in copies:
        c.wait()


def fetch_adapters(count, ints, store_ref, recv_ref, dst, sem, wait):
    reqs, rank = recv_ref.shape[:2]
    for r in range(reqs):
        here = dst.at[pl.ds(r * rank, rank)]
        if wait:
            pltpu.make_async_copy(recv_ref.at[r], here, sem.at[r]).wait()
            continue
        own = ints[count + 2 * reqs + r]

        @pl.when(own == 1)
        def _():
            pltpu.make_async_copy(store_ref.at[ints[count + r]], here, sem.at[r]).start()

        @pl.when(own == 0)
        def _():
            pltpu.make_async_copy(recv_ref.at[r], here, sem.at[r]).start()


def own_kernel(lengths, x_ref, mod_ref, u_out, hot_out, stat_out):
    rows, feat = x_ref.shape
    reqs = mod_ref.shape[1]
    own = pl.ds(pl.multiple_of(lax.axis_index("tensor") * feat, feat), feat)
    x = x_ref[...].astype(F32)
    mean = jnp.mean(x, axis=1, keepdims=True)
    cent = x - mean
    m2 = jnp.sum(cent * cent, axis=1, keepdims=True)
    row = lax.broadcasted_iota(jnp.int32, (rows, 128), 0)
    lane = lax.broadcasted_iota(jnp.int32, (rows, 128), 1)
    first = jnp.zeros((1, 128), jnp.int32)
    after = jnp.zeros((1, 128), jnp.int32)
    lane1 = lax.broadcasted_iota(jnp.int32, (1, 128), 1)
    begin = jnp.int32(0)
    for r in range(reqs):
        end = begin + lengths[0, r]
        first = jnp.where(lane1 == r, begin, first)
        after = jnp.where(lane1 == r, end, after)
        begin = end
    hot = jnp.where((row >= first) & (row < after), 1.0, 0.0)
    hot_out[...] = hot.astype(BF)
    stat_out[...] = jnp.where(lane == 0, mean, jnp.where(lane == 1, m2, 0.0)).T[:8]
    scale_rows = jnp.dot(hot[:, :reqs].astype(BF), mod_ref[1, :, own], preferred_element_type=F32)
    u_out[...] = (cent * (1.0 + scale_rows)).astype(BF)


def low_kernel(
    count, stored, ids, u_ref, hot_ref, stat_ref, mod_ref, mine_ref, recv_ref, low_out, pack_out, down_now
):
    rows, feat = u_ref.shape
    reqs, rank = recv_ref.shape[:2]
    me = lax.axis_index("tensor")
    store = lax.axis_index("store")
    own = pl.ds(pl.multiple_of(me * feat, feat), feat)
    for r in range(reqs):
        here = pl.ds(r * rank, rank)

        @pl.when(ids[store, r] // stored == store)
        def _():
            down_now[here, :] = mine_ref[r]

        @pl.when(ids[store, r] // stored != store)
        def _():
            down_now[here, :] = recv_ref[r]

    hot_t = hot_ref[...].astype(F32).T
    every = lax.dot_general(
        down_now[...], u_ref[...], (((1,), (1,)), ((), ())), preferred_element_type=F32
    )
    total = jnp.zeros((rank, rows), F32)
    side = jnp.zeros((rank, 128), F32)
    lane = lax.broadcasted_iota(jnp.int32, (rank, 128), 1)
    for r in range(reqs):
        total = total + every[r * rank : (r + 1) * rank] * hot_t[r : r + 1]
        mat = down_now[pl.ds(r * rank, rank), :].astype(F32)
        by_scale = jnp.sum(mat * (1.0 + mod_ref[1, pl.ds(r, 1), own].astype(F32)), axis=1, keepdims=True)
        by_shift = jnp.sum(mat * mod_ref[0, pl.ds(r, 1), own].astype(F32), axis=1, keepdims=True)
        side = jnp.where(lane == r, by_scale, side)
        side = jnp.where(lane == reqs + r, by_shift, side)
    low_out[...] = total.astype(BF)
    stat = stat_ref[...]
    here = lax.broadcasted_iota(jnp.int32, (count, rows), 0) == me
    pack_out[pl.ds(0, count), :] = jnp.where(here, stat[0:1], 0.0)
    turned = jnp.concatenate([side, jnp.zeros((128 - rank, 128), F32)], axis=0).T
    flat = jnp.concatenate([turned[: 2 * reqs], jnp.zeros((2 * reqs, rows - 128), F32)], axis=1)
    pack_out[pl.ds(count, 2 * reqs), :] = flat
    pack_out[pl.ds(count + 2 * reqs, 8), :] = jnp.broadcast_to(stat[1:2], (8, rows))


def merge(count, span, reqs, low_a, pack_a, low_b, pack_b, hot_ref):
    hot_t = hot_ref[...].astype(F32).T[:reqs]
    pa, pb = pack_a[...], pack_b[...]
    rank = low_a.shape[0]
    gap = (jnp.sum(pa[:count], axis=0, keepdims=True) - jnp.sum(pb[:count], axis=0, keepdims=True)) / span
    diff = (pa - pb)[count : count + reqs, :rank]
    back = lax.dot_general(
        diff, hot_t, (((0,), (0,)), ((), ())), precision=HIGH, preferred_element_type=F32
    )
    low = low_a[...].astype(F32) + low_b[...].astype(F32) + (0.5 * gap) * back
    return low, pa + pb, hot_t


def merge_kernel(count, span, reqs, *refs):
    low, pack, _ = merge(count, span, reqs, *refs[:5])
    refs[5][...] = low.astype(BF)
    refs[6][...] = pack


def last_merge_kernel(count, span, reqs, feat, *refs):
    wide_out, col_out = refs[5:]
    low, pack, hot_t = merge(count, span, reqs, *refs[:5])
    rank, rows = low.shape
    means = pack[:count]
    mean = jnp.sum(means, axis=0, keepdims=True) / count
    dev = means - mean
    m2 = pack[count + 2 * reqs : count + 2 * reqs + 1] + feat * jnp.sum(dev * dev, axis=0, keepdims=True)
    rstd = lax.rsqrt(m2 / (count * feat) + 1e-06)
    shifted = lax.dot_general(
        pack[count + reqs : count + 2 * reqs, :rank], hot_t, (((0,), (0,)), ((), ())),
        precision=HIGH, preferred_element_type=F32,
    )
    low = (low * rstd + shifted).astype(BF).astype(F32)
    pad = 128 - rank - count - 1
    turned = jnp.concatenate([low, dev * rstd, rstd, jnp.zeros((pad, rows), F32)], axis=0).T
    col_out[...] = jnp.broadcast_to(turned[:, rank + count : rank + count + 1], (rows, 128))
    turned = turned.astype(BF)
    hot8 = refs[4][...][:, :reqs]

    def spread(src_count, width, rule):
        src = lax.broadcasted_iota(jnp.int32, (src_count, width), 0)
        dst = lax.broadcasted_iota(jnp.int32, (src_count, width), 1)
        return jnp.where(rule(src, dst), 1.0, 0.0).astype(BF)

    def times(a, b):
        return jnp.dot(a, b, preferred_element_type=F32)

    width = reqs * rank
    lora = times(turned, spread(128, width, lambda s, d: (d % rank == s) & (s < rank)))
    lora = lora * times(hot8, spread(reqs, width, lambda s, d: d // rank == s))
    pairs = count * reqs
    coef = times(turned, spread(128, 128, lambda s, d: (s == rank + d // reqs) & (d < pairs)))
    coef = coef * times(hot8, spread(reqs, 128, lambda s, d: (d % reqs == s) & (d < pairs)))
    coef = coef + times(
        hot8, spread(reqs, 128, lambda s, d: (d % reqs == s) & (d >= pairs) & (d < pairs + 2 * reqs))
    )
    wide_out[:, pl.ds(0, width)] = lora.astype(BF)
    wide_out[:, pl.ds(width, 128)] = coef.astype(BF)


def means_kernel(count, mod_ref, w_ref, bias_ref, after_ref, out_ref, total):
    step = pl.program_id(0)
    reqs = mod_ref.shape[1]
    feat = mod_ref.shape[2]
    lhs = jnp.concatenate([jnp.ones((reqs, feat), F32), mod_ref[1].astype(F32), mod_ref[0].astype(F32)], axis=0)
    lhs = jnp.concatenate([lhs, jnp.zeros((8, feat), F32)], axis=0).astype(BF)
    got = jnp.dot(lhs, w_ref[...], preferred_element_type=F32)
    total[0, pl.ds(pl.multiple_of(step * reqs, reqs), reqs), :] = got[:reqs] + got[reqs : 2 * reqs]

    @pl.when(step == 0)
    def _():
        total[1, pl.ds(0, reqs), :] = got[2 * reqs : 3 * reqs] + bias_ref[...].astype(F32)

    @pl.when(step > 0)
    def _():
        total[1, pl.ds(0, reqs), :] += got[2 * reqs : 3 * reqs]

    @pl.when(step == count - 1)
    def _():
        shift = total[1, pl.ds(0, reqs), :]
        high = shift.astype(BF).astype(F32)
        both = jnp.concatenate([high, shift - high], axis=0)
        left = 128 - count * reqs - 2 * reqs
        rows = [total[0, pl.ds(0, count * reqs), :], both]
        if left:
            rows.append(jnp.zeros((left, both.shape[1]), F32))
        out_ref[...] = jnp.concatenate(rows, axis=0).astype(BF)


N_TILE = 512


def first_kernel(count, blocks, base, ints, *refs):
    xs = refs[:blocks]
    w_ref, acc_out, w_now, sem = refs[blocks:]
    feat = xs[0].shape[1]
    hidden = acc_out.shape[1]
    tiles = hidden // N_TILE

    def copy(k, n):
        cols = pl.ds(n * N_TILE, N_TILE)
        at = pl.multiple_of(ints[base + k] * feat, feat)
        return pltpu.make_async_copy(
            w_ref.at[pl.ds(at, feat), cols], w_now.at[n, pl.ds(k * feat, feat), :], sem.at[k, n]
        )

    for n in range(tiles):
        for k in range(blocks):
            copy(k, n).start()
    lhs = jnp.concatenate([x[...] for x in xs], axis=1)
    for n in range(tiles):
        for k in range(blocks):
            copy(k, n).wait()
        acc_out[:, pl.ds(n * N_TILE, N_TILE)] = jnp.dot(lhs, w_now[n], preferred_element_type=F32)


def lora_kernel(
    count, blocks, base, ints, *refs
):
    xs = refs[:blocks]
    (w_ref, acc_in, wide_ref, col_ref, tail_ref, up_ref, recv_ref, acc_out, w_now, up_now, sem, up_sem) = refs[blocks:]
    feat = xs[0].shape[1]
    hidden = acc_out.shape[1]
    tiles = hidden // N_TILE
    reqs, rank = recv_ref.shape[:2]

    def copy(k, n):
        cols = pl.ds(n * N_TILE, N_TILE)
        at = pl.multiple_of(ints[base + k] * feat, feat)
        return pltpu.make_async_copy(
            w_ref.at[pl.ds(at, feat), cols], w_now.at[n, pl.ds(k * feat, feat), :], sem.at[k, n]
        )

    for n in range(tiles):
        for k in range(blocks):
            copy(k, n).start()
    fetch_adapters(count, ints, up_ref, recv_ref, up_now, up_sem, False)
    lhs = jnp.concatenate([x[...] for x in xs], axis=1)
    scale = col_ref[:, 0:1]
    for n in range(tiles):
        cols = pl.ds(n * N_TILE, N_TILE)
        for k in range(blocks):
            copy(k, n).wait()
        part = acc_in[:, cols] + jnp.dot(lhs, w_now[n], preferred_element_type=F32)
        acc_out[:, cols] = part * scale
    fetch_adapters(count, ints, up_ref, recv_ref, up_now, up_sem, True)
    width = reqs * rank
    wide = wide_ref[...]
    for n in range(tiles):
        cols = pl.ds(n * N_TILE, N_TILE)
        both = jnp.concatenate([up_now[:, cols], tail_ref[:, cols]], axis=0)
        acc_out[:, cols] += jnp.dot(wide, both, preferred_element_type=F32)


def finish_kernel(ints, c_ref, d_ref, col_ref, w_ref, acc_ref, w2_ref, act_out, part_out):
    upper = pl.program_id(0) < pl.num_programs(0) // 2
    x = jnp.where(upper, c_ref[...].astype(F32), d_ref[...].astype(F32)).astype(BF)
    pre = acc_ref[...] + jnp.dot(x, w_ref[...], preferred_element_type=F32) * col_ref[:, 0:1]
    act = jax.nn.gelu(pre, approximate=True).astype(BF)
    act_out[...] = act
    part_out[...] = jnp.dot(act, w2_ref[...], preferred_element_type=F32).astype(BF)


def second_kernel(blocks, base, ints, act_ref, w_ref, *refs):
    outs = refs[:blocks]
    w_now, sem = refs[blocks:]
    feat = outs[0].shape[1]

    def copy(k):
        at = pl.multiple_of(ints[base - k] * feat, feat)
        return pltpu.make_async_copy(
            w_ref.at[:, pl.ds(at, feat)], w_now.at[:, pl.ds(k * feat, feat)], sem.at[k]
        )

    for k in range(blocks):
        copy(k).start()
    for k in range(blocks):
        copy(k).wait()
    got = jnp.dot(act_ref[...], w_now[...], preferred_element_type=F32)
    for k in range(blocks):
        outs[k][...] = got[:, k * feat : (k + 1) * feat]


def ring_device(
    count, tokens, modulation, adapter_per_request, tokens_per_request, first_weight,
    first_bias, second_weight, second_bias, adapter_down_matrices, adapter_up_matrices,
):
    me = lax.axis_index("tensor")
    store = lax.axis_index("store")
    rows, feat = tokens.shape
    hidden = first_weight.shape[1]
    stored, rank = adapter_up_matrices.shape[:2]
    reqs = tokens_per_request.shape[1]
    order = ring_order(count)
    forth = [(order[i], order[(i + 1) % count]) for i in range(count)]
    back = [(b, a) for a, b in forth]
    half = count // 2
    visits = [0] + [s for k in range(1, half) for s in (-k, k)] + [half]
    table = [[0] * count for _ in range(count)]
    for at, dev in enumerate(order):
        table[dev] = [order[(at + k) % count] for k in visits]
    mine = lax.dynamic_index_in_dim(jnp.array(table, jnp.int32), me, 0, keepdims=False)

    def go(x, route):
        return lax.ppermute(x, "tensor", route)

    def like(*shape, kind=BF):
        return jax.ShapeDtypeStruct(shape, kind)

    down = jnp.swapaxes(adapter_down_matrices, 1, 2)
    mod = jnp.swapaxes(modulation[0], 0, 1)

    my_ids = lax.dynamic_index_in_dim(adapter_per_request, store, 0, keepdims=False)
    their_ids = lax.dynamic_index_in_dim(adapter_per_request, 1 - store, 0, keepdims=False)
    ids = jnp.concatenate([my_ids, their_ids])
    ints = jnp.concatenate(
        [
            mine,
            jnp.clip(ids - store * stored, 0, stored - 1),
            (my_ids // stored == store).astype(jnp.int32),
        ]
    )

    u, hot, stat = pl.pallas_call(
        own_kernel,
        in_specs=[SMEM, WHOLE, WHOLE],
        out_specs=[WHOLE] * 3,
        out_shape=[like(rows, feat), like(rows, 128), like(8, rows, kind=F32)],
        compiler_params=params(60),
        cost_estimate=cost(2 * rows * feat, rows * feat),
        name="own_features",
    )(tokens_per_request, tokens, mod)

    send_down, mine_down, send_up = pl.pallas_call(
        send_kernel,
        in_specs=[SMEM, ANY, ANY],
        out_specs=[WHOLE] * 3,
        out_shape=[like(reqs, rank, feat)] * 2 + [like(reqs, rank, hidden)],
        scratch_shapes=[pltpu.SemaphoreType.DMA((3, reqs))],
        compiler_params=params(SEND_MIB),
        cost_estimate=cost(0, reqs * rank * (feat + hidden)),
        name="adapters_to_send",
    )(adapter_per_request, down, adapter_up_matrices)
    swap = [(s, s ^ 1) for s in range(lax.axis_size("store"))]
    recv_down = lax.ppermute(send_down, "store", swap)

    tail = pl.pallas_call(
        functools.partial(means_kernel, count),
        grid=(count,),
        in_specs=[
            pl.BlockSpec((3, reqs, feat), lambda i: (0, 0, i)),
            pl.BlockSpec((feat, hidden), lambda i: (i, 0)),
            pl.BlockSpec((1, hidden), lambda i: (0, 0)),
            ANY,
        ],
        out_specs=pl.BlockSpec((128, hidden), lambda i: (0, 0)),
        out_shape=like(128, hidden),
        scratch_shapes=[pltpu.VMEM((2, count * reqs, hidden), F32)],
        compiler_params=params(),
        cost_estimate=cost(64 * count * feat * hidden, 2 * count * feat * hidden, scale=0.1),
        name="means_part",
    )(mod, first_weight, first_bias.reshape(1, hidden), send_up)

    low, pack = pl.pallas_call(
        functools.partial(low_kernel, count, stored),
        in_specs=[SMEM] + [WHOLE] * 6,
        out_specs=[WHOLE] * 2,
        out_shape=[like(rank, rows), like(count + 2 * reqs + 8, rows, kind=F32)],
        scratch_shapes=[pltpu.VMEM((reqs * rank, feat), BF)],
        compiler_params=params(),
        cost_estimate=cost(rows * feat * reqs, rows * feat),
        name="low_rank_parts",
    )(adapter_per_request, u, hot, stat, mod, mine_down, recv_down)
    recv_up = lax.ppermute(send_up, "store", swap)

    cut = rows // 2
    a = b = u
    seen = [u]
    for k in range(1, half):
        a, b = go(a, forth), go(b, back)
        seen += [a, b]
        if k == 1:
            a, b, _ = lax.optimization_barrier((a, b, low))
    far_c, far_d = go(a[:cut], forth), go(b[cut:], back)

    turn = 0
    span = 1
    while span < count:
        route = [(t, t ^ span) for t in range(count)]
        low_b, pack_b = go(low, route), go(pack, route)
        turn += 1
        if turn in (1, 2):
            low_b, pack_b, *_ = lax.optimization_barrier((low_b, pack_b, seen[2 * turn - 1], seen[2 * turn]))
        args = (low, pack, low_b, pack_b, hot)
        if 2 * span == count:
            kernel = functools.partial(last_merge_kernel, count, span, reqs, feat)
            shapes = [like(rows, reqs * rank + 128), like(rows, 128, kind=F32)]
        else:
            kernel = functools.partial(merge_kernel, count, span, reqs)
            shapes = [like(*low.shape), like(*pack.shape, kind=F32)]
        low, pack = pl.pallas_call(
            kernel,
            in_specs=[WHOLE] * 5,
            out_specs=[WHOLE] * 2,
            out_shape=shapes,
            compiler_params=params(),
            cost_estimate=cost(1e+09, 8 * rank * rows),
            name="merge_sums",
        )(*args)
        span *= 2
    wide, cols = low, pack


    tiles = hidden // N_TILE
    early, late = seen[:-2], seen[-2:]
    w_scratch = lambda n: [
        pltpu.VMEM((tiles, n * feat, N_TILE), BF),
    ]
    acc = pl.pallas_call(
        functools.partial(first_kernel, count, len(early), 0),
        in_specs=[SMEM] + [WHOLE] * len(early) + [ANY],
        out_specs=WHOLE,
        out_shape=like(rows, hidden, kind=F32),
        scratch_shapes=w_scratch(len(early)) + [pltpu.SemaphoreType.DMA((len(early), tiles))],
        compiler_params=params(24),
        cost_estimate=cost(2 * rows * feat * hidden * len(early), 2 * feat * hidden * len(early), scale=1),
        name="first_blocks",
    )(ints, *early, first_weight)
    acc = pl.pallas_call(
        functools.partial(lora_kernel, count, len(late), len(early)),
        in_specs=[SMEM] + [WHOLE] * len(late) + [ANY] + [WHOLE] * 4 + [ANY, ANY],
        out_specs=WHOLE,
        out_shape=like(rows, hidden, kind=F32),
        scratch_shapes=w_scratch(len(late))
        + [
            pltpu.VMEM((reqs * rank, hidden), BF),
            pltpu.SemaphoreType.DMA((len(late), tiles)),
            pltpu.SemaphoreType.DMA((reqs,)),
        ],
        compiler_params=params(24),
        cost_estimate=cost(
            2 * rows * hidden * (feat * len(late) + reqs * rank), 2 * feat * hidden * len(late), scale=1),
        name="low_rank_added",
    )(ints, *late, first_weight, acc, wide, cols, tail, adapter_up_matrices, recv_up)
    steps = 2
    tile = rows // steps
    last = count - 1
    tiled = lambda width: pl.BlockSpec((tile, width), lambda i, *s: (i, 0))
    act, far_part = pl.pallas_call(
        finish_kernel,
        grid_spec=pltpu.PrefetchScalarGridSpec(
            num_scalar_prefetch=1,
            grid=(steps,),
            in_specs=[
                pl.BlockSpec((tile, feat), lambda i, s: (jnp.minimum(i, steps // 2 - 1), 0)),
                pl.BlockSpec((tile, feat), lambda i, s: (jnp.maximum(i - steps // 2, 0), 0)),
                tiled(128),
                pl.BlockSpec((feat, hidden), lambda i, s: (s[last], 0)),
                tiled(hidden),
                pl.BlockSpec((hidden, feat), lambda i, s: (0, s[last])),
            ],
            out_specs=[tiled(hidden), tiled(feat)],
        ),
        out_shape=[like(rows, hidden), like(rows, feat)],
        compiler_params=params(16),
        cost_estimate=cost(4 * rows * hidden * feat, 14 * rows * hidden, rows * hidden, scale=1),
        name="finish_first",
    )(ints, far_c, far_d, cols, first_weight, acc, second_weight)

    def second(blocks, base, name):
        return pl.pallas_call(
            functools.partial(second_kernel, blocks, base),
            in_specs=[SMEM, WHOLE, ANY],
            out_specs=[WHOLE] * blocks,
            out_shape=[like(rows, feat, kind=F32)] * blocks,
            scratch_shapes=[
                pltpu.VMEM((hidden, blocks * feat), BF),
                pltpu.SemaphoreType.DMA((blocks,)),
            ],
            compiler_params=params(16),
            cost_estimate=cost(rows * hidden * feat * blocks // 2, blocks * rows * feat),
            name=name,
        )(ints, act, second_weight)

    parts = {}
    base = count - 2
    for k in range(half - 1, 0, -1):
        blocks = 3 if k == 1 else 2
        got = second(blocks, base, "second_blocks")
        base -= blocks
        parts[k], parts[-k] = got[0], got[1]
    parts[0] = got[2]
    gate = jnp.dot(
        hot[:, :reqs], lax.dynamic_slice_in_dim(mod[2], me * feat, feat, 1),
        preferred_element_type=F32,
    )
    rights, lefts = [], []
    chains = 1
    size = rows // chains
    for c in range(chains):
        lo = c * size
        mid = size // 2
        right = go(far_part[lo : lo + mid], forth)
        left = go(far_part[lo + mid : lo + size], back)
        for k in range(half - 1, 0, -1):
            r = parts[k][lo : lo + size]
            l = parts[-k][lo : lo + size]
            if k == half - 1:
                r = jnp.concatenate([r[:mid] + right.astype(F32), r[mid:]])
                l = jnp.concatenate([l[:mid], l[mid:] + left.astype(F32)])
            else:
                r = r + right.astype(F32)
                l = l + left.astype(F32)
            right = go(r.astype(BF), forth)
            left = go(l.astype(BF), back)
        rights.append(right)
        lefts.append(left)
    mixed = parts[0] + jnp.concatenate(rights).astype(F32) + jnp.concatenate(lefts).astype(F32)
    return (tokens.astype(F32) + gate * (mixed + second_bias.astype(F32))).astype(BF)


def partner(block, axis, stride):
    count = lax.axis_size(axis)
    route = []
    for low in range(count):
        high = low | 1 << stride
        if high != low and high < count:
            route += [(low, high), (high, low)]
    return lax.ppermute(block, axis, route)


def request_onehot(lengths, row_count, req_count):
    bounds = jnp.cumsum(lengths)
    places = jnp.arange(row_count, dtype=jnp.int32)
    owner_req = jnp.sum((places[:, None] >= bounds[None, :]).astype(jnp.int32), axis=1)
    return (owner_req[:, None] == jnp.arange(req_count, dtype=jnp.int32)[None, :]).astype(
        jnp.float32
    )


def plain_device(
    tokens,
    modulation,
    adapter_per_request,
    tokens_per_request,
    first_weight,
    first_bias,
    second_weight,
    second_bias,
    adapter_down_matrices,
    adapter_up_matrices,
):
    tensor_index = lax.axis_index("tensor")
    store_index = lax.axis_index("store")
    tok_rows, feat_width = tokens.shape
    req_count = tokens_per_request.shape[1]
    rank_column_width = adapter_down_matrices.shape[2]
    hidden_width = first_weight.shape[1]
    store_request_count = adapter_down_matrices.shape[0]
    gathered = lax.all_gather(tokens, "tensor", axis=1, tiled=True).astype(jnp.float32)
    adapter_indicator = request_onehot(tokens_per_request[0], tok_rows, req_count)
    factors = modulation[0].astype(jnp.float32)
    shift_rows = jnp.dot(adapter_indicator, factors[:, 0], precision=lax.Precision.HIGHEST)
    scale_rows = jnp.dot(adapter_indicator, factors[:, 1], precision=lax.Precision.HIGHEST)
    gate_own = lax.dynamic_slice_in_dim(factors[:, 2], tensor_index * feat_width, feat_width, 1)
    gate_rows = jnp.dot(adapter_indicator, gate_own, precision=lax.Precision.HIGHEST)
    center = jnp.mean(gathered, axis=1, keepdims=True)
    spread = jnp.mean((gathered - center) ** 2, axis=1, keepdims=True)
    normed = (gathered - center) * lax.rsqrt(spread + 1e-06)
    modded = ((1.0 + scale_rows) * normed + shift_rows).astype(jnp.bfloat16)

    def pick_owned(wanted):
        owned_mask = wanted // store_request_count == store_index
        request_index_list = jnp.clip(
            wanted - store_index * store_request_count, 0, store_request_count - 1
        )
        down_matrix_rows = jnp.take(adapter_down_matrices, request_index_list, axis=0)
        up_matrix_rows = jnp.take(adapter_up_matrices, request_index_list, axis=0)
        keep = owned_mask[:, None, None]
        return (
            owned_mask,
            jnp.where(keep, down_matrix_rows, jnp.zeros_like(down_matrix_rows)),
            jnp.where(keep, up_matrix_rows, jnp.zeros_like(up_matrix_rows)),
        )

    mine_ids = lax.dynamic_index_in_dim(adapter_per_request, store_index, 0, keepdims=False)
    other_ids = lax.dynamic_index_in_dim(adapter_per_request, 1 - store_index, 0, keepdims=False)
    mine_owned, mine_down, mine_up = pick_owned(mine_ids)
    other_owned, send_down, send_up = pick_owned(other_ids)
    recv_down, recv_up = partner((send_down, send_up), "store", 0)
    down_now = jnp.where(mine_owned[:, None, None], mine_down, recv_down)
    up_now = jnp.where(mine_owned[:, None, None], mine_up, recv_up)
    low_rank_every = jnp.einsum(
        "tn,knr->tkr",
        modded,
        lax.all_gather(down_now, "tensor", axis=1, tiled=True),
        preferred_element_type=jnp.float32,
    )
    low_rank_sum = jnp.sum(adapter_indicator[:, :, None] * low_rank_every, axis=1)
    adapter_low_rank = low_rank_sum.astype(jnp.bfloat16)
    broadcast_low_rank = (
        (adapter_indicator[:, :, None] * adapter_low_rank.astype(jnp.float32)[:, None, :])
        .reshape(tok_rows, req_count * rank_column_width)
        .astype(jnp.bfloat16)
    )
    preact = jnp.dot(modded, first_weight, preferred_element_type=jnp.float32) + first_bias.astype(
        jnp.float32
    )
    preact = preact + jnp.dot(
        broadcast_low_rank,
        up_now.reshape(req_count * rank_column_width, hidden_width),
        preferred_element_type=jnp.float32,
    )
    activated = jax.nn.gelu(preact, approximate=True).astype(jnp.bfloat16)
    own_share = lax.psum_scatter(
        lax.dot_general(
            second_weight, activated, (((0,), (1,)), ((), ())), preferred_element_type=jnp.float32
        ),
        "tensor",
        scatter_dimension=0,
        tiled=True,
    ).T
    block_out = tokens.astype(jnp.float32) + gate_rows * (
        own_share + second_bias.astype(jnp.float32)
    )
    return block_out.astype(jnp.bfloat16)


def on_device(count, tokens, *rest):
    if tokens.shape[1] % 128 == 0 and count % 4 == 0 and count & (count - 1) == 0:
        return ring_device(count, tokens, *rest)
    return plain_device(tokens, *rest)


def solution(mesh):
    in_specs = (
        P(("groups", "store"), "tensor"),
        P(("groups", "store"), None, None, None),
        P("groups", None),
        P(("groups", "store"), None),
        P(None, "tensor"),
        P("tensor"),
        P("tensor", None),
        P("tensor"),
        P("store", "tensor", None),
        P("store", None, "tensor"),
    )
    out_specs = P(("groups", "store"), "tensor")
    return jax.shard_map(
        functools.partial(on_device, mesh.shape["tensor"]), mesh=mesh, in_specs=in_specs, out_specs=out_specs, check_vma=False
    )
```
